32 devices in a mesh: dp: 8 (over y, x, core), shard: 4 (over z).
Axes of the slice: x: 2, y: 2, z: 4, core: 2. Of those that a mesh axis runs over, the one named last changes fastest.
Arguments:
- tokens: bfloat16 [32768, 512], P(('dp', 'shard')), may hold values from -6 to 6
- targets: int32 [32768], P(('dp', 'shard')), may hold values from 0 to 255
- gain_one: bfloat16 [512], P('shard'), may hold values from 0.5 to 1.5
- bias_one: bfloat16 [512], P('shard'), may hold values from -3 to 3
- w_query: bfloat16 [512, 512], P('shard'), may hold values from -0.5 to 0.5
- w_key: bfloat16 [512, 512], P('shard'), may hold values from -0.25 to 0.25
- w_value: bfloat16 [512, 512], P('shard'), may hold values from -0.25 to 0.25
- w_control: bfloat16 [512, 512], P('shard'), may hold values from -0.5 to 0.5
- w_mix: bfloat16 [512, 512], P('shard'), may hold values from -1 to 1
- gain_two: bfloat16 [512], P('shard'), may hold values from 0.5 to 1.5
- bias_two: bfloat16 [512], P('shard'), may hold values from -3 to 3
- w_up: bfloat16 [512, 2048], P('shard'), may hold values from -0.25 to 0.25
- bias_up: bfloat16 [2048], P('shard'), may hold values from -3 to 3
- w_down: bfloat16 [2048, 512], P('shard'), may hold values from -0.125 to 0.125
- bias_down: bfloat16 [512], P('shard'), may hold values from -3 to 3
- w_read: bfloat16 [512, 256], P('shard'), may hold values from -0.25 to 0.25
Outputs:
- output: bfloat16 [32768, 512], P(('dp', 'shard'))
- grad_tokens: float32 [32768, 512], P(('dp', 'shard'))
- grad_gain_one: float32 [512], P('shard')
- grad_bias_one: float32 [512], P('shard')
- grad_query: float32 [512, 512], P('shard')
- grad_key: float32 [512, 512], P('shard')
- grad_value: float32 [512, 512], P('shard')
- grad_control: float32 [512, 512], P('shard')
- grad_mix: float32 [512, 512], P('shard')
- grad_gain_two: float32 [512], P('shard')
- grad_bias_two: float32 [512], P('shard')
- grad_up: float32 [512, 2048], P('shard')
- grad_bias_up: float32 [2048], P('shard')
- grad_down: float32 [2048, 512], P('shard')
- grad_bias_down: float32 [512], P('shard')
- grad_read: float32 [512, 256], P('shard')
The draws below stay inside these ranges and needn't reach their ends.
All inputs are finite; a program needn't handle non-finite values.
Results may differ from the reference program's by a relative error of at most 0.013.
Values may be sent and summed in bfloat16 or wider, within the bound.
No kernel may reach another device: no remote copies, remote signals or barrier semaphores. Data moves between devices by JAX's collectives and lax.ppermute only.
A program may use at most 192 MiB of HBM per device.

```python
import jax
import jax.numpy as jnp
from jax import lax

D = 512
H = 8
HEAD = 64
NS = 64
FF = 2048
V = 256
SEQ_LEN = 1024
TOKENS = 32768


def plant(result, stream_key, least, high):
    index_at = [jax.random.randint(jax.random.fold_in(stream_key, axis), (), 0, length) for axis, length in enumerate(result.shape)]
    widest = result.shape.index(max(result.shape))
    next_to = index_at[:widest] + [(index_at[widest] + 1) % result.shape[widest]] + index_at[widest + 1:]
    return result.at[tuple(index_at)].set(least).at[tuple(next_to)].set(high)


def block_scale(stream_key, shape, shards, low, largest):
    level, own = 1.0, jax.random.fold_in(stream_key, 6)
    for position, parts in shards:
        heights = jnp.exp(jax.random.uniform(jax.random.fold_in(own, position), (parts,), jnp.float32, low / len(shards), largest / len(shards)))
        level = level * jnp.repeat(heights, shape[position] // parts).reshape([-1 if axis == position else 1 for axis in range(len(shape))])
    return level


def centred(own_key, dims, deviation, bound, split=(), held_as=jnp.bfloat16):
    entries = deviation * jax.random.normal(own_key, dims, jnp.float32)
    if split:
        entries = entries * block_scale(own_key, dims, split, -0.22, 0.18)
    return jnp.clip(entries, -bound, bound).astype(held_as)


def setup_inputs(seed: int = 0) -> dict:
    streams_of = jax.random.split(jax.random.key(seed), 17)
    tokens = centred(streams_of[0], (TOKENS, D), 1.0, 6.0, ((0, 32),))
    targets = plant(jax.random.randint(streams_of[1], (TOKENS,), 0, V), jax.random.fold_in(streams_of[1], 1), 0, V - 1).astype(jnp.int32)
    gain_one = jnp.clip(1.0 + 0.1 * jax.random.normal(streams_of[2], (D,), jnp.float32), 0.5, 1.5).astype(jnp.bfloat16)
    bias_one = centred(streams_of[3], (D,), 0.5, 3.0, ((0, 4),))
    w_query = centred(streams_of[4], (D, D), (D // 4) ** -0.5, 0.5, ((0, 4),))
    w_key = centred(streams_of[5], (D, D), D ** -0.5, 0.25, ((0, 4),))
    w_value = centred(streams_of[6], (D, D), D ** -0.5, 0.25, ((0, 4),))
    w_control = centred(streams_of[7], (D, H * NS), (D // 4) ** -0.5, 0.5, ((0, 4),))
    w_mix = centred(streams_of[8], (D, D), (D // 16) ** -0.5, 1.0, ((0, 4),))
    gain_two = jnp.clip(1.0 + 0.1 * jax.random.normal(streams_of[9], (D,), jnp.float32), 0.5, 1.5).astype(jnp.bfloat16)
    bias_two = centred(streams_of[10], (D,), 0.5, 3.0, ((0, 4),))
    w_up = centred(streams_of[11], (D, FF), D ** -0.5, 0.25, ((0, 4),))
    bias_up = centred(streams_of[12], (FF,), 0.5, 3.0, ((0, 4),))
    w_down = centred(streams_of[13], (FF, D), FF ** -0.5, 0.125, ((0, 4),))
    bias_down = centred(streams_of[14], (D,), 0.5, 3.0, ((0, 4),))
    w_read = centred(streams_of[15], (D, V), D ** -0.5, 0.25, ((0, 4),))
    return dict(tokens=tokens, targets=targets, gain_one=gain_one, bias_one=bias_one, w_query=w_query, w_key=w_key, w_value=w_value, w_control=w_control, w_mix=w_mix, gain_two=gain_two, bias_two=bias_two, w_up=w_up, bias_up=bias_up, w_down=w_down, bias_down=bias_down, w_read=w_read)


@jax.custom_vjp
def low(v):
    return lax.optimization_barrier(v.astype(jnp.bfloat16)).astype(jnp.float32)

@jax.custom_vjp
def low_back(v):
    return v

def low_keep(v):
    return (low(v), None)

def low_pass(kept, grad):
    return (grad,)

def back_keep(v):
    return (v, None)

def back_low(kept, grad):
    return (low(grad),)
low.defvjp(low_keep, low_pass)
low_back.defvjp(back_keep, back_low)
EPS = 1e-05
HIGH = lax.Precision.HIGHEST

def matmul(left, right):
    return jnp.dot(left, right, precision=HIGH, preferred_element_type=jnp.float32)

def layer_norm(values, gain, shift):
    centre = values - lax.optimization_barrier(jnp.mean(values, axis=-1, keepdims=True))
    spread = lax.optimization_barrier(jnp.mean(centre * centre, axis=-1, keepdims=True))
    return centre * lax.rsqrt(spread + EPS) * gain + shift

def attend_sequence(item):
    query, keyed, valued, weights = item
    length = query.shape[0]
    places = jnp.arange(length, dtype=jnp.int32)
    causal = (places[None, :] <= places[:, None]).astype(jnp.float32)
    scores = jnp.einsum('thd,shd->hts', query, keyed, precision=HIGH) * causal[None]
    scores = low(low_back(scores))
    numer = low_back(jnp.einsum('hts,shm->thm', scores, weights, precision=HIGH))
    total = low_back(jnp.einsum('ts,shm->thm', causal, weights, precision=HIGH))
    probs = jax.nn.softmax(HEAD ** (-0.5) * numer / total, axis=-1)
    ratio = low(probs / total)
    mixing = jnp.einsum('thm,shm->hts', ratio, weights, precision=HIGH) * causal[None]
    mixing = low(low_back(mixing))
    return low_back(low(jnp.einsum('hts,shd->thd', mixing, valued, precision=HIGH)))

def forward(params, inputs, targets):
    gain_one, bias_one, w_query, w_key, w_value, w_control, w_mix, gain_two, bias_two, w_up, bias_up, w_down, bias_down, w_read = params
    count = inputs.shape[0]
    seqs = count // SEQ_LEN
    normed = low(layer_norm(inputs, gain_one, bias_one))
    query = low(low_back(matmul(normed, w_query))).reshape(seqs, SEQ_LEN, H, HEAD)
    keyed = low(low_back(matmul(normed, w_key))).reshape(seqs, SEQ_LEN, H, HEAD)
    valued = low(low_back(matmul(normed, w_value))).reshape(seqs, SEQ_LEN, H, HEAD)
    control = low_back(matmul(normed, w_control))
    weights = low(jnp.exp(control)).reshape(seqs, SEQ_LEN, H, NS)
    mixed = lax.map(jax.checkpoint(attend_sequence), (query, keyed, valued, weights))
    attn_out = low_back(matmul(mixed.reshape(count, D), w_mix))
    resid = inputs + attn_out
    normed_two = low(layer_norm(resid, gain_two, bias_two))
    hidden = low_back(matmul(normed_two, w_up) + bias_up)
    active = low(jax.nn.gelu(hidden, approximate=True))
    branch = low_back(matmul(active, w_down) + bias_down)
    output = resid + branch
    logits = low_back(matmul(low(output), w_read))
    onehot = (targets[:, None] == jnp.arange(V, dtype=jnp.int32)[None, :]).astype(logits.dtype)
    picked = lax.optimization_barrier(jnp.sum(logits * onehot, axis=-1))
    loss = jnp.sum(jax.nn.logsumexp(logits, axis=-1) - picked)
    return (loss, output)

def reference(tokens, targets, gain_one, bias_one, w_query, w_key, w_value, w_control, w_mix, gain_two, bias_two, w_up, bias_up, w_down, bias_down, w_read):
    params = (gain_one, bias_one, w_query, w_key, w_value, w_control, w_mix, gain_two, bias_two, w_up, bias_up, w_down, bias_down, w_read)
    params = tuple((p.astype(jnp.float32) for p in params))
    inputs = tokens.astype(jnp.float32)

    def objective(params, inputs):
        return forward(params, inputs, targets)
    loss, pullback, output = jax.vjp(objective, params, inputs, has_aux=True)
    grads, d_inputs = pullback(jnp.ones_like(loss))
    return (output.astype(jnp.bfloat16), d_inputs, grads[0], grads[1], grads[2], grads[3], grads[4], grads[5], grads[6], grads[7], grads[8], grads[9], grads[10], grads[11], grads[12], grads[13])
```

```python
import jax
import jax.numpy as jnp
from jax import lax
from jax.experimental import pallas as pl
from jax.experimental.pallas import tpu as pltpu
from jax.sharding import PartitionSpec as P

EPS = 1e-05
WIDTH = 512
HEAD = 64
FF = 2048
VOCAB = 256
SEQ_LEN = 1024
CHUNK = 256
HALF = 256
PIECE = 16
COLS_PROJ = 4 * HALF
COLS_UP = WIDTH + FF
COLS_DOWN = 4 * WIDTH + VOCAB
F32 = jnp.float32
BF16 = jnp.bfloat16
MIB = 1024 * 1024


def nn(a, b):
    return lax.dot_general(a, b, (((1,), (0,)), ((), ())), preferred_element_type=F32)


def nt(a, b):
    return lax.dot_general(a, b, (((1,), (1,)), ((), ())), preferred_element_type=F32)


def tn(a, b):
    return lax.dot_general(a, b, (((0,), (0,)), ((), ())), preferred_element_type=F32)


def norm_parts(values):
    centre = values - jnp.mean(values, axis=-1, keepdims=True)
    inverse = lax.rsqrt(jnp.mean(centre * centre, axis=-1, keepdims=True) + EPS)
    return centre * inverse, inverse


def norm_pull(grad, unit, inverse, gain):
    scaled = grad * gain
    return inverse * (
        scaled
        - jnp.mean(scaled, axis=-1, keepdims=True)
        - unit * jnp.mean(scaled * unit, axis=-1, keepdims=True)
    )


def vector_of(vec_ref, idx, row):
    return jnp.concatenate(
        [vec_ref[s ^ idx[2], row : row + 1, :].astype(F32) for s in range(4)], axis=1
    )


def bias_up_of(vec_ref, idx):
    return jnp.concatenate(
        [
            vec_ref[s ^ idx[2], row : row + 1, :].astype(F32)
            for s in range(4)
            for row in range(5, 9)
        ],
        axis=1,
    )


def each_piece(idx, near, far):
    for c, buf in ((0, near), (1, far)):
        for xy in range(4):
            member = ((xy ^ idx[1]) * 2) + (c ^ idx[0])
            for s in range(4):
                yield s ^ idx[2], member, buf.at[xy, s]


def rows_at(start, size):
    return pl.ds(pl.multiple_of(start, PIECE), size)


def put_parts(idx, keep, send, tile, shard, columns):
    for xy in range(4):
        first = tile[32 * xy : 32 * xy + 16]
        second = tile[32 * xy + 16 : 32 * xy + 32]
        own_first = idx[0] == 0
        keep[xy ^ idx[1], shard ^ idx[2], :, columns] = jnp.where(own_first, first, second)
        send[xy ^ idx[1], shard ^ idx[2], :, columns] = jnp.where(own_first, second, first)


def pack_kernel(idx, wq, wk, wv, wc, wm, wu, wd, wr, pa, pb, pc, pd):
    member = idx[1] * 2 + idx[0]
    rows = rows_at(member * PIECE, PIECE)
    for j, w in enumerate((wq, wk, wv, wc)):
        pa[:, j * HALF : (j + 1) * HALF] = w[rows, :HALF]
        pb[:, j * HALF : (j + 1) * HALF] = w[rows, HALF:]
    pc[:, :WIDTH] = wm[rows, :]
    pc[:, WIDTH:] = wu[rows, :]
    for i in range(4):
        pd[:, i * WIDTH : (i + 1) * WIDTH] = wd[rows_at(member * 64 + 16 * i, PIECE), :]
    pd[:, 4 * WIDTH :] = wr[rows, :]


def first_norm_kernel(idx, vec, x, a1, a1t):
    unit, _ = norm_parts(x[...].astype(F32))
    low = (unit * vector_of(vec, idx, 0) + vector_of(vec, idx, 1)).astype(BF16)
    a1[...] = low
    a1t[...] = low.T


def lanes_low():
    return lax.broadcasted_iota(jnp.int32, (1, 128), 1) < HEAD


def spread(value):
    low = lanes_low().astype(F32).astype(BF16)
    high = (1.0 - lanes_low().astype(F32)).astype(BF16)
    return jnp.concatenate([value * low, value * high], axis=0)


def join(value):
    return jnp.where(lanes_low(), value[:CHUNK], value[CHUNK:])


def head_sum(value):
    low = lanes_low()
    first = jnp.sum(jnp.where(low, value, 0.0), axis=-1, keepdims=True)
    second = jnp.sum(jnp.where(low, 0.0, value), axis=-1, keepdims=True)
    return jnp.where(low, first, second)


def head_max(value):
    low = lanes_low()
    first = jnp.max(jnp.where(low, value, -jnp.inf), axis=-1, keepdims=True)
    second = jnp.max(jnp.where(low, -jnp.inf, value), axis=-1, keepdims=True)
    return jnp.where(low, first, second)


def same_head():
    row = lax.broadcasted_iota(jnp.int32, (128, 128), 0) < HEAD
    col = lax.broadcasted_iota(jnp.int32, (128, 128), 1) < HEAD
    return row == col


def causal_mask(rows, transposed=False):
    row = lax.broadcasted_iota(jnp.int32, (rows, CHUNK), 0) & (CHUNK - 1)
    col = lax.broadcasted_iota(jnp.int32, (rows, CHUNK), 1)
    return (row <= col) if transposed else (col <= row)


def attend_kernel(
    idx, a1, near, far,
    q_o, k_o, v_o, e_o, x_o, p_o, s_o, z_o, r_o, o_o, kept_s, kept_u, w_o,
    state_s, state_u, count_z,
):
    step = pl.program_id(0)

    @pl.when(step == 0)
    def _():
        for shard, member, piece in each_piece(idx, near, far):
            w_o[rows_at(shard * 128 + member * PIECE, PIECE), :] = piece[...]
        state_s[...] = jnp.zeros_like(state_s)
        state_u[...] = jnp.zeros_like(state_u)
        count_z[...] = jnp.zeros_like(count_z)

    a = a1[...]
    q_o[...] = nn(a, w_o[:, :HALF]).astype(BF16)
    k_o[...] = nn(a, w_o[:, HALF : 2 * HALF]).astype(BF16)
    v_o[...] = nn(a, w_o[:, 2 * HALF : 3 * HALF]).astype(BF16)
    expo = jnp.exp(nn(a, w_o[:, 3 * HALF :]))
    x_o[...] = expo
    e_o[...] = expo.astype(BF16)
    tri = causal_mask(2 * CHUNK)
    total = nn(tri[:CHUNK].astype(F32).astype(BF16), e_o[...]) + count_z[...]
    count_z[...] = total[CHUNK - 1 :, :]
    inverse = 1.0 / total
    z_o[...] = inverse
    for pair in range(2):
        at = slice(128 * pair, 128 * pair + 128)
        q, k, v, e = q_o[:, at], k_o[:, at], v_o[:, at], e_o[:, at]
        inv = inverse[:, at]
        low_s = state_s[pair].astype(BF16)
        low_u = state_u[pair].astype(BF16)
        kept_s[0, pair] = low_s
        kept_u[0, pair] = low_u
        scores = jnp.where(tri, nt(spread(q), k), 0.0).astype(BF16)
        numer = join(nn(scores, e)) + nn(q, low_s)
        logits = (HEAD ** -0.5) * numer * inv
        expd = jnp.exp(logits - head_max(logits))
        probs = expd / head_sum(expd)
        ratio = (probs * inv).astype(BF16)
        mixing = jnp.where(tri, nt(spread(ratio), e), 0.0).astype(BF16)
        o_o[:, at] = (join(nn(mixing, v)) + nn(ratio, low_u)).astype(BF16)
        s_o[:, at] = logits
        p_o[:, at] = probs
        r_o[:, at] = ratio
        block = same_head()
        state_s[pair] += jnp.where(block, tn(k, e), 0.0)
        state_u[pair] += jnp.where(block, tn(e, v), 0.0)


def feed_kernel(
    idx, vec, x, o0, o1, target, up_near, up_far, down_near, down_far,
    out_o, h_o, slope_o, dy_o, bias_o, keep, send,
    w_mix, w_up, w_down, w_read, act_s, out_s, dl_s, df_s,
):
    step = pl.program_id(0)

    @pl.when(step == 0)
    def _():
        for shard, member, piece in each_piece(idx, up_near, up_far):
            rows = rows_at(shard * 128 + member * PIECE, PIECE)
            w_mix[rows, :] = piece[:, :WIDTH]
            w_up[rows, :] = piece[:, WIDTH:]
        for shard, member, piece in each_piece(idx, down_near, down_far):
            for i in range(4):
                rows = rows_at(shard * 512 + member * 64 + 16 * i, PIECE)
                w_down[rows, :] = piece[:, i * WIDTH : (i + 1) * WIDTH]
            w_read[rows_at(shard * 128 + member * PIECE, PIECE), :] = piece[:, 4 * WIDTH :]
        bias_o[...] = jnp.zeros_like(bias_o)

    rows = pl.ds(pl.multiple_of(step * CHUNK, CHUNK), CHUNK)
    attn = nn(o0[...], w_mix[:HALF, :]) + nn(o1[...], w_mix[HALF:, :])
    resid = x[...].astype(F32) + attn
    h_o[...] = resid
    unit, _ = norm_parts(resid)
    second = (unit * vector_of(vec, idx, 2) + vector_of(vec, idx, 3)).astype(BF16)
    bias = bias_up_of(vec, idx)
    branch = jnp.zeros((CHUNK, WIDTH), F32)
    scale = (2.0 / jnp.pi) ** 0.5
    for j in range(4):
        at = slice(512 * j, 512 * j + 512)
        z = nn(second, w_up[:, at]) + bias[:, at]
        zz = z * z
        t = jnp.tanh(scale * z * (1.0 + 0.044715 * zz))
        cdf = 0.5 * (1.0 + t)
        act = (z * cdf).astype(BF16)
        slope_o[:, at] = cdf + 0.5 * z * (1.0 - t * t) * (scale * (1.0 + 3 * 0.044715 * zz))
        act_s[rows, at] = act
        branch += nn(act, w_down[at, :])
    out = (resid + (branch + vector_of(vec, idx, 4))).astype(BF16)
    out_o[...] = out
    out_s[rows, :] = out
    logits = nn(out, w_read[...])
    expd = jnp.exp(logits - jnp.max(logits, axis=-1, keepdims=True))
    soft = expd / jnp.sum(expd, axis=-1, keepdims=True)
    classes = lax.broadcasted_iota(jnp.int32, (CHUNK, VOCAB), 1)
    dl = (soft - jnp.where(classes == target[...], 1.0, 0.0)).astype(BF16)
    dl_s[rows, :] = dl
    dy = nt(dl, w_read[...])
    dy_o[...] = dy
    df = dy.astype(BF16)
    df_s[rows, :] = df
    bias_o[...] += jnp.sum(df.astype(F32), axis=0, keepdims=True)

    @pl.when(step == pl.num_programs(0) - 1)
    def _():
        for shard in range(4):
            tile = tn(out_s[:, shard * 128 : shard * 128 + 128], dl_s[...]).astype(BF16)
            put_parts(idx, keep, send, tile, shard, slice(4 * WIDTH, None))
            for xy in range(4):
                start = shard * 512 + xy * 128
                tile = tn(act_s[:, start : start + 128], df_s[...]).astype(BF16)
                own_first = idx[0] == 0
                for i in range(4):
                    first = tile[16 * i : 16 * i + 16]
                    later = tile[64 + 16 * i : 64 + 16 * i + 16]
                    at = slice(i * WIDTH, (i + 1) * WIDTH)
                    keep[xy ^ idx[1], shard ^ idx[2], :, at] = jnp.where(own_first, first, later)
                    send[xy ^ idx[1], shard ^ idx[2], :, at] = jnp.where(own_first, later, first)


def feed_back_kernel(
    idx, vec, h, slope, dy, o0, o1, up_near, up_far, down_near, down_far,
    dh_o, do_o, gain_o, shift_o, bias_o, keep, send,
    w_mix, w_up, w_down, dz_s, a2_s, da_s,
):
    step = pl.program_id(0)

    @pl.when(step == 0)
    def _():
        for shard, member, piece in each_piece(idx, up_near, up_far):
            rows = rows_at(shard * 128 + member * PIECE, PIECE)
            w_mix[rows, :] = piece[:, :WIDTH]
            w_up[rows, :] = piece[:, WIDTH:]
        for shard, member, piece in each_piece(idx, down_near, down_far):
            for i in range(4):
                rows = rows_at(shard * 512 + member * 64 + 16 * i, PIECE)
                w_down[rows, :] = piece[:, i * WIDTH : (i + 1) * WIDTH]
        gain_o[...] = jnp.zeros_like(gain_o)
        shift_o[...] = jnp.zeros_like(shift_o)
        bias_o[...] = jnp.zeros_like(bias_o)

    rows = pl.ds(pl.multiple_of(step * CHUNK, CHUNK), CHUNK)
    gain = vector_of(vec, idx, 2)
    unit, inverse = norm_parts(h[...])
    a2_s[rows, :] = (unit * gain + vector_of(vec, idx, 3)).astype(BF16)
    d_out = dy[...]
    df = d_out.astype(BF16)
    d_second = jnp.zeros((CHUNK, WIDTH), F32)
    for j in range(4):
        at = slice(512 * j, 512 * j + 512)
        dz = (nt(df, w_down[at, :]) * slope[:, at]).astype(BF16)
        dz_s[rows, at] = dz
        bias_o[:, at] += jnp.sum(dz.astype(F32), axis=0, keepdims=True)
        d_second += nt(dz, w_up[:, at])
    gain_o[...] += jnp.sum(d_second * unit, axis=0, keepdims=True)
    shift_o[...] += jnp.sum(d_second, axis=0, keepdims=True)
    dh = d_out + norm_pull(d_second, unit, inverse, gain)
    dh_o[...] = dh
    da = dh.astype(BF16)
    da_s[rows, :] = da
    do_o[...] = nt(da, w_mix[...]).astype(BF16)

    @pl.when(step == pl.num_programs(0) - 1)
    def _():
        for shard in range(4):
            half = (o0, o1)[shard // 2]
            start = (shard % 2) * 128
            tile = tn(half[:, start : start + 128], da_s[...]).astype(BF16)
            put_parts(idx, keep, send, tile, shard, slice(0, WIDTH))
            for j in range(4):
                tile = tn(
                    a2_s[:, shard * 128 : shard * 128 + 128], dz_s[:, 512 * j : 512 * j + 512]
                ).astype(BF16)
                at = slice(WIDTH + 512 * j, WIDTH + 512 * j + 512)
                put_parts(idx, keep, send, tile, shard, at)


def attend_back_kernel(
    idx, a1t, q_i, k_i, v_i, e_i, x_i, p_i, s_i, z_i, r_i, do_i, kept_s, kept_u,
    dx_o, keep, send,
    state_r, state_t, count_z, dx_s,
):
    step = pl.program_id(0)
    chunk = pl.num_programs(0) - 1 - step

    @pl.when(step == 0)
    def _():
        state_r[...] = jnp.zeros_like(state_r)
        state_t[...] = jnp.zeros_like(state_t)
        count_z[...] = jnp.zeros_like(count_z)

    rows = pl.ds(pl.multiple_of(chunk * CHUNK, CHUNK), CHUNK)
    tri = causal_mask(2 * CHUNK)
    trt = causal_mask(2 * CHUNK, True)
    later = trt[:CHUNK].astype(F32).astype(BF16)
    for pair in range(2):
        at = slice(128 * pair, 128 * pair + 128)
        q, k, v, e = q_i[:, at], k_i[:, at], v_i[:, at], e_i[:, at]
        ratio, do = r_i[:, at], do_i[:, at]
        probs, logits, inv = p_i[:, at], s_i[:, at], z_i[:, at]
        low_s, low_u = kept_s[0, pair], kept_u[0, pair]
        low_r = state_r[pair].astype(BF16)
        low_t = state_t[pair].astype(BF16)
        d_mix = jnp.where(tri, nt(spread(do), v), 0.0).astype(BF16)
        d_ratio = (join(nn(d_mix, e)) + nt(do, low_u)) * inv
        d_logits = probs * (d_ratio - head_sum(d_ratio * probs))
        d_numer = ((HEAD ** -0.5) * d_logits * inv).astype(BF16)
        d_total = (-d_ratio * (probs * inv) - d_logits * logits * inv).astype(BF16)
        d_scores = jnp.where(tri, nt(spread(d_numer), e), 0.0).astype(BF16)
        dq = join(nn(d_scores, k)) + nt(d_numer, low_s)
        scores = jnp.where(trt, nt(spread(k), q), 0.0).astype(BF16)
        wide_e = spread(e)
        mixing = jnp.where(trt, nt(wide_e, ratio), 0.0).astype(BF16)
        d_mix_t = jnp.where(trt, nt(spread(v), do), 0.0).astype(BF16)
        d_scores_t = jnp.where(trt, nt(wide_e, d_numer), 0.0).astype(BF16)
        dv = join(nn(mixing, do)) + nn(e, low_r)
        dk = join(nn(d_scores_t, q)) + nt(e, low_t)
        total_z = nn(later, d_total) + count_z[:, at]
        count_z[:, at] = total_z[:1, :]
        de = join(nn(d_mix_t, ratio) + nn(scores, d_numer)) + nt(v, low_r) + nn(k, low_t) + total_z
        dc = de * x_i[:, at]
        for j, value in enumerate((dq, dk, dv, dc)):
            dx_o[:, j * HALF + 128 * pair : j * HALF + 128 * pair + 128] = value.astype(BF16)
        block = same_head()
        state_r[pair] += jnp.where(block, tn(ratio, do), 0.0)
        state_t[pair] += jnp.where(block, tn(q, d_numer), 0.0)
    dx_s[rows, :] = dx_o[...]

    @pl.when(step == pl.num_programs(0) - 1)
    def _():
        for shard in range(4):
            for j in range(4):
                at = slice(j * HALF, (j + 1) * HALF)
                tile = nn(a1t[shard * 128 : shard * 128 + 128, :], dx_s[:, at]).astype(BF16)
                put_parts(idx, keep, send, tile, shard, at)


def inputs_kernel(idx, vec, x, dh, dx0, dx1, w0, w1, g_bd, g_g2, g_b2, g_bu, dx_o, vec_o, gain, shift):
    step = pl.program_id(0)

    @pl.when(step == 0)
    def _():
        gain[...] = jnp.zeros_like(gain)
        shift[...] = jnp.zeros_like(shift)

    unit, inverse = norm_parts(x[...].astype(F32))
    d_first = nt(dx0[...], w0[...]) + nt(dx1[...], w1[...])
    gain[...] += jnp.sum(d_first * unit, axis=0, keepdims=True)
    shift[...] += jnp.sum(d_first, axis=0, keepdims=True)
    dx_o[...] = dh[...] + norm_pull(d_first, unit, inverse, vector_of(vec, idx, 0))

    @pl.when(step == pl.num_programs(0) - 1)
    def _():
        for s in range(4):
            at = slice(128 * s, 128 * s + 128)
            rows = [gain[:, at], shift[:, at], g_g2[:, at], g_b2[:, at], g_bd[:, at]]
            rows += [g_bu[:, 512 * s + 128 * j : 512 * s + 128 * j + 128] for j in range(4)]
            rows.append(jnp.zeros((7, 128), F32))
            vec_o[s ^ idx[2]] = jnp.concatenate(rows, axis=0)


def unpack_proj_kernel(idx, *refs):
    first, second, outs = refs[:8], refs[8:16], refs[16:]
    member = idx[1] * 2 + idx[0]
    for k in range(8):
        rows = rows_at((member ^ k) * PIECE, PIECE)
        for j, out in enumerate(outs):
            at = slice(j * HALF, (j + 1) * HALF)
            out[rows, :HALF] = first[k][:, at].astype(F32)
            out[rows, HALF:] = second[k][:, at].astype(F32)


def unpack_up_kernel(idx, *refs):
    pieces, (mix, up) = refs[:8], refs[8:]
    member = idx[1] * 2 + idx[0]
    for k in range(8):
        rows = rows_at((member ^ k) * PIECE, PIECE)
        mix[rows, :] = pieces[k][:, :WIDTH].astype(F32)
        up[rows, :] = pieces[k][:, WIDTH:].astype(F32)


def unpack_down_kernel(idx, *refs):
    pieces, (down, read) = refs[:8], refs[8:]
    member = idx[1] * 2 + idx[0]
    for k in range(8):
        other = member ^ k
        for i in range(4):
            at = slice(i * WIDTH, (i + 1) * WIDTH)
            down[rows_at(other * 64 + 16 * i, PIECE), :] = pieces[k][:, at].astype(F32)
        read[rows_at(other * PIECE, PIECE), :] = pieces[k][:, 4 * WIDTH :].astype(F32)


def shaped(shape, dtype):
    return jax.ShapeDtypeStruct(shape, dtype)


def call(kernel, name, args, outs, steps=None, scratch=(), flops=0, limit=56):
    grid = (steps,) if steps else ()

    def spec(shape, block):
        if block is None:
            return pl.BlockSpec(tuple(shape), lambda *_: (0,) * len(shape))
        return pl.BlockSpec(*block)

    in_specs = []
    for array, block in args:
        if array.dtype == jnp.int32 and array.shape == (3,):
            in_specs.append(pl.BlockSpec(memory_space=pltpu.SMEM))
        else:
            in_specs.append(spec(array.shape, block))
    moved = sum(a.size * a.dtype.itemsize for a, _ in args)
    return pl.pallas_call(
        kernel,
        grid=grid,
        in_specs=in_specs,
        out_specs=[spec(shape, block) for shape, _, block in outs],
        out_shape=[shaped(shape, dtype) for shape, dtype, _ in outs],
        scratch_shapes=list(scratch),
        compiler_params=pltpu.CompilerParams(
            vmem_limit_bytes=limit * MIB,
            dimension_semantics=("arbitrary",) * len(grid) if grid else None,
        ),
        cost_estimate=pl.CostEstimate(flops=int(flops), bytes_accessed=int(moved), transcendentals=0),
        name=name,
    )(*[array for array, _ in args])


def swap(value, axis, size, distance):
    return lax.ppermute(value, axis, [(i, i ^ distance) for i in range(size)])


def gather_pieces(piece, dp, shards):
    rows = jnp.stack([piece] + [swap(piece, "shard", shards, k) for k in range(1, 4)])
    near = jnp.stack([rows] + [swap(rows, "dp", dp, 2 * k) for k in range(1, 4)])
    return near, swap(near, "dp", dp, 1)


def reduce_pieces(keep, send, dp, shards):
    got = swap(send, "dp", dp, 1)
    part = [(keep[k].astype(F32) + got[k].astype(F32)).astype(BF16) for k in range(4)]
    got = [swap(part[k], "dp", dp, 2 * k) for k in range(1, 4)]
    rows = [
        (
            (part[0][k].astype(F32) + got[0][k].astype(F32))
            + (got[1][k].astype(F32) + got[2][k].astype(F32))
        ).astype(BF16)
        for k in range(4)
    ]
    got = [swap(rows[k], "shard", shards, k) for k in range(1, 4)]
    total = (
        (rows[0].astype(F32) + got[0].astype(F32)) + (got[1].astype(F32) + got[2].astype(F32))
    ).astype(BF16)
    distance = 8
    while distance < dp:
        total = (total.astype(F32) + swap(total, "dp", dp, distance).astype(F32)).astype(BF16)
        distance *= 2
    return [total] + [swap(total, "dp", dp, k) for k in range(1, 8)]


def reduce_vectors(block, dp, shards):
    got = [swap(block[k], "shard", shards, k) for k in range(1, 4)]
    total = (block[0] + got[0]) + (got[1] + got[2])
    got = [total] + [swap(total, "dp", dp, k) for k in range(1, 8)]
    total = ((got[0] + got[1]) + (got[2] + got[3])) + ((got[4] + got[5]) + (got[6] + got[7]))
    distance = 8
    while distance < dp:
        total = total + swap(total, "dp", dp, distance)
        distance *= 2
    return total


def body(dp, shards):
    def on_device(
        tokens, targets, gain_one, bias_one, w_query, w_key, w_value, w_control, w_mix,
        gain_two, bias_two, w_up, bias_up, w_down, bias_down, w_read,
    ):
        count = tokens.shape[0]
        steps = count // CHUNK
        member = lax.axis_index("dp") % 8
        idx = jnp.stack([member % 2, member // 2, lax.axis_index("shard")]).astype(jnp.int32)

        own = jnp.concatenate(
            [
                jnp.stack([gain_one, bias_one, gain_two, bias_two, bias_down]),
                bias_up.reshape(4, 128),
                jnp.zeros((7, 128), BF16),
            ]
        )
        vec = jnp.stack([own] + [swap(own, "shard", shards, k) for k in range(1, 4)])
        weights = (w_query, w_key, w_value, w_control, w_mix, w_up, w_down, w_read)
        packed = call(
            pack_kernel,
            "pack_weights",
            [(idx, None)] + [(w, None) for w in weights],
            [((PIECE, n), BF16, None) for n in (COLS_PROJ, COLS_PROJ, COLS_UP, COLS_DOWN)],
            limit=16,
        )
        proj0, proj1, up, down = [gather_pieces(p, dp, shards) for p in packed]

        a1, a1t = call(
            first_norm_kernel,
            "first_norm",
            [(idx, None), (vec, None), (tokens, None)],
            [((count, WIDTH), BF16, None), ((WIDTH, count), BF16, None)],
            limit=24,
        )

        forward = lambda i: (i, 0)
        tok = lambda n: ((CHUNK, n), forward)
        kept = ((1, 2, 128, 128), lambda i: (i, 0, 0, 0))
        halves = []
        for bufs in (proj0, proj1):
            names = [((count, HALF), t, tok(HALF)) for t in (BF16,) * 4 + (F32,) * 4 + (BF16,) * 2]
            states = [((steps, 2, 128, 128), BF16, kept)] * 2
            halves.append(
                call(
                    attend_kernel,
                    "attend",
                    [(idx, None), (a1, tok(WIDTH)), (bufs[0], None), (bufs[1], None)],
                    names + states + [((WIDTH, COLS_PROJ), BF16, None)],
                    steps,
                    [
                        pltpu.VMEM((2, 128, 128), F32),
                        pltpu.VMEM((2, 128, 128), F32),
                        pltpu.VMEM((1, HALF), F32),
                    ],
                    flops=6e9,
                )
            )
        o0, o1 = halves[0][9], halves[1][9]

        parts = (4, 4, PIECE)
        out, h, slope, dy, g_bias_down, keep_down, send_down = call(
            feed_kernel,
            "feed_forward",
            [
                (idx, None), (vec, None), (tokens, tok(WIDTH)), (o0, tok(HALF)), (o1, tok(HALF)),
                (targets.reshape(count, 1), tok(1)),
                (up[0], None), (up[1], None), (down[0], None), (down[1], None),
            ],
            [
                ((count, WIDTH), BF16, tok(WIDTH)),
                ((count, WIDTH), F32, tok(WIDTH)),
                ((count, FF), F32, tok(FF)),
                ((count, WIDTH), F32, tok(WIDTH)),
                ((1, WIDTH), F32, None),
                (parts + (COLS_DOWN,), BF16, None),
                (parts + (COLS_DOWN,), BF16, None),
            ],
            steps,
            [
                pltpu.VMEM((WIDTH, WIDTH), BF16),
                pltpu.VMEM((WIDTH, FF), BF16),
                pltpu.VMEM((FF, WIDTH), BF16),
                pltpu.VMEM((WIDTH, VOCAB), BF16),
                pltpu.VMEM((count, FF), BF16),
                pltpu.VMEM((count, WIDTH), BF16),
                pltpu.VMEM((count, VOCAB), BF16),
                pltpu.VMEM((count, WIDTH), BF16),
            ],
            flops=8e9,
        )
        pieces_down = reduce_pieces(keep_down, send_down, dp, shards)

        dh, d_mixed, g_gain_two, g_bias_two, g_bias_up, keep_up, send_up = call(
            feed_back_kernel,
            "feed_backward",
            [
                (idx, None), (vec, None), (h, tok(WIDTH)), (slope, tok(FF)), (dy, tok(WIDTH)),
                (o0, None), (o1, None),
                (up[0], None), (up[1], None), (down[0], None), (down[1], None),
            ],
            [
                ((count, WIDTH), F32, tok(WIDTH)),
                ((count, WIDTH), BF16, tok(WIDTH)),
                ((1, WIDTH), F32, None),
                ((1, WIDTH), F32, None),
                ((1, FF), F32, None),
                (parts + (COLS_UP,), BF16, None),
                (parts + (COLS_UP,), BF16, None),
            ],
            steps,
            [
                pltpu.VMEM((WIDTH, WIDTH), BF16),
                pltpu.VMEM((WIDTH, FF), BF16),
                pltpu.VMEM((FF, WIDTH), BF16),
                pltpu.VMEM((count, FF), BF16),
                pltpu.VMEM((count, WIDTH), BF16),
                pltpu.VMEM((count, WIDTH), BF16),
            ],
            flops=8e9,
        )
        pieces_up = reduce_pieces(keep_up, send_up, dp, shards)

        back = lambda i: (steps - 1 - i, 0)
        kept_back = ((1, 2, 128, 128), lambda i: (steps - 1 - i, 0, 0, 0))
        d_proj, pieces_proj = [], []
        for half in range(2):
            q, k, v, e, x, p, s, z, r, _, ks, ku, w = halves[half]
            tb = ((CHUNK, HALF), back)
            column = ((CHUNK, HALF), lambda i, half=half: (steps - 1 - i, half))
            dx, keep, send = call(
                attend_back_kernel,
                "attend_backward",
                [(idx, None), (a1t, None)]
                + [(t, tb) for t in (q, k, v, e, x, p, s, z, r)]
                + [(d_mixed, column), (ks, kept_back), (ku, kept_back)],
                [
                    ((count, COLS_PROJ), BF16, ((CHUNK, COLS_PROJ), back)),
                    (parts + (COLS_PROJ,), BF16, None),
                    (parts + (COLS_PROJ,), BF16, None),
                ],
                steps,
                [
                    pltpu.VMEM((2, 128, 128), F32),
                    pltpu.VMEM((2, 128, 128), F32),
                    pltpu.VMEM((1, HALF), F32),
                    pltpu.VMEM((count, COLS_PROJ), BF16),
                ],
                flops=10e9,
            )
            d_proj.append(dx)
            pieces_proj.append(reduce_pieces(keep, send, dp, shards))

        d_tokens, block = call(
            inputs_kernel,
            "input_gradient",
            [
                (idx, None), (vec, None), (tokens, tok(WIDTH)), (dh, tok(WIDTH)),
                (d_proj[0], tok(COLS_PROJ)), (d_proj[1], tok(COLS_PROJ)),
                (halves[0][12], None), (halves[1][12], None),
                (g_bias_down, None), (g_gain_two, None), (g_bias_two, None), (g_bias_up, None),
            ],
            [((count, WIDTH), F32, tok(WIDTH)), ((4, 16, 128), F32, None)],
            steps,
            [pltpu.VMEM((1, WIDTH), F32), pltpu.VMEM((1, WIDTH), F32)],
            flops=3e9,
            limit=32,
        )
        vectors = reduce_vectors(block, dp, shards)

        rows = WIDTH // shards
        g_down, g_read = call(
            unpack_down_kernel,
            "unpack_down",
            [(idx, None)] + [(p, None) for p in pieces_down],
            [((4 * rows, WIDTH), F32, None), ((rows, VOCAB), F32, None)],
            limit=16,
        )
        g_mix, g_up = call(
            unpack_up_kernel,
            "unpack_up",
            [(idx, None)] + [(p, None) for p in pieces_up],
            [((rows, WIDTH), F32, None), ((rows, FF), F32, None)],
            limit=16,
        )
        g_query, g_key, g_value, g_control = call(
            unpack_proj_kernel,
            "unpack_proj",
            [(idx, None)] + [(p, None) for p in pieces_proj[0] + pieces_proj[1]],
            [((rows, WIDTH), F32, None)] * 4,
            limit=16,
        )
        return (
            out, d_tokens, vectors[0], vectors[1], g_query, g_key, g_value, g_control, g_mix,
            vectors[2], vectors[3], g_up, vectors[5:9].reshape(512), g_down, vectors[4], g_read,
        )

    return on_device


def solution(mesh):
    dp, shards = mesh.shape["dp"], mesh.shape["shard"]
    vector, matrix = P("shard"), P("shard", None)
    rows = P(("dp", "shard"), None)
    params = (
        vector, vector, matrix, matrix, matrix, matrix, matrix,
        vector, vector, matrix, vector, matrix, vector, matrix,
    )
    return jax.shard_map(
        body(dp, shards),
        mesh=mesh,
        in_specs=(rows, P(("dp", "shard"))) + params,
        out_specs=(rows, rows) + params,
        check_vma=False,
    )
```

```python
import jax
import jax.numpy as jnp
from jax import lax
from jax.experimental import pallas as pl
from jax.experimental.pallas import tpu as pltpu
from jax.sharding import PartitionSpec as P

EPS = 1e-05
WIDTH = 512
HEAD = 64
FF = 2048
VOCAB = 256
SEQ_LEN = 1024
CHUNK = 256
HALF = 256
PIECE = 16
COLS_PROJ = 4 * HALF
COLS_BOTH = 2 * COLS_PROJ
COLS_LAST = COLS_PROJ + 128
COLS_UP = WIDTH + FF
COLS_DOWN = 4 * WIDTH + VOCAB
F32 = jnp.float32
BF16 = jnp.bfloat16
MIB = 1024 * 1024


def nn(a, b):
    return lax.dot_general(a, b, (((1,), (0,)), ((), ())), preferred_element_type=F32)


def nt(a, b):
    return lax.dot_general(a, b, (((1,), (1,)), ((), ())), preferred_element_type=F32)


def tn(a, b):
    return lax.dot_general(a, b, (((0,), (0,)), ((), ())), preferred_element_type=F32)


def norm_parts(values):
    centre = values - jnp.mean(values, axis=-1, keepdims=True)
    inverse = lax.rsqrt(jnp.mean(centre * centre, axis=-1, keepdims=True) + EPS)
    return centre * inverse, inverse


def norm_pull(grad, unit, inverse, gain):
    scaled = grad * gain
    return inverse * (
        scaled
        - jnp.mean(scaled, axis=-1, keepdims=True)
        - unit * jnp.mean(scaled * unit, axis=-1, keepdims=True)
    )


def vector_of(vec_ref, idx, row):
    return jnp.concatenate(
        [vec_ref[s ^ idx[2], row : row + 1, :].astype(F32) for s in range(4)], axis=1
    )


def bias_up_of(vec_ref, idx):
    return jnp.concatenate(
        [
            vec_ref[s ^ idx[2], row : row + 1, :].astype(F32)
            for s in range(4)
            for row in range(5, 9)
        ],
        axis=1,
    )


def each_piece(idx, near, far):
    for c, buf in ((0, near), (1, far)):
        for xy in range(4):
            member = ((xy ^ idx[1]) * 2) + (c ^ idx[0])
            for s in range(4):
                yield s ^ idx[2], member, buf.at[xy, s]


def each_member(idx, near, far):
    for c, buf in ((0, near), (1, far)):
        for xy in range(4):
            yield None, ((xy ^ idx[1]) * 2) + (c ^ idx[0]), buf.at[xy]


def rows_at(start, size):
    return pl.ds(pl.multiple_of(start, PIECE), size)


def put_parts(idx, keep, send, tile, shard, columns):
    for xy in range(4):
        first = tile[32 * xy : 32 * xy + 16]
        second = tile[32 * xy + 16 : 32 * xy + 32]
        own_first = idx[0] == 0
        keep[xy ^ idx[1], shard ^ idx[2], :, columns] = jnp.where(own_first, first, second)
        send[xy ^ idx[1], shard ^ idx[2], :, columns] = jnp.where(own_first, second, first)


def pack_kernel(
    idx, g1, b1, g2, b2, bd, bu, wq, wk, wv, wc, wm, wu, wd, wr, pa, pc, pd, sems
):
    member = idx[1] * 2 + idx[0]
    across = (idx[1] ^ 3) * 2 + idx[0]
    rows = rows_at(member * PIECE, PIECE)
    moves = []
    for j, w in enumerate((wq, wk, wv, wc)):
        for half in range(2):
            start = half * COLS_PROJ + j * HALF
            part = w.at[rows, half * HALF : (half + 1) * HALF]
            moves.append((part, pa.at[:, start : start + HALF]))
    moves.append((wm.at[rows, :], pc.at[:, :WIDTH]))
    moves.append((wu.at[rows, :], pc.at[:, WIDTH:]))
    for place, who in enumerate((member, across)):
        for i in range(4):
            part = wd.at[rows_at(who * 64 + 16 * i, PIECE), :]
            moves.append((part, pd.at[place, :, i * WIDTH : (i + 1) * WIDTH]))
        moves.append((wr.at[rows_at(who * PIECE, PIECE), :], pd.at[place, :, 4 * WIDTH :]))
    copies = [pltpu.make_async_copy(src, dst, sems.at[i]) for i, (src, dst) in enumerate(moves)]
    for copy in copies:
        copy.start()
    lines = [v[...].astype(F32).reshape(1, 128) for v in (g1, b1, g2, b2, bd)]
    lines += [bu[128 * j : 128 * j + 128].astype(F32).reshape(1, 128) for j in range(4)]
    lines.append(jnp.zeros((7, 128), F32))
    pa[:, COLS_BOTH:] = jnp.concatenate(lines, axis=0).astype(BF16)
    for copy in copies:
        copy.wait()


def first_norm_kernel(idx, vec, x, a1, unit_t, columns):
    unit, _ = norm_parts(x[...].astype(F32))
    gain, shift = vector_of(vec, idx, 0), vector_of(vec, idx, 1)
    a1[...] = (unit * gain + shift).astype(BF16)
    unit_t[...] = unit.astype(BF16).T
    columns[...] = jnp.concatenate([gain, shift, jnp.zeros((6, WIDTH), F32)], axis=0).T


def lanes_low():
    return lax.broadcasted_iota(jnp.int32, (1, 128), 1) < HEAD


def stacked(value):
    low = lanes_low().astype(F32).astype(BF16)
    high = (1.0 - lanes_low().astype(F32)).astype(BF16)
    return jnp.concatenate([value * low, value * high], axis=0)


def join(value):
    return jnp.where(lanes_low(), value[:CHUNK], value[CHUNK:])


def head_sum(value):
    low = lanes_low()
    first = jnp.sum(jnp.where(low, value, 0.0), axis=-1, keepdims=True)
    second = jnp.sum(jnp.where(low, 0.0, value), axis=-1, keepdims=True)
    return jnp.where(low, first, second)


def head_max(value):
    low = lanes_low()
    first = jnp.max(jnp.where(low, value, -jnp.inf), axis=-1, keepdims=True)
    second = jnp.max(jnp.where(low, -jnp.inf, value), axis=-1, keepdims=True)
    return jnp.where(low, first, second)


def same_head():
    row = lax.broadcasted_iota(jnp.int32, (128, 128), 0) < HEAD
    col = lax.broadcasted_iota(jnp.int32, (128, 128), 1) < HEAD
    return row == col


def causal_mask(rows, transposed=False):
    row = lax.broadcasted_iota(jnp.int32, (rows, CHUNK), 0) & (CHUNK - 1)
    col = lax.broadcasted_iota(jnp.int32, (rows, CHUNK), 1)
    return (row <= col) if transposed else (col <= row)


def attend_kernel(
    idx, a1, near, far,
    q_o, k_o, v_o, e_o, x_o, p_o, s_o, z_o, r_o, o_o, kept_s, kept_u, w_o,
    state_s, state_u, count_z,
):
    step = pl.program_id(0)

    @pl.when(step == 0)
    def _():
        for shard, member, piece in each_piece(idx, near, far):
            w_o[rows_at(shard * 128 + member * PIECE, PIECE), :] = piece[...]
        state_s[...] = jnp.zeros_like(state_s)
        state_u[...] = jnp.zeros_like(state_u)
        count_z[...] = jnp.zeros_like(count_z)

    a = a1[...]
    q_o[...] = nn(a, w_o[:, :HALF]).astype(BF16)
    k_o[...] = nn(a, w_o[:, HALF : 2 * HALF]).astype(BF16)
    v_o[...] = nn(a, w_o[:, 2 * HALF : 3 * HALF]).astype(BF16)
    expo = jnp.exp(nn(a, w_o[:, 3 * HALF :]))
    x_o[...] = expo
    e_o[...] = expo.astype(BF16)
    tri = causal_mask(2 * CHUNK)
    total = nn(tri[:CHUNK].astype(F32).astype(BF16), e_o[...]) + count_z[...]
    count_z[...] = total[CHUNK - 1 :, :]
    inverse = 1.0 / total
    z_o[...] = inverse
    for pair in range(2):
        at = slice(128 * pair, 128 * pair + 128)
        q, k, v, e = q_o[:, at], k_o[:, at], v_o[:, at], e_o[:, at]
        inv = inverse[:, at]
        low_s = state_s[pair].astype(BF16)
        low_u = state_u[pair].astype(BF16)
        kept_s[0, pair] = low_s
        kept_u[0, pair] = low_u
        scores = jnp.where(tri, nt(stacked(q), k), 0.0).astype(BF16)
        numer = join(nn(scores, e)) + nn(q, low_s)
        logits = (HEAD ** -0.5) * numer * inv
        expd = jnp.exp(logits - head_max(logits))
        probs = expd / head_sum(expd)
        ratio = (probs * inv).astype(BF16)
        mixing = jnp.where(tri, nt(stacked(ratio), e), 0.0).astype(BF16)
        o_o[:, at] = (join(nn(mixing, v)) + nn(ratio, low_u)).astype(BF16)
        s_o[:, at] = logits
        p_o[:, at] = probs
        r_o[:, at] = ratio
        block = same_head()
        state_s[pair] += jnp.where(block, tn(k, e), 0.0)
        state_u[pair] += jnp.where(block, tn(e, v), 0.0)


def feed_kernel(
    idx, vec, x, o0, o1, target, up_near, up_far, down_near, down_far,
    out_o, h_o, slope_o, dy_o, bias_o, keep, send,
    w_mix, w_up, w_down, w_read, act_s, out_s, dl_s, df_s,
):
    step = pl.program_id(0)

    @pl.when(step == 0)
    def _():
        for shard, member, piece in each_piece(idx, up_near, up_far):
            rows = rows_at(shard * 128 + member * PIECE, PIECE)
            w_mix[rows, :] = piece[:, :WIDTH]
            w_up[rows, :] = piece[:, WIDTH:]
        for shard, member, piece in each_piece(idx, down_near, down_far):
            for i in range(4):
                rows = rows_at(shard * 512 + member * 64 + 16 * i, PIECE)
                w_down[rows, :] = piece[:, i * WIDTH : (i + 1) * WIDTH]
            w_read[rows_at(shard * 128 + member * PIECE, PIECE), :] = piece[:, 4 * WIDTH :]
        bias_o[...] = jnp.zeros_like(bias_o)

    rows = pl.ds(pl.multiple_of(step * CHUNK, CHUNK), CHUNK)
    attn = nn(o0[...], w_mix[:HALF, :]) + nn(o1[...], w_mix[HALF:, :])
    resid = x[...].astype(F32) + attn
    h_o[...] = resid
    unit, _ = norm_parts(resid)
    second = (unit * vector_of(vec, idx, 2) + vector_of(vec, idx, 3)).astype(BF16)
    bias = bias_up_of(vec, idx)
    branch = jnp.zeros((CHUNK, WIDTH), F32)
    scale = (2.0 / jnp.pi) ** 0.5
    for j in range(4):
        at = slice(512 * j, 512 * j + 512)
        z = nn(second, w_up[:, at]) + bias[:, at]
        zz = z * z
        t = jnp.tanh(scale * z * (1.0 + 0.044715 * zz))
        cdf = 0.5 * (1.0 + t)
        act = (z * cdf).astype(BF16)
        slope_o[:, at] = cdf + 0.5 * z * (1.0 - t * t) * (scale * (1.0 + 3 * 0.044715 * zz))
        act_s[rows, at] = act
        branch += nn(act, w_down[at, :])
    out = (resid + (branch + vector_of(vec, idx, 4))).astype(BF16)
    out_o[...] = out
    out_s[rows, :] = out
    logits = nn(out, w_read[...])
    expd = jnp.exp(logits - jnp.max(logits, axis=-1, keepdims=True))
    soft = expd / jnp.sum(expd, axis=-1, keepdims=True)
    classes = lax.broadcasted_iota(jnp.int32, (CHUNK, VOCAB), 1)
    dl = (soft - jnp.where(classes == target[...], 1.0, 0.0)).astype(BF16)
    dl_s[rows, :] = dl
    dy = nt(dl, w_read[...])
    dy_o[...] = dy
    df = dy.astype(BF16)
    df_s[rows, :] = df
    bias_o[...] += jnp.sum(df.astype(F32), axis=0, keepdims=True)

    @pl.when(step == pl.num_programs(0) - 1)
    def _():
        for shard in range(4):
            tile = tn(out_s[:, shard * 128 : shard * 128 + 128], dl_s[...]).astype(BF16)
            put_parts(idx, keep, send, tile, shard, slice(4 * WIDTH, None))
            for xy in range(4):
                start = shard * 512 + xy * 128
                tile = tn(act_s[:, start : start + 128], df_s[...]).astype(BF16)
                own_first = idx[0] == 0
                for i in range(4):
                    first = tile[16 * i : 16 * i + 16]
                    later = tile[64 + 16 * i : 64 + 16 * i + 16]
                    at = slice(i * WIDTH, (i + 1) * WIDTH)
                    keep[xy ^ idx[1], shard ^ idx[2], :, at] = jnp.where(own_first, first, later)
                    send[xy ^ idx[1], shard ^ idx[2], :, at] = jnp.where(own_first, later, first)


def feed_back_kernel(
    idx, vec, h, slope, dy, o0, o1, up_near, up_far, down_near, down_far,
    dh_o, do_o, gain_o, shift_o, bias_o, keep, send,
    w_mix, w_up, w_down, dz_s, a2_s, da_s,
):
    step = pl.program_id(0)

    @pl.when(step == 0)
    def _():
        for shard, member, piece in each_piece(idx, up_near, up_far):
            rows = rows_at(shard * 128 + member * PIECE, PIECE)
            w_mix[rows, :] = piece[:, :WIDTH]
            w_up[rows, :] = piece[:, WIDTH:]
        for shard, member, piece in each_piece(idx, down_near, down_far):
            for i in range(4):
                rows = rows_at(shard * 512 + member * 64 + 16 * i, PIECE)
                w_down[rows, :] = piece[:, i * WIDTH : (i + 1) * WIDTH]
        gain_o[...] = jnp.zeros_like(gain_o)
        shift_o[...] = jnp.zeros_like(shift_o)
        bias_o[...] = jnp.zeros_like(bias_o)

    rows = pl.ds(pl.multiple_of(step * CHUNK, CHUNK), CHUNK)
    gain = vector_of(vec, idx, 2)
    unit, inverse = norm_parts(h[...])
    a2_s[rows, :] = (unit * gain + vector_of(vec, idx, 3)).astype(BF16)
    d_out = dy[...]
    df = d_out.astype(BF16)
    d_second = jnp.zeros((CHUNK, WIDTH), F32)
    for j in range(4):
        at = slice(512 * j, 512 * j + 512)
        dz = (nt(df, w_down[at, :]) * slope[:, at]).astype(BF16)
        dz_s[rows, at] = dz
        bias_o[:, at] += jnp.sum(dz.astype(F32), axis=0, keepdims=True)
        d_second += nt(dz, w_up[:, at])
    gain_o[...] += jnp.sum(d_second * unit, axis=0, keepdims=True)
    shift_o[...] += jnp.sum(d_second, axis=0, keepdims=True)
    dh = d_out + norm_pull(d_second, unit, inverse, gain)
    dh_o[...] = dh
    da = dh.astype(BF16)
    da_s[rows, :] = da
    do_o[...] = nt(da, w_mix[...]).astype(BF16)

    @pl.when(step == pl.num_programs(0) - 1)
    def _():
        for shard in range(4):
            half = (o0, o1)[shard // 2]
            start = (shard % 2) * 128
            tile = tn(half[:, start : start + 128], da_s[...]).astype(BF16)
            put_parts(idx, keep, send, tile, shard, slice(0, WIDTH))
            for j in range(4):
                tile = tn(
                    a2_s[:, shard * 128 : shard * 128 + 128], dz_s[:, 512 * j : 512 * j + 512]
                ).astype(BF16)
                at = slice(WIDTH + 512 * j, WIDTH + 512 * j + 512)
                put_parts(idx, keep, send, tile, shard, at)


def proj_gradient(idx, unit_t, columns, w, dx, keep, send):
    ones = jnp.ones((PIECE, dx.shape[0]), BF16)
    sums = nn(ones, dx[...])[:1]
    shares = []
    for shard in range(4):
        rows = slice(shard * 128, shard * 128 + 128)
        gain, shift = columns[rows, 0:1], columns[rows, 1:2]
        on_gain = jnp.zeros((128, HALF), F32)
        on_shift = jnp.zeros((128, HALF), F32)
        for j in range(4):
            at = slice(j * HALF, (j + 1) * HALF)
            tile = nn(unit_t[rows, :], dx[:, at])
            weight = w[rows, at].astype(F32)
            on_gain += tile * weight
            on_shift += weight * sums[:, at]
            put_parts(idx, keep, send, (tile * gain + shift * sums[:, at]).astype(BF16), shard, at)
        both = [jnp.sum(v, axis=1, keepdims=True) for v in (on_gain, on_shift)]
        shares.append(jnp.concatenate(both + [jnp.zeros((128, 6), F32)], axis=1))
    return jnp.concatenate(shares, axis=0).T


def attend_back_kernel(
    idx, unit_t, columns, w, q_i, k_i, v_i, e_i, x_i, p_i, s_i, z_i, r_i, do_i, kept_s, kept_u,
    dx_o, keep, send, share_o,
    state_r, state_t, count_z, dx_s,
):
    attend_back_step(
        q_i, k_i, v_i, e_i, x_i, p_i, s_i, z_i, r_i, do_i, kept_s, kept_u,
        dx_o, state_r, state_t, count_z, dx_s,
    )

    @pl.when(pl.program_id(0) == pl.num_programs(0) - 1)
    def _():
        share_o[...] = proj_gradient(idx, unit_t, columns, w, dx_s, keep, send)


def attend_back_last_kernel(
    idx, unit_t, columns, w, q_i, k_i, v_i, e_i, x_i, p_i, s_i, z_i, r_i, do_i, kept_s, kept_u,
    share, g_g2, g_b2, g_bd, g_bu,
    dx_o, keep, send,
    state_r, state_t, count_z, dx_s,
):
    attend_back_step(
        q_i, k_i, v_i, e_i, x_i, p_i, s_i, z_i, r_i, do_i, kept_s, kept_u,
        dx_o, state_r, state_t, count_z, dx_s,
    )

    @pl.when(pl.program_id(0) == pl.num_programs(0) - 1)
    def _():
        total = proj_gradient(idx, unit_t, columns, w, dx_s, keep, send) + share[...]
        for s in range(4):
            at = slice(128 * s, 128 * s + 128)
            lines = [total[:2, at], g_g2[:, at], g_b2[:, at], g_bd[:, at]]
            lines += [g_bu[:, 512 * s + 128 * j : 512 * s + 128 * j + 128] for j in range(4)]
            lines.append(jnp.zeros((7, 128), F32))
            block = jnp.concatenate(lines, axis=0).astype(BF16)
            for xy in range(4):
                keep[xy, s ^ idx[2], :, COLS_PROJ:] = block
                send[xy, s ^ idx[2], :, COLS_PROJ:] = block


def attend_back_step(
    q_i, k_i, v_i, e_i, x_i, p_i, s_i, z_i, r_i, do_i, kept_s, kept_u,
    dx_o, state_r, state_t, count_z, dx_s,
):
    step = pl.program_id(0)
    chunk = pl.num_programs(0) - 1 - step

    @pl.when(step == 0)
    def _():
        state_r[...] = jnp.zeros_like(state_r)
        state_t[...] = jnp.zeros_like(state_t)
        count_z[...] = jnp.zeros_like(count_z)

    rows = pl.ds(pl.multiple_of(chunk * CHUNK, CHUNK), CHUNK)
    tri = causal_mask(2 * CHUNK)
    trt = causal_mask(2 * CHUNK, True)
    later = trt[:CHUNK].astype(F32).astype(BF16)
    for pair in range(2):
        at = slice(128 * pair, 128 * pair + 128)
        q, k, v, e = q_i[:, at], k_i[:, at], v_i[:, at], e_i[:, at]
        ratio, do = r_i[:, at], do_i[:, at]
        probs, logits, inv = p_i[:, at], s_i[:, at], z_i[:, at]
        low_s, low_u = kept_s[0, pair], kept_u[0, pair]
        low_r = state_r[pair].astype(BF16)
        low_t = state_t[pair].astype(BF16)
        d_mix = jnp.where(tri, nt(stacked(do), v), 0.0).astype(BF16)
        d_ratio = (join(nn(d_mix, e)) + nt(do, low_u)) * inv
        d_logits = probs * (d_ratio - head_sum(d_ratio * probs))
        d_numer = ((HEAD ** -0.5) * d_logits * inv).astype(BF16)
        d_total = (-d_ratio * (probs * inv) - d_logits * logits * inv).astype(BF16)
        d_scores = jnp.where(tri, nt(stacked(d_numer), e), 0.0).astype(BF16)
        dq = join(nn(d_scores, k)) + nt(d_numer, low_s)
        scores = jnp.where(trt, nt(stacked(k), q), 0.0).astype(BF16)
        wide_e = stacked(e)
        mixing = jnp.where(trt, nt(wide_e, ratio), 0.0).astype(BF16)
        d_mix_t = jnp.where(trt, nt(stacked(v), do), 0.0).astype(BF16)
        d_scores_t = jnp.where(trt, nt(wide_e, d_numer), 0.0).astype(BF16)
        dv = join(nn(mixing, do)) + nn(e, low_r)
        dk = join(nn(d_scores_t, q)) + nt(e, low_t)
        total_z = nn(later, d_total) + count_z[:, at]
        count_z[:, at] = total_z[:1, :]
        de = join(nn(d_mix_t, ratio) + nn(scores, d_numer)) + nt(v, low_r) + nn(k, low_t) + total_z
        dc = de * x_i[:, at]
        for j, value in enumerate((dq, dk, dv, dc)):
            dx_o[:, j * HALF + 128 * pair : j * HALF + 128 * pair + 128] = value.astype(BF16)
        block = same_head()
        state_r[pair] += jnp.where(block, tn(ratio, do), 0.0)
        state_t[pair] += jnp.where(block, tn(q, d_numer), 0.0)
    dx_s[rows, :] = dx_o[...]


def inputs_kernel(idx, vec, x, dh, dx0, dx1, w0, w1, dx_o):
    unit, inverse = norm_parts(x[...].astype(F32))
    d_first = nt(dx0[...], w0[...]) + nt(dx1[...], w1[...])
    dx_o[...] = dh[...] + norm_pull(d_first, unit, inverse, vector_of(vec, idx, 0))


def unpack_proj_kernel(idx, near, far, query, key, value, control, g1, b1, g2, b2, bd, bu):
    for shard, member, piece in each_member(idx, near, far):
        rows = rows_at(member * PIECE, PIECE)
        for j, out in enumerate((query, key, value, control)):
            for half in range(2):
                start = half * COLS_PROJ + j * HALF
                out[rows, half * HALF : (half + 1) * HALF] = piece[:, start : start + HALF].astype(F32)

        @pl.when(member == 0)
        def _():
            lines = piece[:, COLS_BOTH:].astype(F32)
            for i, out in enumerate((g1, b1, g2, b2, bd)):
                out[...] = lines[i]
            for i in range(4):
                bu[128 * i : 128 * i + 128] = lines[5 + i]


def unpack_feed_kernel(idx, near, far, mix, up, down, read):
    for shard, member, piece in each_member(idx, near, far):
        rows = rows_at(member * PIECE, PIECE)
        mix[rows, :] = piece[:, :WIDTH].astype(F32)
        up[rows, :] = piece[:, WIDTH:COLS_UP].astype(F32)
        for i in range(4):
            start = COLS_UP + i * WIDTH
            down[rows_at(member * 64 + 16 * i, PIECE), :] = piece[:, start : start + WIDTH].astype(F32)
        read[rows, :] = piece[:, COLS_UP + 4 * WIDTH :].astype(F32)


def shaped(shape, dtype):
    return jax.ShapeDtypeStruct(shape, dtype)


def call(kernel, name, args, outs, steps=None, scratch=(), flops=0, limit=56):
    grid = (steps,) if steps else ()

    def spec(shape, block):
        if block is None:
            return pl.BlockSpec(tuple(shape), lambda *_: (0,) * len(shape))
        return pl.BlockSpec(*block)

    in_specs = []
    for array, block in args:
        if array.dtype == jnp.int32 and array.shape == (3,):
            in_specs.append(pl.BlockSpec(memory_space=pltpu.SMEM))
        elif block == "hbm":
            in_specs.append(pl.BlockSpec(memory_space=pl.ANY))
        else:
            in_specs.append(spec(array.shape, block))
    moved = sum(a.size * a.dtype.itemsize for a, _ in args)
    return pl.pallas_call(
        kernel,
        grid=grid,
        in_specs=in_specs,
        out_specs=[spec(shape, block) for shape, _, block in outs],
        out_shape=[shaped(shape, dtype) for shape, dtype, _ in outs],
        scratch_shapes=list(scratch),
        compiler_params=pltpu.CompilerParams(
            vmem_limit_bytes=limit * MIB,
            dimension_semantics=("arbitrary",) * len(grid) if grid else None,
        ),
        cost_estimate=pl.CostEstimate(flops=int(flops), bytes_accessed=int(moved), transcendentals=0),
        name=name,
    )(*[array for array, _ in args])


def swap(value, axis, size, distance):
    return lax.ppermute(value, axis, [(i, i ^ distance) for i in range(size)])


def pin(*values):
    return lax.optimization_barrier(values)


def near_rows(piece, shards):
    return [swap(piece, "shard", shards, k) for k in range(1, 4)]


def sum_of(values):
    values = [v.astype(F32) for v in values]
    return ((values[0] + values[1]) + (values[2] + values[3])).astype(BF16)


def core_sum(keep, got):
    return [(keep[k].astype(F32) + got[k].astype(F32)).astype(BF16) for k in range(4)]


def plane_start(parts, dp):
    return [swap(parts[k], "dp", dp, 2 * k) for k in range(1, 4)]


def plane_sum(parts, got):
    return [sum_of([parts[0][k], got[0][k], got[1][k], got[2][k]]) for k in range(4)]


def shard_start(rows, shards):
    return [swap(rows[k], "shard", shards, k) for k in range(1, 4)]


def shard_sum(rows, got, dp):
    total = sum_of([rows[0]] + got)
    distance = 8
    while distance < dp:
        total = (total.astype(F32) + swap(total, "dp", dp, distance).astype(F32)).astype(BF16)
        distance *= 2
    return total


def spread(total, dp):
    pair = jnp.stack([total, swap(total, "dp", dp, 2)])
    near = jnp.concatenate([pair, swap(pair, "dp", dp, 4)])
    return near, swap(near, "dp", dp, 1)


def body(dp, shards):
    def on_device(
        tokens, targets, gain_one, bias_one, w_query, w_key, w_value, w_control, w_mix,
        gain_two, bias_two, w_up, bias_up, w_down, bias_down, w_read,
    ):
        count = tokens.shape[0]
        steps = count // CHUNK
        rows = WIDTH // shards
        member = lax.axis_index("dp") % 8
        idx = jnp.stack([member % 2, member // 2, lax.axis_index("shard")]).astype(jnp.int32)
        forward = lambda i: (i, 0)
        back = lambda i: (steps - 1 - i, 0)
        tok = lambda n: ((CHUNK, n), forward)
        parts = (4, 4, PIECE)

        weights = (w_query, w_key, w_value, w_control, w_mix, w_up, w_down, w_read)
        sizes = [(PIECE, COLS_BOTH + 128), (PIECE, COLS_UP), (2, PIECE, COLS_DOWN)]
        vectors = (gain_one, bias_one, gain_two, bias_two, bias_down, bias_up)
        pa, pu, pd = call(
            pack_kernel,
            "pack_weights",
            [(idx, None)] + [(v, None) for v in vectors] + [(w, "hbm") for w in weights],
            [(size, BF16, None) for size in sizes],
            scratch=[pltpu.SemaphoreType.DMA((20,))],
        )
        pa, pu, pd = pin(pa, pu, pd)
        got_a = near_rows(pa, shards)
        rows_a = jnp.stack([pa[:, :COLS_BOTH]] + [g[:, :COLS_BOTH] for g in got_a])
        vec = jnp.stack([pa[:, COLS_BOTH:]] + [g[:, COLS_BOTH:] for g in got_a])
        rows_a, vec, pu, pd, tokens_a = pin(rows_a, vec, pu, pd, tokens)
        plane_a = [swap(rows_a, "dp", dp, 2 * k) for k in range(1, 4)]
        got_u = near_rows(pu, shards)
        got_d = near_rows(pd, shards)
        a1, unit_t, columns = call(
            first_norm_kernel,
            "first_norm",
            [(idx, None), (vec, None), (tokens_a, None)],
            [
                ((count, WIDTH), BF16, None),
                ((WIDTH, count), BF16, None),
                ((WIDTH, 8), F32, None),
            ],
        )
        target = targets.reshape(count, 1)
        plane_a, a1, unit_t, columns, target = pin(plane_a, a1, unit_t, columns, target)
        near_a = jnp.stack([rows_a] + plane_a)
        far_a = swap(near_a, "dp", dp, 1)
        near_a, got_u, got_d, a1 = pin(near_a, got_u, got_d, a1)
        rows_u = jnp.stack([pu] + got_u)
        plane_u = [swap(rows_u, "dp", dp, 2 * k) for k in range(1, 4)]
        rows_d = jnp.stack([pd] + got_d)
        plane_d = [swap(rows_d[:, 0], "dp", dp, 2 * k) for k in range(1, 3)]
        far_a, a1 = pin(far_a, a1)

        kept = ((1, 2, 128, 128), lambda i: (i, 0, 0, 0))

        def attend(a1, half):
            at = ((4, 4, PIECE, COLS_PROJ), lambda i: (0, 0, 0, half))
            names = [((count, HALF), t, tok(HALF)) for t in (BF16,) * 4 + (F32,) * 4 + (BF16,) * 2]
            states = [((steps, 2, 128, 128), BF16, kept)] * 2
            return call(
                attend_kernel,
                "attend",
                [(idx, None), (a1, tok(WIDTH)), (near_a, at), (far_a, at)],
                names + states + [((WIDTH, COLS_PROJ), BF16, None)],
                steps,
                [
                    pltpu.VMEM((2, 128, 128), F32),
                    pltpu.VMEM((2, 128, 128), F32),
                    pltpu.VMEM((1, HALF), F32),
                ],
                flops=6e9,
            )

        first = attend(a1, 0)
        first, plane_u, plane_d, a1 = pin(first, plane_u, plane_d, a1)
        near_u = jnp.stack([rows_u] + plane_u)
        far_u = swap(near_u, "dp", dp, 1)
        near_d = jnp.stack([rows_d[:, 0]] + plane_d + [rows_d[:, 1]])
        far_d = swap(near_d, "dp", dp, 1)
        second = attend(a1, 1)
        second, far_u, far_d = pin(second, far_u, far_d)
        halves = (first, second)
        o0, o1 = first[9], second[9]

        out, h, slope, dy, g_bias_down, keep_d, send_d = call(
            feed_kernel,
            "feed_forward",
            [
                (idx, None), (vec, None), (tokens, tok(WIDTH)), (o0, tok(HALF)), (o1, tok(HALF)),
                (target, tok(1)), (near_u, None), (far_u, None), (near_d, None), (far_d, None),
            ],
            [
                ((count, WIDTH), BF16, tok(WIDTH)),
                ((count, WIDTH), F32, tok(WIDTH)),
                ((count, FF), F32, tok(FF)),
                ((count, WIDTH), F32, tok(WIDTH)),
                ((1, WIDTH), F32, None),
                (parts + (COLS_DOWN,), BF16, None),
                (parts + (COLS_DOWN,), BF16, None),
            ],
            steps,
            [
                pltpu.VMEM((WIDTH, WIDTH), BF16),
                pltpu.VMEM((WIDTH, FF), BF16),
                pltpu.VMEM((FF, WIDTH), BF16),
                pltpu.VMEM((WIDTH, VOCAB), BF16),
                pltpu.VMEM((count, FF), BF16),
                pltpu.VMEM((count, WIDTH), BF16),
                pltpu.VMEM((count, VOCAB), BF16),
                pltpu.VMEM((count, WIDTH), BF16),
            ],
            flops=8e9,
        )
        got_d = swap(send_d, "dp", dp, 1)

        dh, d_mixed, g_gain_two, g_bias_two, g_bias_up, keep_u, send_u = call(
            feed_back_kernel,
            "feed_backward",
            [
                (idx, None), (vec, None), (h, tok(WIDTH)), (slope, tok(FF)), (dy, tok(WIDTH)),
                (o0, None), (o1, None),
                (near_u, None), (far_u, None), (near_d, None), (far_d, None),
            ],
            [
                ((count, WIDTH), F32, tok(WIDTH)),
                ((count, WIDTH), BF16, tok(WIDTH)),
                ((1, WIDTH), F32, None),
                ((1, WIDTH), F32, None),
                ((1, FF), F32, None),
                (parts + (COLS_UP,), BF16, None),
                (parts + (COLS_UP,), BF16, None),
            ],
            steps,
            [
                pltpu.VMEM((WIDTH, WIDTH), BF16),
                pltpu.VMEM((WIDTH, FF), BF16),
                pltpu.VMEM((FF, WIDTH), BF16),
                pltpu.VMEM((count, FF), BF16),
                pltpu.VMEM((count, WIDTH), BF16),
                pltpu.VMEM((count, WIDTH), BF16),
            ],
            flops=8e9,
        )
        got_d, d_mixed, send_u = pin(got_d, d_mixed, send_u)
        got_u = swap(send_u, "dp", dp, 1)
        sum_d = core_sum(keep_d, got_d)
        sum_d, d_mixed = pin(sum_d, d_mixed)
        got_d = plane_start(sum_d, dp)

        kept_back = ((1, 2, 128, 128), lambda i: (steps - 1 - i, 0, 0, 0))

        def attend_back(half, d_mixed, extra=()):
            q, k, v, e, x, p, s, z, r, _, ks, ku, w = halves[half]
            tb = ((CHUNK, HALF), back)
            column = ((CHUNK, HALF), lambda i: (steps - 1 - i, half))
            last = half == 1
            cols = COLS_LAST if last else COLS_PROJ
            return call(
                attend_back_last_kernel if last else attend_back_kernel,
                "attend_backward",
                [(idx, None), (unit_t, None), (columns, None), (w, None)]
                + [(t, tb) for t in (q, k, v, e, x, p, s, z, r)]
                + [(d_mixed, column), (ks, kept_back), (ku, kept_back)]
                + [(t, None) for t in extra],
                [
                    ((count, COLS_PROJ), BF16, ((CHUNK, COLS_PROJ), back)),
                    (parts + (cols,), BF16, None),
                    (parts + (cols,), BF16, None),
                ]
                + ([] if last else [((8, WIDTH), F32, None)]),
                steps,
                [
                    pltpu.VMEM((2, 128, 128), F32),
                    pltpu.VMEM((2, 128, 128), F32),
                    pltpu.VMEM((1, HALF), F32),
                    pltpu.VMEM((count, COLS_PROJ), BF16),
                ],
                flops=10e9,
            )

        dx0, keep_a, send_a, share = attend_back(0, d_mixed)
        got_d, got_u, send_a, d_mixed = pin(got_d, got_u, send_a, d_mixed)
        got_a = swap(send_a, "dp", dp, 1)
        sum_u = core_sum(keep_u, got_u)
        rows_d = plane_sum(sum_d, got_d)
        sum_u, rows_d, d_mixed = pin(sum_u, rows_d, d_mixed)
        got_u = plane_start(sum_u, dp)
        got_d = shard_start(rows_d, shards)

        extra = (share, g_gain_two, g_bias_two, g_bias_down, g_bias_up)
        dx1, keep_b, send_b = attend_back(1, d_mixed, extra)
        got_d, got_u, got_a, send_b, dx1 = pin(got_d, got_u, got_a, send_b, dx1)
        got_b = swap(send_b, "dp", dp, 1)
        sum_p = [
            jnp.concatenate(both, axis=-1)
            for both in zip(core_sum(keep_a, got_a), core_sum(keep_b, got_b))
        ]
        sum_p, got_u, dx1 = pin(sum_p, got_u, dx1)
        got_p = plane_start(sum_p, dp)
        rows_u = plane_sum(sum_u, got_u)
        got_u = shard_start(rows_u, shards)
        d_tokens = call(
            inputs_kernel,
            "input_gradient",
            [
                (idx, None), (vec, None), (tokens, tok(WIDTH)), (dh, tok(WIDTH)),
                (dx0, tok(COLS_PROJ)), (dx1, tok(COLS_PROJ)),
                (first[12], None), (second[12], None),
            ],
            [((count, WIDTH), F32, tok(WIDTH))],
            steps,
            flops=3e9,
        )[0]
        got_p, got_u, got_d, d_tokens = pin(got_p, got_u, got_d, d_tokens)
        rows_p = plane_sum(sum_p, got_p)
        got_p = shard_start(rows_p, shards)
        total_u = shard_sum(rows_u, got_u, dp)
        total_d = shard_sum(rows_d, got_d, dp)
        near_f, far_f = spread(jnp.concatenate([total_u, total_d], axis=-1), dp)
        near_p, far_p = spread(shard_sum(rows_p, got_p, dp), dp)
        g_mix, g_up, g_down, g_read = call(
            unpack_feed_kernel,
            "unpack_feed",
            [(idx, None), (near_f, None), (far_f, None)],
            [
                ((rows, WIDTH), F32, None),
                ((rows, FF), F32, None),
                ((4 * rows, WIDTH), F32, None),
                ((rows, VOCAB), F32, None),
            ],
        )
        g_query, g_key, g_value, g_control, g1, b1, g2, b2, bd, bu = call(
            unpack_proj_kernel,
            "unpack_proj",
            [(idx, None), (near_p, None), (far_p, None)],
            [((rows, WIDTH), F32, None)] * 4 + [((128,), F32, None)] * 5 + [((512,), F32, None)],
        )
        return (
            out, d_tokens, g1, b1, g_query, g_key, g_value, g_control, g_mix,
            g2, b2, g_up, bu, g_down, bd, g_read,
        )

    return on_device


def solution(mesh):
    dp, shards = mesh.shape["dp"], mesh.shape["shard"]
    vector, matrix = P("shard"), P("shard", None)
    rows = P(("dp", "shard"), None)
    params = (
        vector, vector, matrix, matrix, matrix, matrix, matrix,
        vector, vector, matrix, vector, matrix, vector, matrix,
    )
    return jax.shard_map(
        body(dp, shards),
        mesh=mesh,
        in_specs=(rows, P(("dp", "shard"))) + params,
        out_specs=(rows, rows) + params,
        check_vma=False,
    )
```

```python
import jax
import jax.numpy as jnp
from jax import lax
from jax.experimental import pallas as pl
from jax.experimental.pallas import tpu as pltpu
from jax.sharding import PartitionSpec as P

EPS = 1e-05
WIDTH = 512
HEAD = 64
FF = 2048
VOCAB = 256
SEQ_LEN = 1024
CHUNK = 256
SUB = 128
HALF = 256
PIECE = 16
COLS_PROJ = 4 * HALF
COLS_BOTH = 2 * COLS_PROJ
COLS_LAST = COLS_PROJ + 128
COLS_UP = WIDTH + FF
COLS_DOWN = 4 * WIDTH + VOCAB
F32 = jnp.float32
BF16 = jnp.bfloat16
MIB = 1024 * 1024


def nn(a, b):
    return lax.dot_general(a, b, (((1,), (0,)), ((), ())), preferred_element_type=F32)


def nt(a, b):
    return lax.dot_general(a, b, (((1,), (1,)), ((), ())), preferred_element_type=F32)


def tn(a, b):
    return lax.dot_general(a, b, (((0,), (0,)), ((), ())), preferred_element_type=F32)


def norm_parts(values):
    centre = values - jnp.mean(values, axis=-1, keepdims=True)
    inverse = lax.rsqrt(jnp.mean(centre * centre, axis=-1, keepdims=True) + EPS)
    return centre * inverse, inverse


def norm_pull(grad, unit, inverse, gain):
    scaled = grad * gain
    return inverse * (
        scaled
        - jnp.mean(scaled, axis=-1, keepdims=True)
        - unit * jnp.mean(scaled * unit, axis=-1, keepdims=True)
    )


def vector_of(vec_ref, idx, row):
    return jnp.concatenate(
        [vec_ref[s ^ idx[2], row : row + 1, :].astype(F32) for s in range(4)], axis=1
    )


def bias_up_of(vec_ref, idx):
    return jnp.concatenate(
        [
            vec_ref[s ^ idx[2], row : row + 1, :].astype(F32)
            for s in range(4)
            for row in range(5, 9)
        ],
        axis=1,
    )


def each_piece(idx, near, far):
    for c, buf in ((0, near), (1, far)):
        for xy in range(4):
            member = ((xy ^ idx[1]) * 2) + (c ^ idx[0])
            for s in range(4):
                yield s ^ idx[2], member, buf.at[xy, s]


def each_member(idx, near, far):
    for c, buf in ((0, near), (1, far)):
        for xy in range(4):
            yield None, ((xy ^ idx[1]) * 2) + (c ^ idx[0]), buf.at[xy]


def rows_at(start, size):
    return pl.ds(pl.multiple_of(start, PIECE), size)


def put_parts(idx, keep, send, tile, shard, columns):
    for xy in range(4):
        first = tile[32 * xy : 32 * xy + 16]
        second = tile[32 * xy + 16 : 32 * xy + 32]
        own_first = idx[0] == 0
        keep[xy ^ idx[1], shard ^ idx[2], :, columns] = jnp.where(own_first, first, second)
        send[xy ^ idx[1], shard ^ idx[2], :, columns] = jnp.where(own_first, second, first)


def pack_kernel(
    idx, g1, b1, g2, b2, bd, bu, wq, wk, wv, wc, wm, wu, wd, wr, pa, pc, pd, sems
):
    member = idx[1] * 2 + idx[0]
    across = (idx[1] ^ 3) * 2 + idx[0]
    rows = rows_at(member * PIECE, PIECE)
    moves = []
    for j, w in enumerate((wq, wk, wv, wc)):
        for half in range(2):
            start = half * COLS_PROJ + j * HALF
            part = w.at[rows, half * HALF : (half + 1) * HALF]
            moves.append((part, pa.at[:, start : start + HALF]))
    moves.append((wm.at[rows, :], pc.at[:, :WIDTH]))
    moves.append((wu.at[rows, :], pc.at[:, WIDTH:]))
    for place, who in enumerate((member, across)):
        for i in range(4):
            part = wd.at[rows_at(who * 64 + 16 * i, PIECE), :]
            moves.append((part, pd.at[place, :, i * WIDTH : (i + 1) * WIDTH]))
        moves.append((wr.at[rows_at(who * PIECE, PIECE), :], pd.at[place, :, 4 * WIDTH :]))
    copies = [pltpu.make_async_copy(src, dst, sems.at[i]) for i, (src, dst) in enumerate(moves)]
    for copy in copies:
        copy.start()
    lines = [v[...].astype(F32).reshape(1, 128) for v in (g1, b1, g2, b2, bd)]
    lines += [bu[128 * j : 128 * j + 128].astype(F32).reshape(1, 128) for j in range(4)]
    lines.append(jnp.zeros((7, 128), F32))
    pa[:, COLS_BOTH:] = jnp.concatenate(lines, axis=0).astype(BF16)
    for copy in copies:
        copy.wait()


def first_norm_kernel(idx, vec, x, a1, unit_t, columns):
    unit, _ = norm_parts(x[...].astype(F32))
    gain, shift = vector_of(vec, idx, 0), vector_of(vec, idx, 1)
    a1[...] = (unit * gain + shift).astype(BF16)
    unit_t[...] = unit.astype(BF16).T
    columns[...] = jnp.concatenate([gain, shift, jnp.zeros((6, WIDTH), F32)], axis=0).T


def lanes_low():
    return lax.broadcasted_iota(jnp.int32, (1, 128), 1) < HEAD


def stacked(value):
    low = lanes_low().astype(F32).astype(BF16)
    high = (1.0 - lanes_low().astype(F32)).astype(BF16)
    return jnp.concatenate([value * low, value * high], axis=0)


def head_ones():
    row = (lax.broadcasted_iota(jnp.int32, (256, 128), 0) & 127) < HEAD
    col = lax.broadcasted_iota(jnp.int32, (256, 128), 1) < HEAD
    return (row == col).astype(F32).astype(BF16)


def head_sum(value, ones):
    high = value.astype(BF16)
    rest = (value - high.astype(F32)).astype(BF16)
    return nn(side(high, rest), ones)


def sub_places(subs):
    return [
        (sub, pair, slice(SUB * sub, SUB * sub + SUB), slice(128 * pair, 128 * pair + 128))
        for sub in subs
        for pair in range(2)
    ]


def head_max(value):
    low = lanes_low()
    first = jnp.max(jnp.where(low, value, -jnp.inf), axis=-1, keepdims=True)
    second = jnp.max(jnp.where(low, -jnp.inf, value), axis=-1, keepdims=True)
    return jnp.where(low, first, second)


def same_head():
    row = lax.broadcasted_iota(jnp.int32, (128, 256), 0) < HEAD
    col = (lax.broadcasted_iota(jnp.int32, (128, 256), 1) & 127) < HEAD
    return row == col


def causal_pair(transposed=False):
    row = lax.broadcasted_iota(jnp.int32, (SUB, 2 * SUB), 0)
    col = lax.broadcasted_iota(jnp.int32, (SUB, 2 * SUB), 1) & (SUB - 1)
    return (row <= col) if transposed else (col <= row)


def causal_whole(transposed=False):
    row = lax.broadcasted_iota(jnp.int32, (CHUNK, CHUNK), 0)
    col = lax.broadcasted_iota(jnp.int32, (CHUNK, CHUNK), 1)
    keep = (row <= col) if transposed else (col <= row)
    return keep.astype(F32).astype(BF16)


def side(*values):
    return jnp.concatenate(values, axis=1)


def masked(keep, value):
    return jnp.where(keep, value, 0.0).astype(BF16)


def attend_kernel(idx, a1, near, far, proj_o, float_o, mixed_o, kept, w_o, state, count_z):
    step = pl.program_id(0)

    @pl.when(step == 0)
    def _():
        for shard, member, piece in each_piece(idx, near, far):
            w_o[rows_at(shard * 128 + member * PIECE, PIECE), :] = piece[...]
        state[...] = jnp.zeros_like(state)
        count_z[...] = jnp.zeros_like(count_z)

    a = a1[...]
    q_all = nn(a, w_o[:, :HALF]).astype(BF16)
    k_all = nn(a, w_o[:, HALF : 2 * HALF]).astype(BF16)
    expo = jnp.exp(nn(a, w_o[:, 3 * HALF :]))
    e_all = expo.astype(BF16)
    v_all = nn(a, w_o[:, 2 * HALF : 3 * HALF]).astype(BF16)
    for j, value in enumerate((q_all, k_all, v_all, e_all)):
        proj_o[:, j * HALF : (j + 1) * HALF] = value
    float_o[:, :HALF] = expo
    total = nn(causal_whole(), e_all) + count_z[...]
    count_z[...] = total[CHUNK - 1 :, :]
    inverse = 1.0 / total
    float_o[:, HALF : 2 * HALF] = inverse
    tri, block, ones = causal_pair(), same_head(), head_ones()
    places = sub_places((0, 1))
    lows, wide_e, numers, ratios = {}, {}, {}, {}
    for pair in range(2):
        current = state[pair]
        for sub in range(2):
            rows, at = slice(SUB * sub, SUB * sub + SUB), slice(128 * pair, 128 * pair + 128)
            lows[sub, pair] = current.astype(BF16)
            kept[sub, pair] = lows[sub, pair]
            wide_e[sub, pair] = stacked(e_all[rows, at])
            more = tn(e_all[rows, at], side(k_all[rows, at], v_all[rows, at]))
            current = current + jnp.where(block, more, 0.0)
        state[pair] = current
    for sub, pair, rows, at in places:
        scores = masked(tri, nt(q_all[rows, at], stacked(k_all[rows, at])))
        numer = nn(scores, wide_e[sub, pair])
        numers[sub, pair] = numer + nt(q_all[rows, at], lows[sub, pair][:, :128])

    def soften(sub, pair, rows, at):
        inv = inverse[rows, at]
        logits = (HEAD ** -0.5) * numers[sub, pair] * inv
        expd = jnp.exp(logits - head_max(logits))
        probs = expd * (1.0 / head_sum(expd, ones))
        ratios[sub, pair] = (probs * inv).astype(BF16)
        float_o[rows, 2 * HALF + 128 * pair : 2 * HALF + 128 * pair + 128] = logits
        float_o[rows, 3 * HALF + 128 * pair : 3 * HALF + 128 * pair + 128] = probs
        mixed_o[rows, at] = ratios[sub, pair]

    def mix(sub, pair, rows, at):
        mixing = masked(tri, nt(ratios[sub, pair], wide_e[sub, pair]))
        out = nn(mixing, stacked(v_all[rows, at])) + nn(ratios[sub, pair], lows[sub, pair][:, 128:])
        mixed_o[rows, HALF + 128 * pair : HALF + 128 * pair + 128] = out.astype(BF16)

    for i, place in enumerate(places):
        soften(*place)
        if i:
            mix(*places[i - 1])
    mix(*places[-1])


def feed_kernel(
    idx, vec, x, o0, o1, target, up_near, up_far, down_near, down_far,
    out_o, h_o, slope_o, dy_o, bias_o, keep, send,
    w_mix, w_up, w_down, w_read, act_s, out_s, dl_s, df_s,
):
    step = pl.program_id(0)

    @pl.when(step == 0)
    def _():
        for shard, member, piece in each_piece(idx, up_near, up_far):
            rows = rows_at(shard * 128 + member * PIECE, PIECE)
            w_mix[rows, :] = piece[:, :WIDTH]
            w_up[rows, :] = piece[:, WIDTH:]
        for shard, member, piece in each_piece(idx, down_near, down_far):
            for i in range(4):
                rows = rows_at(shard * 512 + member * 64 + 16 * i, PIECE)
                w_down[rows, :] = piece[:, i * WIDTH : (i + 1) * WIDTH]
            w_read[rows_at(shard * 128 + member * PIECE, PIECE), :] = piece[:, 4 * WIDTH :]
        bias_o[...] = jnp.zeros_like(bias_o)

    rows = pl.ds(pl.multiple_of(step * CHUNK, CHUNK), CHUNK)
    attn = nn(o0[...], w_mix[:HALF, :]) + nn(o1[...], w_mix[HALF:, :])
    resid = x[...].astype(F32) + attn
    h_o[...] = resid
    unit, _ = norm_parts(resid)
    second = (unit * vector_of(vec, idx, 2) + vector_of(vec, idx, 3)).astype(BF16)
    bias = bias_up_of(vec, idx)
    branch = jnp.zeros((CHUNK, WIDTH), F32)
    scale = (2.0 / jnp.pi) ** 0.5
    at = [slice(512 * j, 512 * j + 512) for j in range(4)]
    products = nn(second, w_up[:, at[0]])
    for j in range(4):
        z = products + bias[:, at[j]]
        if j < 3:
            products = nn(second, w_up[:, at[j + 1]])
        zz = z * z
        cdf = 0.5 + 0.5 * jnp.tanh(z * (scale + (scale * 0.044715) * zz))
        active = z * cdf
        slope_o[:, at[j]] = cdf + (active - active * cdf) * (2 * scale + (6 * scale * 0.044715) * zz)
        act = active.astype(BF16)
        act_s[rows, at[j]] = act
        branch += nn(act, w_down[at[j], :])
    out = (resid + (branch + vector_of(vec, idx, 4))).astype(BF16)
    out_o[...] = out
    out_s[rows, :] = out
    logits = nn(out, w_read[...])
    expd = jnp.exp(logits - jnp.max(logits, axis=-1, keepdims=True))
    soft = expd / jnp.sum(expd, axis=-1, keepdims=True)
    classes = lax.broadcasted_iota(jnp.int32, (CHUNK, VOCAB), 1)
    dl = (soft - jnp.where(classes == target[...], 1.0, 0.0)).astype(BF16)
    dl_s[rows, :] = dl
    dy = nt(dl, w_read[...])
    dy_o[...] = dy
    df = dy.astype(BF16)
    df_s[rows, :] = df
    bias_o[...] += jnp.sum(df.astype(F32), axis=0, keepdims=True)

    @pl.when(step == pl.num_programs(0) - 1)
    def _():
        whole = tn(out_s[...], dl_s[...]).astype(BF16)
        for shard in range(4):
            tile = whole[shard * 128 : shard * 128 + 128]
            put_parts(idx, keep, send, tile, shard, slice(4 * WIDTH, None))
            large = tn(act_s[:, shard * 512 : shard * 512 + 512], df_s[...]).astype(BF16)
            for xy in range(4):
                tile = large[xy * 128 : xy * 128 + 128]
                own_first = idx[0] == 0
                for i in range(4):
                    first = tile[16 * i : 16 * i + 16]
                    later = tile[64 + 16 * i : 64 + 16 * i + 16]
                    at = slice(i * WIDTH, (i + 1) * WIDTH)
                    keep[xy ^ idx[1], shard ^ idx[2], :, at] = jnp.where(own_first, first, later)
                    send[xy ^ idx[1], shard ^ idx[2], :, at] = jnp.where(own_first, later, first)


def feed_back_kernel(
    idx, vec, h, slope, dy, o0, o1, up_near, up_far, down_near, down_far,
    dh_o, do_o, gain_o, shift_o, bias_o, keep, send,
    w_mix, w_up, w_down, dz_s, a2_s, da_s,
):
    step = pl.program_id(0)

    @pl.when(step == 0)
    def _():
        for shard, member, piece in each_piece(idx, up_near, up_far):
            rows = rows_at(shard * 128 + member * PIECE, PIECE)
            w_mix[rows, :] = piece[:, :WIDTH]
            w_up[rows, :] = piece[:, WIDTH:]
        for shard, member, piece in each_piece(idx, down_near, down_far):
            for i in range(4):
                rows = rows_at(shard * 512 + member * 64 + 16 * i, PIECE)
                w_down[rows, :] = piece[:, i * WIDTH : (i + 1) * WIDTH]
        gain_o[...] = jnp.zeros_like(gain_o)
        shift_o[...] = jnp.zeros_like(shift_o)
        bias_o[...] = jnp.zeros_like(bias_o)

    rows = pl.ds(pl.multiple_of(step * CHUNK, CHUNK), CHUNK)
    gain = vector_of(vec, idx, 2)
    unit, inverse = norm_parts(h[...])
    a2_s[rows, :] = (unit * gain + vector_of(vec, idx, 3)).astype(BF16)
    d_out = dy[...]
    df = d_out.astype(BF16)
    d_second = jnp.zeros((CHUNK, WIDTH), F32)
    for j in range(4):
        at = slice(512 * j, 512 * j + 512)
        dz = (nt(df, w_down[at, :]) * slope[:, at]).astype(BF16)
        dz_s[rows, at] = dz
        bias_o[:, at] += jnp.sum(dz.astype(F32), axis=0, keepdims=True)
        d_second += nt(dz, w_up[:, at])
    gain_o[...] += jnp.sum(d_second * unit, axis=0, keepdims=True)
    shift_o[...] += jnp.sum(d_second, axis=0, keepdims=True)
    dh = d_out + norm_pull(d_second, unit, inverse, gain)
    dh_o[...] = dh
    da = dh.astype(BF16)
    da_s[rows, :] = da
    do_o[...] = nt(da, w_mix[...]).astype(BF16)

    @pl.when(step == pl.num_programs(0) - 1)
    def _():
        for half in range(2):
            large = tn((o0, o1)[half][...], da_s[...]).astype(BF16)
            for i in range(2):
                tile = large[128 * i : 128 * i + 128]
                put_parts(idx, keep, send, tile, 2 * half + i, slice(0, WIDTH))
        for j in range(4):
            large = tn(a2_s[...], dz_s[:, 512 * j : 512 * j + 512]).astype(BF16)
            at = slice(WIDTH + 512 * j, WIDTH + 512 * j + 512)
            for shard in range(4):
                put_parts(idx, keep, send, large[shard * 128 : shard * 128 + 128], shard, at)


def proj_gradient(idx, unit_t, columns, w, dx, keep, send):
    sums = nn(jnp.ones((PIECE, dx.shape[0]), BF16), dx[...])[:8]
    high = sums.astype(BF16)
    rest = (sums - high.astype(F32)).astype(BF16)
    shift_rows = nt(jnp.concatenate([high, rest], axis=0), w[...])
    gain, shift = columns[:, 0:1], columns[:, 1:2]
    on_gain = jnp.zeros((WIDTH, HALF), F32)
    for j in range(4):
        at = slice(j * HALF, (j + 1) * HALF)
        tile = nn(unit_t[...], dx[:, at])
        on_gain += tile * w[:, at].astype(F32)
        low = (tile * gain + shift * sums[:1, at]).astype(BF16)
        for shard in range(4):
            put_parts(idx, keep, send, low[shard * 128 : shard * 128 + 128], shard, at)
    gain_column = jnp.sum(on_gain, axis=1, keepdims=True)
    gain_row = side(gain_column, jnp.zeros((WIDTH, 7), F32)).T[:1]
    return jnp.concatenate([gain_row, shift_rows[:1] + shift_rows[8:9], jnp.zeros((6, WIDTH), F32)])


def attend_back_kernel(
    idx, unit_t, columns, w, proj, floats, ratios, do_i, kept,
    dx_o, keep, send, share_o,
    state, count_z, dx_s,
):
    attend_back_step(proj, floats, ratios, do_i, kept, dx_o, state, count_z, dx_s)

    @pl.when(pl.program_id(0) == pl.num_programs(0) - 1)
    def _():
        share_o[...] = proj_gradient(idx, unit_t, columns, w, dx_s, keep, send)


def attend_back_last_kernel(
    idx, unit_t, columns, w, proj, floats, ratios, do_i, kept,
    share, g_g2, g_b2, g_bd, g_bu,
    dx_o, keep, send,
    state, count_z, dx_s,
):
    attend_back_step(proj, floats, ratios, do_i, kept, dx_o, state, count_z, dx_s)

    @pl.when(pl.program_id(0) == pl.num_programs(0) - 1)
    def _():
        total = proj_gradient(idx, unit_t, columns, w, dx_s, keep, send) + share[...]
        for s in range(4):
            at = slice(128 * s, 128 * s + 128)
            lines = [total[:2, at], g_g2[:, at], g_b2[:, at], g_bd[:, at]]
            lines += [g_bu[:, 512 * s + 128 * j : 512 * s + 128 * j + 128] for j in range(4)]
            lines.append(jnp.zeros((7, 128), F32))
            block = jnp.concatenate(lines, axis=0).astype(BF16)
            for xy in range(4):
                keep[xy, s ^ idx[2], :, COLS_PROJ:] = block
                send[xy, s ^ idx[2], :, COLS_PROJ:] = block


def attend_back_step(proj, floats, ratios, do_i, kept, dx_o, state, count_z, dx_s):
    step = pl.program_id(0)
    chunk = pl.num_programs(0) - 1 - step

    @pl.when(step == 0)
    def _():
        state[...] = jnp.zeros_like(state)
        count_z[...] = jnp.zeros_like(count_z)

    def take(ref, j, rows, pair):
        return ref[rows, j * HALF + 128 * pair : j * HALF + 128 * pair + 128]

    tri, trt, block, ones = causal_pair(), causal_pair(True), same_head(), head_ones()
    places = sub_places((1, 0))
    d_mixes, wide, d_numers, d_totals, others = {}, {}, {}, {}, {}
    for sub, pair, rows, at in places:
        v = take(proj, 2, rows, pair)
        d_mixes[sub, pair] = masked(tri, nt(do_i[rows, at], stacked(v)))
        wide[sub, pair] = stacked(take(proj, 3, rows, pair))
    for sub, pair, rows, at in places:
        do, ratio = do_i[rows, at], ratios[rows, at]
        q, k, v, e = [take(proj, j, rows, pair) for j in range(4)]
        inv, logits, probs = [take(floats, j, rows, pair) for j in (1, 2, 3)]
        d_ratio = nn(d_mixes[sub, pair], wide[sub, pair])
        d_ratio = (d_ratio + nt(do, kept[sub, pair][:, 128:])) * inv
        weighed = d_ratio * probs
        d_logits = weighed - probs * head_sum(weighed, ones)
        d_numers[sub, pair] = ((HEAD ** -0.5) * d_logits * inv).astype(BF16)
        d_totals[sub, pair] = (-(weighed + d_logits * logits) * inv).astype(BF16)
        wide_q, wide_r, wide_do = stacked(q), stacked(ratio), stacked(do)
        scores = masked(trt, nt(k, wide_q))
        mixing = masked(trt, nt(e, wide_r))
        d_mix_t = masked(trt, nt(v, wide_do))
        others[sub, pair] = (scores, d_mix_t, nn(mixing, wide_do), wide_q, wide_r)
    d_total = jnp.concatenate([side(d_totals[sub, 0], d_totals[sub, 1]) for sub in range(2)], axis=0)
    total_z = nn(causal_whole(True), d_total) + count_z[...]
    count_z[...] = total_z[:1, :]
    currents = [state[0], state[1]]
    lows = {}
    for sub, pair, rows, at in places:
        lows[sub, pair] = currents[pair].astype(BF16)
        more = side(
            tn(ratios[rows, at], do_i[rows, at]), tn(d_numers[sub, pair], take(proj, 0, rows, pair))
        )
        currents[pair] = currents[pair] + jnp.where(block, more, 0.0)
    state[0], state[1] = currents
    for sub, pair, rows, at in places:
        k, v, e = [take(proj, j, rows, pair) for j in (1, 2, 3)]
        scores, d_mix_t, dv, wide_q, wide_r = others[sub, pair]
        d_numer, low = d_numers[sub, pair], lows[sub, pair]
        wide_n = stacked(d_numer)
        d_scores = masked(tri, nt(d_numer, wide[sub, pair]))
        d_scores_t = masked(trt, nt(e, wide_n))
        both = nn(e, low)
        de = nn(side(d_mix_t, scores), jnp.concatenate([wide_r, wide_n], axis=0))
        de = de + nt(side(v, k), low) + total_z[rows, at]
        dq = nn(d_scores, stacked(k)) + nn(d_numer, kept[sub, pair][:, :128])
        dk = nn(d_scores_t, wide_q) + both[:, 128:]
        dv = dv + both[:, :128]
        dc = de * take(floats, 0, rows, pair)
        for j, value in enumerate((dq, dk, dv, dc)):
            dx_o[rows, j * HALF + 128 * pair : j * HALF + 128 * pair + 128] = value.astype(BF16)
    dx_s[pl.ds(pl.multiple_of(chunk * CHUNK, CHUNK), CHUNK), :] = dx_o[...]


def inputs_kernel(idx, vec, x, dh, dx0, dx1, w0, w1, dx_o):
    unit, inverse = norm_parts(x[...].astype(F32))
    d_first = nt(dx0[...], w0[...]) + nt(dx1[...], w1[...])
    dx_o[...] = dh[...] + norm_pull(d_first, unit, inverse, vector_of(vec, idx, 0))


def unpack_proj_kernel(idx, near, far, query, key, value, control, g1, b1, g2, b2, bd, bu):
    for shard, member, piece in each_member(idx, near, far):
        rows = rows_at(member * PIECE, PIECE)
        for j, out in enumerate((query, key, value, control)):
            for half in range(2):
                start = half * COLS_PROJ + j * HALF
                out[rows, half * HALF : (half + 1) * HALF] = piece[:, start : start + HALF].astype(F32)

        @pl.when(member == 0)
        def _():
            lines = piece[:, COLS_BOTH:].astype(F32)
            for i, out in enumerate((g1, b1, g2, b2, bd)):
                out[...] = lines[i]
            for i in range(4):
                bu[128 * i : 128 * i + 128] = lines[5 + i]


def unpack_feed_kernel(idx, near, far, mix, up, down, read):
    for shard, member, piece in each_member(idx, near, far):
        rows = rows_at(member * PIECE, PIECE)
        mix[rows, :] = piece[:, :WIDTH].astype(F32)
        up[rows, :] = piece[:, WIDTH:COLS_UP].astype(F32)
        for i in range(4):
            start = COLS_UP + i * WIDTH
            down[rows_at(member * 64 + 16 * i, PIECE), :] = piece[:, start : start + WIDTH].astype(F32)
        read[rows, :] = piece[:, COLS_UP + 4 * WIDTH :].astype(F32)


def shaped(shape, dtype):
    return jax.ShapeDtypeStruct(shape, dtype)


def call(kernel, name, args, outs, steps=None, scratch=(), flops=0, limit=56):
    grid = (steps,) if steps else ()

    def spec(shape, block):
        if block is None:
            return pl.BlockSpec(tuple(shape), lambda *_: (0,) * len(shape))
        return pl.BlockSpec(*block)

    in_specs = []
    for array, block in args:
        if array.dtype == jnp.int32 and array.shape == (3,):
            in_specs.append(pl.BlockSpec(memory_space=pltpu.SMEM))
        elif block == "hbm":
            in_specs.append(pl.BlockSpec(memory_space=pl.ANY))
        else:
            in_specs.append(spec(array.shape, block))
    moved = sum(a.size * a.dtype.itemsize for a, _ in args)
    return pl.pallas_call(
        kernel,
        grid=grid,
        in_specs=in_specs,
        out_specs=[spec(shape, block) for shape, _, block in outs],
        out_shape=[shaped(shape, dtype) for shape, dtype, _ in outs],
        scratch_shapes=list(scratch),
        compiler_params=pltpu.CompilerParams(
            vmem_limit_bytes=limit * MIB,
            dimension_semantics=("arbitrary",) * len(grid) if grid else None,
        ),
        cost_estimate=pl.CostEstimate(flops=int(flops), bytes_accessed=int(moved), transcendentals=0),
        name=name,
    )(*[array for array, _ in args])


def swap(value, axis, size, distance):
    return lax.ppermute(value, axis, [(i, i ^ distance) for i in range(size)])


def pin(*values):
    return lax.optimization_barrier(values)


def near_rows(piece, shards):
    return [swap(piece, "shard", shards, k) for k in range(1, 4)]


def near_pair(piece, shards):
    return jnp.stack([piece, swap(piece, "shard", shards, 1)])


def far_pair(pair, shards):
    return swap(pair, "shard", shards, 2)


def sum_of(values):
    values = [v.astype(F32) for v in values]
    return ((values[0] + values[1]) + (values[2] + values[3])).astype(BF16)


def core_sum(keep, got):
    return [(keep[k].astype(F32) + got[k].astype(F32)).astype(BF16) for k in range(4)]


def plane_start(parts, dp):
    return [swap(parts[k], "dp", dp, 2 * k) for k in range(1, 4)]


def plane_sum(parts, got):
    return [sum_of([parts[0][k], got[0][k], got[1][k], got[2][k]]) for k in range(4)]


def plane_halves(parts, got):
    total = [p.astype(F32) for p in [parts[0]] + got]
    total = ((total[0] + total[1]) + (total[2] + total[3])).astype(BF16)
    return total[:2], total[2:]


def half_start(high, shards):
    return swap(high, "shard", shards, 2)


def half_sum(low, got):
    return [(low[k].astype(F32) + got[k].astype(F32)).astype(BF16) for k in range(2)]


def last_start(pair, shards):
    return swap(pair[1], "shard", shards, 1)


def last_sum(pair, got, dp):
    return across_planes((pair[0].astype(F32) + got.astype(F32)).astype(BF16), dp)


def across_planes(total, dp):
    distance = 8
    while distance < dp:
        total = (total.astype(F32) + swap(total, "dp", dp, distance).astype(F32)).astype(BF16)
        distance *= 2
    return total


def shard_start(rows, shards):
    return [swap(rows[k], "shard", shards, k) for k in range(1, 4)]


def shard_sum(rows, got, dp):
    return across_planes(sum_of([rows[0]] + got), dp)


def body(dp, shards):
    def on_device(
        tokens, targets, gain_one, bias_one, w_query, w_key, w_value, w_control, w_mix,
        gain_two, bias_two, w_up, bias_up, w_down, bias_down, w_read,
    ):
        count = tokens.shape[0]
        steps = count // CHUNK
        rows = WIDTH // shards
        member = lax.axis_index("dp") % 8
        idx = jnp.stack([member % 2, member // 2, lax.axis_index("shard")]).astype(jnp.int32)
        forward = lambda i: (i, 0)
        back = lambda i: (steps - 1 - i, 0)
        tok = lambda n: ((CHUNK, n), forward)
        parts = (4, 4, PIECE)

        weights = (w_query, w_key, w_value, w_control, w_mix, w_up, w_down, w_read)
        sizes = [(PIECE, COLS_BOTH + 128), (PIECE, COLS_UP), (2, PIECE, COLS_DOWN)]
        vectors = (gain_one, bias_one, gain_two, bias_two, bias_down, bias_up)
        pa, pu, pd = call(
            pack_kernel,
            "pack_weights",
            [(idx, None)] + [(v, None) for v in vectors] + [(w, "hbm") for w in weights],
            [(size, BF16, None) for size in sizes],
            scratch=[pltpu.SemaphoreType.DMA((20,))],
        )
        got_a = near_rows(pa, shards)
        pair_u = near_pair(pu, shards)
        rows_a = jnp.stack([pa[:, :COLS_BOTH]] + [g[:, :COLS_BOTH] for g in got_a])
        vec = jnp.stack([pa[:, COLS_BOTH:]] + [g[:, COLS_BOTH:] for g in got_a])
        rows_a, vec, pair_u, pd, tokens_a = pin(rows_a, vec, pair_u, pd, tokens)
        plane_a = [swap(rows_a, "dp", dp, 2 * k) for k in range(1, 4)]
        got_u = far_pair(pair_u, shards)
        pair_d = near_pair(pd, shards)
        a1, unit_t, columns = call(
            first_norm_kernel,
            "first_norm",
            [(idx, None), (vec, None), (tokens_a, None)],
            [
                ((count, WIDTH), BF16, None),
                ((WIDTH, count), BF16, None),
                ((WIDTH, 8), F32, None),
            ],
        )
        target = targets.reshape(count, 1)
        plane_a, got_u, pair_d, a1, unit_t, columns, target = pin(
            plane_a, got_u, pair_d, a1, unit_t, columns, target
        )
        near_a = jnp.stack([rows_a] + plane_a)
        far_a = swap(near_a, "dp", dp, 1)
        got_d = far_pair(pair_d, shards)
        got_u, _ = pin(got_u, near_a)
        rows_u = jnp.concatenate([pair_u, got_u])
        plane_u = plane_start([rows_u] * 4, dp)

        kept = ((2, 2, 128, 256), lambda i: (i, 0, 0, 0))

        def attend(a1, half):
            at = ((4, 4, PIECE, COLS_PROJ), lambda i: (0, 0, 0, half))
            return call(
                attend_kernel,
                "attend",
                [(idx, None), (a1, tok(WIDTH)), (near_a, at), (far_a, at)],
                [
                    ((count, COLS_PROJ), BF16, tok(COLS_PROJ)),
                    ((count, COLS_PROJ), F32, tok(COLS_PROJ)),
                    ((count, 2 * HALF), BF16, tok(2 * HALF)),
                    ((2 * steps, 2, 128, 256), BF16, kept),
                    ((WIDTH, COLS_PROJ), BF16, None),
                ],
                steps,
                [
                    pltpu.VMEM((2, 128, 256), F32),
                    pltpu.VMEM((1, HALF), F32),
                ],
                flops=6e9,
            )

        first = attend(a1, 0)
        first, plane_u, got_d, a1 = pin(first, plane_u, got_d, a1)
        rows_d = jnp.concatenate([pair_d, got_d])
        plane_d = [swap(rows_d[:, 0], "dp", dp, 2 * k) for k in range(1, 3)]
        near_u = jnp.stack([rows_u] + plane_u)
        far_u = swap(near_u, "dp", dp, 1)
        second = attend(a1, 1)
        second, far_u, plane_d = pin(second, far_u, plane_d)
        near_d = jnp.stack([rows_d[:, 0]] + plane_d + [rows_d[:, 1]])
        far_d = swap(near_d, "dp", dp, 1)
        halves = (first, second)
        o0, o1 = first[2], second[2]
        mixed_at = ((CHUNK, HALF), lambda i: (i, 1))
        mixed_all = ((count, HALF), lambda i: (0, 1))

        out, h, slope, dy, g_bias_down, keep_d, send_d = call(
            feed_kernel,
            "feed_forward",
            [
                (idx, None), (vec, None), (tokens, tok(WIDTH)), (o0, mixed_at), (o1, mixed_at),
                (target, tok(1)), (near_u, None), (far_u, None), (near_d, None), (far_d, None),
            ],
            [
                ((count, WIDTH), BF16, tok(WIDTH)),
                ((count, WIDTH), F32, tok(WIDTH)),
                ((count, FF), F32, tok(FF)),
                ((count, WIDTH), F32, tok(WIDTH)),
                ((1, WIDTH), F32, None),
                (parts + (COLS_DOWN,), BF16, None),
                (parts + (COLS_DOWN,), BF16, None),
            ],
            steps,
            [
                pltpu.VMEM((WIDTH, WIDTH), BF16),
                pltpu.VMEM((WIDTH, FF), BF16),
                pltpu.VMEM((FF, WIDTH), BF16),
                pltpu.VMEM((WIDTH, VOCAB), BF16),
                pltpu.VMEM((count, FF), BF16),
                pltpu.VMEM((count, WIDTH), BF16),
                pltpu.VMEM((count, VOCAB), BF16),
                pltpu.VMEM((count, WIDTH), BF16),
            ],
            flops=8e9,
        )
        got_d = swap(send_d, "dp", dp, 1)

        dh, d_mixed, g_gain_two, g_bias_two, g_bias_up, keep_u, send_u = call(
            feed_back_kernel,
            "feed_backward",
            [
                (idx, None), (vec, None), (h, tok(WIDTH)), (slope, tok(FF)), (dy, tok(WIDTH)),
                (o0, mixed_all), (o1, mixed_all),
                (near_u, None), (far_u, None), (near_d, None), (far_d, None),
            ],
            [
                ((count, WIDTH), F32, tok(WIDTH)),
                ((count, WIDTH), BF16, tok(WIDTH)),
                ((1, WIDTH), F32, None),
                ((1, WIDTH), F32, None),
                ((1, FF), F32, None),
                (parts + (COLS_UP,), BF16, None),
                (parts + (COLS_UP,), BF16, None),
            ],
            steps,
            [
                pltpu.VMEM((WIDTH, WIDTH), BF16),
                pltpu.VMEM((WIDTH, FF), BF16),
                pltpu.VMEM((FF, WIDTH), BF16),
                pltpu.VMEM((count, FF), BF16),
                pltpu.VMEM((count, WIDTH), BF16),
                pltpu.VMEM((count, WIDTH), BF16),
            ],
            flops=8e9,
        )
        got_d, d_mixed, send_u = pin(got_d, d_mixed, send_u)
        got_u = swap(send_u, "dp", dp, 1)
        sum_d = core_sum(keep_d, got_d)
        sum_d, d_mixed = pin(sum_d, d_mixed)
        got_d = plane_start(sum_d, dp)

        kept_back = ((2, 2, 128, 256), lambda i: (steps - 1 - i, 0, 0, 0))

        def attend_back(half, d_mixed, extra=()):
            proj, floats, mixed, states, w = halves[half]
            wide = ((CHUNK, COLS_PROJ), back)
            column = ((CHUNK, HALF), lambda i: (steps - 1 - i, half))
            last = half == 1
            cols = COLS_LAST if last else COLS_PROJ
            return call(
                attend_back_last_kernel if last else attend_back_kernel,
                "attend_backward",
                [(idx, None), (unit_t, None), (columns, None), (w, None)]
                + [(proj, wide), (floats, wide), (mixed, ((CHUNK, HALF), back))]
                + [(d_mixed, column), (states, kept_back)]
                + [(t, None) for t in extra],
                [
                    ((count, COLS_PROJ), BF16, ((CHUNK, COLS_PROJ), back)),
                    (parts + (cols,), BF16, None),
                    (parts + (cols,), BF16, None),
                ]
                + ([] if last else [((8, WIDTH), F32, None)]),
                steps,
                [
                    pltpu.VMEM((2, 128, 256), F32),
                    pltpu.VMEM((1, HALF), F32),
                    pltpu.VMEM((count, COLS_PROJ), BF16),
                ],
                flops=10e9,
            )

        dx0, keep_a, send_a, share = attend_back(0, d_mixed)
        got_d, got_u, send_a, d_mixed = pin(got_d, got_u, send_a, d_mixed)
        got_a = swap(send_a, "dp", dp, 1)
        sum_u = core_sum(keep_u, got_u)
        low_d, high_d = plane_halves(sum_d, got_d)
        sum_u, low_d, high_d, d_mixed = pin(sum_u, low_d, high_d, d_mixed)
        got_u = plane_start(sum_u, dp)
        got_d = half_start(high_d, shards)

        extra = (share, g_gain_two, g_bias_two, g_bias_down, g_bias_up)
        dx1, keep_b, send_b = attend_back(1, d_mixed, extra)
        got_d, got_u, got_a, send_b, dx1 = pin(got_d, got_u, got_a, send_b, dx1)
        got_b = swap(send_b, "dp", dp, 1)
        sum_p = [
            jnp.concatenate(both, axis=-1)
            for both in zip(core_sum(keep_a, got_a), core_sum(keep_b, got_b))
        ]
        sum_p, dx1 = pin(sum_p, dx1)
        got_p = plane_start(sum_p, dp)
        got_u, got_d, _ = pin(got_u, got_d, sum_p)
        low_u, high_u = plane_halves(sum_u, got_u)
        got_u = half_start(high_u, shards)
        pair_d = half_sum(low_d, got_d)
        got_d = last_start(pair_d, shards)
        d_tokens = call(
            inputs_kernel,
            "input_gradient",
            [
                (idx, None), (vec, None), (tokens, tok(WIDTH)), (dh, tok(WIDTH)),
                (dx0, tok(COLS_PROJ)), (dx1, tok(COLS_PROJ)),
                (first[4], None), (second[4], None),
            ],
            [((count, WIDTH), F32, tok(WIDTH))],
            steps,
            flops=3e9,
        )[0]
        got_u, got_p, got_d, d_tokens = pin(got_u, got_p, got_d, d_tokens)
        pair_u = half_sum(low_u, got_u)
        got_u = last_start(pair_u, shards)
        total_d = last_sum(pair_d, got_d, dp)
        rows_p = plane_sum(sum_p, got_p)
        got_p = shard_start(rows_p, shards)
        got_u, _ = pin(got_u, rows_p)
        total_f = jnp.concatenate([last_sum(pair_u, got_u, dp), total_d], axis=-1)
        along_f = swap(total_f, "dp", dp, 4)
        got_p, _ = pin(got_p, total_f)
        pair_f = jnp.stack([total_f, along_f])
        up_f = swap(pair_f, "dp", dp, 2)
        total_p = shard_sum(rows_p, got_p, dp)
        along_p = swap(total_p, "dp", dp, 4)
        pair_p = jnp.stack([total_p, along_p])
        up_p = swap(pair_p, "dp", dp, 2)
        up_f, _ = pin(up_f, pair_p)
        near_f = jnp.stack([pair_f, up_f], axis=1).reshape((4,) + total_f.shape)
        far_f = swap(near_f, "dp", dp, 1)
        up_p, _ = pin(up_p, near_f)
        near_p = jnp.stack([pair_p, up_p], axis=1).reshape((4,) + total_p.shape)
        far_p = swap(near_p, "dp", dp, 1)
        g_mix, g_up, g_down, g_read = call(
            unpack_feed_kernel,
            "unpack_feed",
            [(idx, None), (near_f, None), (far_f, None)],
            [
                ((rows, WIDTH), F32, None),
                ((rows, FF), F32, None),
                ((4 * rows, WIDTH), F32, None),
                ((rows, VOCAB), F32, None),
            ],
        )
        far_p, g_up = pin(far_p, g_up)
        g_query, g_key, g_value, g_control, g1, b1, g2, b2, bd, bu = call(
            unpack_proj_kernel,
            "unpack_proj",
            [(idx, None), (near_p, None), (far_p, None)],
            [((rows, WIDTH), F32, None)] * 4 + [((128,), F32, None)] * 5 + [((512,), F32, None)],
        )
        return (
            out, d_tokens, g1, b1, g_query, g_key, g_value, g_control, g_mix,
            g2, b2, g_up, bu, g_down, bd, g_read,
        )

    return on_device


def solution(mesh):
    dp, shards = mesh.shape["dp"], mesh.shape["shard"]
    vector, matrix = P("shard"), P("shard", None)
    rows = P(("dp", "shard"), None)
    params = (
        vector, vector, matrix, matrix, matrix, matrix, matrix,
        vector, vector, matrix, vector, matrix, vector, matrix,
    )
    return jax.shard_map(
        body(dp, shards),
        mesh=mesh,
        in_specs=(rows, P(("dp", "shard"))) + params,
        out_specs=(rows, rows) + params,
        check_vma=False,
    )
```

```python
import jax
import jax.numpy as jnp
from jax import lax
from jax.experimental import pallas as pl
from jax.experimental.pallas import tpu as pltpu
from jax.sharding import PartitionSpec as P

EPS = 1e-05
WIDTH = 512
HEAD = 64
FF = 2048
VOCAB = 256
SEQ_LEN = 1024
CHUNK = 256
SUB = 128
ROWS = 512
HALF = 256
PIECE = 16
COLS_PROJ = 4 * HALF
COLS_BOTH = 2 * COLS_PROJ
COLS_LAST = COLS_PROJ + 128
COLS_UP = WIDTH + FF
COLS_DOWN = 4 * WIDTH + VOCAB
F32 = jnp.float32
BF16 = jnp.bfloat16
MIB = 1024 * 1024


def nn(a, b):
    return lax.dot_general(a, b, (((1,), (0,)), ((), ())), preferred_element_type=F32)


def nt(a, b):
    return lax.dot_general(a, b, (((1,), (1,)), ((), ())), preferred_element_type=F32)


def tn(a, b):
    return lax.dot_general(a, b, (((0,), (0,)), ((), ())), preferred_element_type=F32)


def norm_parts(values):
    centre = values - jnp.mean(values, axis=-1, keepdims=True)
    inverse = lax.rsqrt(jnp.mean(centre * centre, axis=-1, keepdims=True) + EPS)
    return centre * inverse, inverse


def norm_pull(grad, unit, inverse, gain):
    scaled = grad * gain
    return inverse * (
        scaled
        - jnp.mean(scaled, axis=-1, keepdims=True)
        - unit * jnp.mean(scaled * unit, axis=-1, keepdims=True)
    )


def vector_of(vec_ref, idx, row):
    return jnp.concatenate(
        [vec_ref[s ^ idx[2], row : row + 1, :].astype(F32) for s in range(4)], axis=1
    )


def bias_up_of(vec_ref, idx):
    return jnp.concatenate(
        [
            vec_ref[s ^ idx[2], row : row + 1, :].astype(F32)
            for s in range(4)
            for row in range(5, 9)
        ],
        axis=1,
    )


def each_piece(idx, near, far):
    for c, buf in ((0, near), (1, far)):
        for xy in range(4):
            member = ((xy ^ idx[1]) * 2) + (c ^ idx[0])
            for s in range(4):
                yield s ^ idx[2], member, buf.at[xy, s]


def each_member(idx, near, far):
    for c, buf in ((0, near), (1, far)):
        for xy in range(4):
            yield None, ((xy ^ idx[1]) * 2) + (c ^ idx[0]), buf.at[xy]


def rows_at(start, size):
    return pl.ds(pl.multiple_of(start, PIECE), size)


def put_parts(idx, keep, send, tile, shard, columns):
    for xy in range(4):
        first = tile[32 * xy : 32 * xy + 16]
        second = tile[32 * xy + 16 : 32 * xy + 32]
        own_first = idx[0] == 0
        keep[xy ^ idx[1], shard ^ idx[2], :, columns] = jnp.where(own_first, first, second)
        send[xy ^ idx[1], shard ^ idx[2], :, columns] = jnp.where(own_first, second, first)


def pack_kernel(
    idx, g1, b1, g2, b2, bd, bu, wq, wk, wv, wc, wm, wu, wd, wr, pa, pc, pd, sems
):
    member = idx[1] * 2 + idx[0]
    across = (idx[1] ^ 3) * 2 + idx[0]
    rows = rows_at(member * PIECE, PIECE)
    moves = []
    for j, w in enumerate((wq, wk, wv, wc)):
        for half in range(2):
            start = half * COLS_PROJ + j * HALF
            part = w.at[rows, half * HALF : (half + 1) * HALF]
            moves.append((part, pa.at[:, start : start + HALF]))
    moves.append((wm.at[rows, :], pc.at[:, :WIDTH]))
    moves.append((wu.at[rows, :], pc.at[:, WIDTH:]))
    for place, who in enumerate((member, across)):
        for i in range(4):
            part = wd.at[rows_at(who * 64 + 16 * i, PIECE), :]
            moves.append((part, pd.at[place, :, i * WIDTH : (i + 1) * WIDTH]))
        moves.append((wr.at[rows_at(who * PIECE, PIECE), :], pd.at[place, :, 4 * WIDTH :]))
    copies = [pltpu.make_async_copy(src, dst, sems.at[i]) for i, (src, dst) in enumerate(moves)]
    for copy in copies:
        copy.start()
    lines = [v[...].astype(F32).reshape(1, 128) for v in (g1, b1, g2, b2, bd)]
    lines += [bu[128 * j : 128 * j + 128].astype(F32).reshape(1, 128) for j in range(4)]
    lines.append(jnp.zeros((7, 128), F32))
    pa[:, COLS_BOTH:] = jnp.concatenate(lines, axis=0).astype(BF16)
    for copy in copies:
        copy.wait()


def first_norm_kernel(idx, vec, x, a1, both_t):
    unit, _ = norm_parts(x[...].astype(F32))
    low = (unit * vector_of(vec, idx, 0) + vector_of(vec, idx, 1)).astype(BF16)
    a1[...] = low
    both_t[:WIDTH, :] = low.T
    both_t[WIDTH : 2 * WIDTH, :] = unit.astype(BF16).T
    both_t[2 * WIDTH :, :] = jnp.ones((PIECE, both_t.shape[1]), BF16)


def lanes_low():
    return lax.broadcasted_iota(jnp.int32, (1, 128), 1) < HEAD


def stacked(value):
    low = lanes_low().astype(F32).astype(BF16)
    high = (1.0 - lanes_low().astype(F32)).astype(BF16)
    return jnp.concatenate([value * low, value * high], axis=0)


def head_ones():
    row = (lax.broadcasted_iota(jnp.int32, (256, 128), 0) & 127) < HEAD
    col = lax.broadcasted_iota(jnp.int32, (256, 128), 1) < HEAD
    return (row == col).astype(F32).astype(BF16)


def head_sum(value, ones):
    high = value.astype(BF16)
    rest = (value - high.astype(F32)).astype(BF16)
    return nn(side(high, rest), ones)


def sub_places(subs):
    return [
        (sub, pair, slice(SUB * sub, SUB * sub + SUB), slice(128 * pair, 128 * pair + 128))
        for sub in subs
        for pair in range(2)
    ]


def head_max(value):
    low = lanes_low()
    first = jnp.max(jnp.where(low, value, -jnp.inf), axis=-1, keepdims=True)
    second = jnp.max(jnp.where(low, -jnp.inf, value), axis=-1, keepdims=True)
    return jnp.where(low, first, second)


def same_head():
    row = lax.broadcasted_iota(jnp.int32, (128, 256), 0) < HEAD
    col = (lax.broadcasted_iota(jnp.int32, (128, 256), 1) & 127) < HEAD
    return row == col


def causal_pair(transposed=False):
    row = lax.broadcasted_iota(jnp.int32, (SUB, 2 * SUB), 0)
    col = lax.broadcasted_iota(jnp.int32, (SUB, 2 * SUB), 1) & (SUB - 1)
    return (row <= col) if transposed else (col <= row)


def causal_whole(transposed=False):
    row = lax.broadcasted_iota(jnp.int32, (CHUNK, CHUNK), 0)
    col = lax.broadcasted_iota(jnp.int32, (CHUNK, CHUNK), 1)
    keep = (row <= col) if transposed else (col <= row)
    return keep.astype(F32).astype(BF16)


def side(*values):
    return jnp.concatenate(values, axis=1)


def masked(keep, value):
    return jnp.where(keep, value, 0.0).astype(BF16)


def attend_kernel(idx, a1, near, far, proj_o, float_o, mixed_o, kept, w_o, state, count_z):
    step = pl.program_id(0)

    @pl.when(step == 0)
    def _():
        for shard, member, piece in each_piece(idx, near, far):
            w_o[rows_at(shard * 128 + member * PIECE, PIECE), :] = piece[...]
        state[...] = jnp.zeros_like(state)
        count_z[...] = jnp.zeros_like(count_z)

    a = a1[...]
    q_all = nn(a, w_o[:, :HALF]).astype(BF16)
    k_all = nn(a, w_o[:, HALF : 2 * HALF]).astype(BF16)
    expo = jnp.exp(nn(a, w_o[:, 3 * HALF :]))
    e_all = expo.astype(BF16)
    v_all = nn(a, w_o[:, 2 * HALF : 3 * HALF]).astype(BF16)
    for j, value in enumerate((q_all, k_all, v_all, e_all)):
        proj_o[:, j * HALF : (j + 1) * HALF] = value
    float_o[:, :HALF] = expo
    total = nn(causal_whole(), e_all) + count_z[...]
    count_z[...] = total[CHUNK - 1 :, :]
    inverse = 1.0 / total
    float_o[:, HALF : 2 * HALF] = inverse
    tri, block, ones = causal_pair(), same_head(), head_ones()
    places = sub_places((0, 1))
    lows, wide_e, numers, ratios = {}, {}, {}, {}
    for pair in range(2):
        current = state[pair]
        for sub in range(2):
            rows, at = slice(SUB * sub, SUB * sub + SUB), slice(128 * pair, 128 * pair + 128)
            lows[sub, pair] = current.astype(BF16)
            kept[sub, pair] = lows[sub, pair]
            wide_e[sub, pair] = stacked(e_all[rows, at])
            more = tn(e_all[rows, at], side(k_all[rows, at], v_all[rows, at]))
            current = current + jnp.where(block, more, 0.0)
        state[pair] = current
    for sub, pair, rows, at in places:
        scores = masked(tri, nt(q_all[rows, at], stacked(k_all[rows, at])))
        numer = nn(scores, wide_e[sub, pair])
        numers[sub, pair] = numer + nt(q_all[rows, at], lows[sub, pair][:, :128])

    def soften(sub, pair, rows, at):
        inv = inverse[rows, at]
        logits = (HEAD ** -0.5) * numers[sub, pair] * inv
        expd = jnp.exp(logits - head_max(logits))
        probs = expd * (1.0 / head_sum(expd, ones))
        ratios[sub, pair] = (probs * inv).astype(BF16)
        float_o[rows, 2 * HALF + 128 * pair : 2 * HALF + 128 * pair + 128] = logits
        float_o[rows, 3 * HALF + 128 * pair : 3 * HALF + 128 * pair + 128] = probs
        mixed_o[rows, at] = ratios[sub, pair]

    def mix(sub, pair, rows, at):
        mixing = masked(tri, nt(ratios[sub, pair], wide_e[sub, pair]))
        out = nn(mixing, stacked(v_all[rows, at])) + nn(ratios[sub, pair], lows[sub, pair][:, 128:])
        mixed_o[rows, HALF + 128 * pair : HALF + 128 * pair + 128] = out.astype(BF16)

    for i, place in enumerate(places):
        soften(*place)
        if i:
            mix(*places[i - 1])
    mix(*places[-1])


def feed_kernel(
    idx, vec, x, o0, o1, target, up_near_i, up_far_i, down_near_i, down_far_i,
    out_o, h_o, slope_o, dy_o, bias_o, keep, send, mix_o, up_o, down_o,
    up_near, up_far, down_near, down_far,
    w_mix, w_up, w_down, w_read, act_s, out_s, h_s, slope_s, dy_s, dl_s, df_s, sems, row_sems,
):
    step = pl.program_id(0)
    moves = (
        (up_near_i, up_near), (up_far_i, up_far), (down_near_i, down_near), (down_far_i, down_far),
        (w_mix, mix_o), (w_up, up_o), (w_down, down_o),
    )
    copies = [pltpu.make_async_copy(src, dst, sems.at[i]) for i, (src, dst) in enumerate(moves)]

    @pl.when(step == 0)
    def _():
        for copy in copies[:4]:
            copy.start()
        for copy in copies[:2]:
            copy.wait()
        for shard, member, piece in each_piece(idx, up_near, up_far):
            rows = rows_at(shard * 128 + member * PIECE, PIECE)
            w_mix[rows, :] = piece[:, :WIDTH]
            w_up[rows, :] = piece[:, WIDTH:]
        for copy in copies[2:4]:
            copy.wait()
        for shard, member, piece in each_piece(idx, down_near, down_far):
            for i in range(4):
                rows = rows_at(shard * 512 + member * 64 + 16 * i, PIECE)
                w_down[rows, :] = piece[:, i * WIDTH : (i + 1) * WIDTH]
            w_read[rows_at(shard * 128 + member * PIECE, PIECE), :] = piece[:, 4 * WIDTH :]
        for copy in copies[4:]:
            copy.start()
        bias_o[...] = jnp.zeros_like(bias_o)

    def row_copies(place):
        at = pl.ds(pl.multiple_of(place * ROWS, ROWS), ROWS)
        pairs = ((out_s, out_o), (h_s, h_o), (slope_s, slope_o), (dy_s, dy_o))
        return [
            pltpu.make_async_copy(src.at[at], dst.at[at], row_sems.at[place, i])
            for i, (src, dst) in enumerate(pairs)
        ]

    rows = pl.ds(pl.multiple_of(step * ROWS, ROWS), ROWS)
    attn = nn(o0[...], w_mix[:HALF, :]) + nn(o1[...], w_mix[HALF:, :])
    resid = x[...].astype(F32) + attn
    h_s[rows, :] = resid
    unit, _ = norm_parts(resid)
    second = (unit * vector_of(vec, idx, 2) + vector_of(vec, idx, 3)).astype(BF16)
    bias = bias_up_of(vec, idx)
    branch = jnp.zeros((ROWS, WIDTH), F32)
    scale = (2.0 / jnp.pi) ** 0.5
    at = [slice(512 * j, 512 * j + 512) for j in range(4)]
    products = nn(second, w_up[:, at[0]])
    for j in range(4):
        z = products + bias[:, at[j]]
        if j < 3:
            products = nn(second, w_up[:, at[j + 1]])
        zz = z * z
        cdf = 0.5 + 0.5 * jnp.tanh(z * (scale + (scale * 0.044715) * zz))
        active = z * cdf
        slope = cdf + (active - active * cdf) * (2 * scale + (6 * scale * 0.044715) * zz)
        slope_s[rows, at[j]] = slope.astype(BF16)
        act = active.astype(BF16)
        act_s[rows, at[j]] = act
        branch += nn(act, w_down[at[j], :])
    out = (resid + (branch + vector_of(vec, idx, 4))).astype(BF16)
    out_s[rows, :] = out
    logits = nn(out, w_read[...])
    expd = jnp.exp(logits - jnp.max(logits, axis=-1, keepdims=True))
    soft = expd / jnp.sum(expd, axis=-1, keepdims=True)
    classes = lax.broadcasted_iota(jnp.int32, (ROWS, VOCAB), 1)
    dl = (soft - jnp.where(classes == target[...], 1.0, 0.0)).astype(BF16)
    dl_s[rows, :] = dl
    dy = nt(dl, w_read[...])
    dy_s[rows, :] = dy
    df = dy.astype(BF16)
    df_s[rows, :] = df
    bias_o[...] += jnp.sum(df.astype(F32), axis=0, keepdims=True)
    for copy in row_copies(step):
        copy.start()

    @pl.when(step == pl.num_programs(0) - 1)
    def _():
        whole = tn(out_s[...], dl_s[...]).astype(BF16)
        for shard in range(4):
            tile = whole[shard * 128 : shard * 128 + 128]
            put_parts(idx, keep, send, tile, shard, slice(4 * WIDTH, None))
            large = tn(act_s[:, shard * 512 : shard * 512 + 512], df_s[...]).astype(BF16)
            for xy in range(4):
                tile = large[xy * 128 : xy * 128 + 128]
                own_first = idx[0] == 0
                for i in range(4):
                    first = tile[16 * i : 16 * i + 16]
                    later = tile[64 + 16 * i : 64 + 16 * i + 16]
                    at = slice(i * WIDTH, (i + 1) * WIDTH)
                    keep[xy ^ idx[1], shard ^ idx[2], :, at] = jnp.where(own_first, first, later)
                    send[xy ^ idx[1], shard ^ idx[2], :, at] = jnp.where(own_first, later, first)
        for copy in copies[4:]:
            copy.wait()
        for place in range(act_s.shape[0] // ROWS):
            for copy in row_copies(place):
                copy.wait()


def feed_back_kernel(
    idx, vec, h_i, slope_i, dy_i, o0_i, o1_i, mix_i, up_i, down_i,
    dh_o, do_o, gain_o, shift_o, bias_o, keep, send,
    w_mix, w_up, w_down, h_s, slope_s, dy_s, o0, o1, dz_s, a2_s, da_s, dh_s, do_s,
    sems, row_sems, out_sems,
):
    step = pl.program_id(0)
    places = dz_s.shape[0] // ROWS
    half = pl.ds(HALF, HALF)
    moves = (
        (down_i, w_down), (up_i, w_up), (mix_i, w_mix), (o0_i.at[:, half], o0), (o1_i.at[:, half], o1)
    )
    copies = [pltpu.make_async_copy(src, dst, sems.at[i]) for i, (src, dst) in enumerate(moves)]

    def row_copies(place):
        at = pl.ds(pl.multiple_of(place * ROWS, ROWS), ROWS)
        pairs = ((dy_i, dy_s), (slope_i, slope_s), (h_i, h_s))
        return [
            pltpu.make_async_copy(src.at[at], dst.at[at], row_sems.at[place, i])
            for i, (src, dst) in enumerate(pairs)
        ]

    def out_copies(place):
        at = pl.ds(pl.multiple_of(place * ROWS, ROWS), ROWS)
        pairs = ((dh_s, dh_o), (do_s, do_o))
        return [
            pltpu.make_async_copy(src.at[at], dst.at[at], out_sems.at[place, i])
            for i, (src, dst) in enumerate(pairs)
        ]

    @pl.when(step == 0)
    def _():
        copies[0].start()
        for copy in row_copies(0):
            copy.start()
        for copy in copies[1:3]:
            copy.start()
        gain_o[...] = jnp.zeros_like(gain_o)
        shift_o[...] = jnp.zeros_like(shift_o)
        bias_o[...] = jnp.zeros_like(bias_o)
        copies[0].wait()

    for copy in row_copies(step)[:2]:
        copy.wait()
    rows = pl.ds(pl.multiple_of(step * ROWS, ROWS), ROWS)
    gain = vector_of(vec, idx, 2)
    d_out = dy_s[rows, :]
    df = d_out.astype(BF16)
    for j in range(4):
        at = slice(512 * j, 512 * j + 512)
        dz = (nt(df, w_down[at, :]) * slope_s[rows, at].astype(F32)).astype(BF16)
        dz_s[rows, at] = dz
        bias_o[:, at] += jnp.sum(dz.astype(F32), axis=0, keepdims=True)

    @pl.when(step == 0)
    def _():
        for place in range(1, places):
            for copy in row_copies(place):
                copy.start()
        for copy in copies[3:]:
            copy.start()
        for copy in copies[1:3]:
            copy.wait()

    row_copies(step)[2].wait()
    d_second = nt(dz_s[rows, :], w_up[...])
    unit, inverse = norm_parts(h_s[rows, :])
    a2_s[rows, :] = (unit * gain + vector_of(vec, idx, 3)).astype(BF16)
    gain_o[...] += jnp.sum(d_second * unit, axis=0, keepdims=True)
    shift_o[...] += jnp.sum(d_second, axis=0, keepdims=True)
    dh = d_out + norm_pull(d_second, unit, inverse, gain)
    dh_s[rows, :] = dh
    da = dh.astype(BF16)
    da_s[rows, :] = da
    do_s[rows, :] = nt(da, w_mix[...]).astype(BF16)
    for copy in out_copies(step):
        copy.start()

    @pl.when(step == pl.num_programs(0) - 1)
    def _():
        for copy in copies[3:]:
            copy.wait()
        for half in range(2):
            large = tn((o0, o1)[half][...], da_s[...]).astype(BF16)
            for i in range(2):
                tile = large[128 * i : 128 * i + 128]
                put_parts(idx, keep, send, tile, 2 * half + i, slice(0, WIDTH))
        for j in range(4):
            large = tn(a2_s[...], dz_s[:, 512 * j : 512 * j + 512]).astype(BF16)
            at = slice(WIDTH + 512 * j, WIDTH + 512 * j + 512)
            for shard in range(4):
                put_parts(idx, keep, send, large[shard * 128 : shard * 128 + 128], shard, at)
        for place in range(places):
            for copy in out_copies(place):
                copy.wait()


def proj_gradient(idx, both_t, w, dx, keep, send):
    on_gain = jnp.zeros((WIDTH, HALF), F32)
    sums = []
    for j in range(4):
        at = slice(j * HALF, (j + 1) * HALF)
        product = nn(both_t[...], dx[:, at])
        low = product[:WIDTH].astype(BF16)
        for shard in range(4):
            put_parts(idx, keep, send, low[shard * 128 : shard * 128 + 128], shard, at)
        on_gain += product[WIDTH : 2 * WIDTH] * w[:, at].astype(F32)
        sums.append(product[2 * WIDTH : 2 * WIDTH + 8])
    sums = side(*sums)
    high = sums.astype(BF16)
    rest = (sums - high.astype(F32)).astype(BF16)
    shift_rows = nt(jnp.concatenate([high, rest], axis=0), w[...])
    gain_column = jnp.sum(on_gain, axis=1, keepdims=True)
    gain_row = side(gain_column, jnp.zeros((WIDTH, 7), F32)).T[:1]
    return jnp.concatenate([gain_row, shift_rows[:1] + shift_rows[8:9], jnp.zeros((6, WIDTH), F32)])


def late_operands(pairs, sems):
    copies = [pltpu.make_async_copy(src, dst, sems.at[i]) for i, (src, dst) in enumerate(pairs)]

    @pl.when(pl.program_id(0) == 0)
    def _():
        for copy in copies:
            copy.start()

    return copies


def attend_back_kernel(
    idx, both_t, w, proj, floats, ratios, do_i, kept,
    dx_o, keep, send, share_o,
    state, count_z, dx_s, both_s, w_s, sems,
):
    copies = late_operands(((both_t, both_s), (w, w_s)), sems)
    attend_back_step(proj, floats, ratios, do_i, kept, dx_o, state, count_z, dx_s)

    @pl.when(pl.program_id(0) == pl.num_programs(0) - 1)
    def _():
        for copy in copies:
            copy.wait()
        share_o[...] = proj_gradient(idx, both_s, w_s, dx_s, keep, send)


def attend_back_last_kernel(
    idx, both_t, w, proj, floats, ratios, do_i, kept,
    share, g_g2, g_b2, g_bd, g_bu,
    dx_o, keep, send,
    state, count_z, dx_s, both_s, w_s, sems,
):
    copies = late_operands(((both_t, both_s), (w, w_s)), sems)
    attend_back_step(proj, floats, ratios, do_i, kept, dx_o, state, count_z, dx_s)

    @pl.when(pl.program_id(0) == pl.num_programs(0) - 1)
    def _():
        for copy in copies:
            copy.wait()
        total = proj_gradient(idx, both_s, w_s, dx_s, keep, send) + share[...]
        for s in range(4):
            at = slice(128 * s, 128 * s + 128)
            lines = [total[:2, at], g_g2[:, at], g_b2[:, at], g_bd[:, at]]
            lines += [g_bu[:, 512 * s + 128 * j : 512 * s + 128 * j + 128] for j in range(4)]
            lines.append(jnp.zeros((7, 128), F32))
            block = jnp.concatenate(lines, axis=0).astype(BF16)
            for xy in range(4):
                keep[xy, s ^ idx[2], :, COLS_PROJ:] = block
                send[xy, s ^ idx[2], :, COLS_PROJ:] = block


def attend_back_step(proj, floats, ratios, do_i, kept, dx_o, state, count_z, dx_s):
    step = pl.program_id(0)
    chunk = pl.num_programs(0) - 1 - step

    @pl.when(step == 0)
    def _():
        state[...] = jnp.zeros_like(state)
        count_z[...] = jnp.zeros_like(count_z)

    def take(ref, j, rows, pair):
        return ref[rows, j * HALF + 128 * pair : j * HALF + 128 * pair + 128]

    tri, trt, block, ones = causal_pair(), causal_pair(True), same_head(), head_ones()
    places = sub_places((1, 0))
    d_mixes, wide, d_numers, d_totals, others = {}, {}, {}, {}, {}
    for sub, pair, rows, at in places:
        v = take(proj, 2, rows, pair)
        d_mixes[sub, pair] = masked(tri, nt(do_i[rows, at], stacked(v)))
        wide[sub, pair] = stacked(take(proj, 3, rows, pair))
    for sub, pair, rows, at in places:
        do, ratio = do_i[rows, at], ratios[rows, at]
        q, k, v, e = [take(proj, j, rows, pair) for j in range(4)]
        inv, logits, probs = [take(floats, j, rows, pair) for j in (1, 2, 3)]
        d_ratio = nn(d_mixes[sub, pair], wide[sub, pair])
        d_ratio = (d_ratio + nt(do, kept[sub, pair][:, 128:])) * inv
        weighed = d_ratio * probs
        d_logits = weighed - probs * head_sum(weighed, ones)
        d_numers[sub, pair] = ((HEAD ** -0.5) * d_logits * inv).astype(BF16)
        d_totals[sub, pair] = (-(weighed + d_logits * logits) * inv).astype(BF16)
        wide_q, wide_r, wide_do = stacked(q), stacked(ratio), stacked(do)
        scores = masked(trt, nt(k, wide_q))
        mixing = masked(trt, nt(e, wide_r))
        d_mix_t = masked(trt, nt(v, wide_do))
        others[sub, pair] = (scores, d_mix_t, nn(mixing, wide_do), wide_q, wide_r)
    d_total = jnp.concatenate([side(d_totals[sub, 0], d_totals[sub, 1]) for sub in range(2)], axis=0)
    total_z = nn(causal_whole(True), d_total) + count_z[...]
    count_z[...] = total_z[:1, :]
    currents = [state[0], state[1]]
    lows = {}
    for sub, pair, rows, at in places:
        lows[sub, pair] = currents[pair].astype(BF16)
        more = side(
            tn(ratios[rows, at], do_i[rows, at]), tn(d_numers[sub, pair], take(proj, 0, rows, pair))
        )
        currents[pair] = currents[pair] + jnp.where(block, more, 0.0)
    state[0], state[1] = currents
    for sub, pair, rows, at in places:
        k, v, e = [take(proj, j, rows, pair) for j in (1, 2, 3)]
        scores, d_mix_t, dv, wide_q, wide_r = others[sub, pair]
        d_numer, low = d_numers[sub, pair], lows[sub, pair]
        wide_n = stacked(d_numer)
        d_scores = masked(tri, nt(d_numer, wide[sub, pair]))
        d_scores_t = masked(trt, nt(e, wide_n))
        both = nn(e, low)
        de = nn(side(d_mix_t, scores), jnp.concatenate([wide_r, wide_n], axis=0))
        de = de + nt(side(v, k), low) + total_z[rows, at]
        dq = nn(d_scores, stacked(k)) + nn(d_numer, kept[sub, pair][:, :128])
        dk = nn(d_scores_t, wide_q) + both[:, 128:]
        dv = dv + both[:, :128]
        dc = de * take(floats, 0, rows, pair)
        for j, value in enumerate((dq, dk, dv, dc)):
            dx_o[rows, j * HALF + 128 * pair : j * HALF + 128 * pair + 128] = value.astype(BF16)
    dx_s[pl.ds(pl.multiple_of(chunk * CHUNK, CHUNK), CHUNK), :] = dx_o[...]


def inputs_kernel(idx, vec, x, dh, dx0, dx1, w0, w1, dx_o):
    unit, inverse = norm_parts(x[...].astype(F32))
    d_first = nt(dx0[...], w0[...]) + nt(dx1[...], w1[...])
    dx_o[...] = dh[...] + norm_pull(d_first, unit, inverse, vector_of(vec, idx, 0))


def unpack_proj_kernel(idx, near, far, query, key, value, control, g1, b1, g2, b2, bd, bu):
    for shard, member, piece in each_member(idx, near, far):
        rows = rows_at(member * PIECE, PIECE)
        for j, out in enumerate((query, key, value, control)):
            for half in range(2):
                start = half * COLS_PROJ + j * HALF
                out[rows, half * HALF : (half + 1) * HALF] = piece[:, start : start + HALF].astype(F32)

        @pl.when(member == 0)
        def _():
            lines = piece[:, COLS_BOTH:].astype(F32)
            for i, out in enumerate((g1, b1, g2, b2, bd)):
                out[...] = lines[i]
            for i in range(4):
                bu[128 * i : 128 * i + 128] = lines[5 + i]


def unpack_feed_kernel(idx, near, far, mix, up, down, read):
    for shard, member, piece in each_member(idx, near, far):
        rows = rows_at(member * PIECE, PIECE)
        mix[rows, :] = piece[:, :WIDTH].astype(F32)
        up[rows, :] = piece[:, WIDTH:COLS_UP].astype(F32)
        for i in range(4):
            start = COLS_UP + i * WIDTH
            down[rows_at(member * 64 + 16 * i, PIECE), :] = piece[:, start : start + WIDTH].astype(F32)
        read[rows, :] = piece[:, COLS_UP + 4 * WIDTH :].astype(F32)


def shaped(shape, dtype):
    return jax.ShapeDtypeStruct(shape, dtype)


def call(kernel, name, args, outs, steps=None, scratch=(), flops=0, limit=56):
    grid = (steps,) if steps else ()

    def spec(shape, block):
        if block == "hbm":
            return pl.BlockSpec(memory_space=pl.ANY)
        if block is None:
            return pl.BlockSpec(tuple(shape), lambda *_: (0,) * len(shape))
        return pl.BlockSpec(*block)

    in_specs = []
    for array, block in args:
        if array.dtype == jnp.int32 and array.shape == (3,):
            in_specs.append(pl.BlockSpec(memory_space=pltpu.SMEM))
        else:
            in_specs.append(spec(array.shape, block))
    moved = sum(a.size * a.dtype.itemsize for a, _ in args)
    return pl.pallas_call(
        kernel,
        grid=grid,
        in_specs=in_specs,
        out_specs=[spec(shape, block) for shape, _, block in outs],
        out_shape=[shaped(shape, dtype) for shape, dtype, _ in outs],
        scratch_shapes=list(scratch),
        compiler_params=pltpu.CompilerParams(
            vmem_limit_bytes=limit * MIB,
            dimension_semantics=("arbitrary",) * len(grid) if grid else None,
        ),
        cost_estimate=pl.CostEstimate(flops=1000, bytes_accessed=1000, transcendentals=0),
        name=name,
    )(*[array for array, _ in args])


def swap(value, axis, size, distance):
    return lax.ppermute(value, axis, [(i, i ^ distance) for i in range(size)])


def pin(*values):
    return lax.optimization_barrier(values)


def near_rows(piece, shards):
    return [swap(piece, "shard", shards, k) for k in range(1, 4)]


def near_pair(piece, shards):
    return jnp.stack([piece, swap(piece, "shard", shards, 1)])


def far_pair(pair, shards):
    return swap(pair, "shard", shards, 2)


def sum_of(values):
    values = [v.astype(F32) for v in values]
    return ((values[0] + values[1]) + (values[2] + values[3])).astype(BF16)


def core_sum(keep, got):
    return [(keep[k].astype(F32) + got[k].astype(F32)).astype(BF16) for k in range(4)]


def plane_start(parts, dp):
    return [swap(parts[k], "dp", dp, 2 * k) for k in range(1, 4)]


def plane_sum(parts, got):
    return [sum_of([parts[0][k], got[0][k], got[1][k], got[2][k]]) for k in range(4)]


def plane_halves(parts, got):
    total = [p.astype(F32) for p in [parts[0]] + got]
    total = ((total[0] + total[1]) + (total[2] + total[3])).astype(BF16)
    return total[:2], total[2:]


def half_start(high, shards):
    return swap(high, "shard", shards, 2)


def half_sum(low, got):
    return [(low[k].astype(F32) + got[k].astype(F32)).astype(BF16) for k in range(2)]


def last_start(pair, shards):
    return swap(pair[1], "shard", shards, 1)


def last_sum(pair, got, dp):
    return across_planes((pair[0].astype(F32) + got.astype(F32)).astype(BF16), dp)


def across_planes(total, dp):
    distance = 8
    while distance < dp:
        total = (total.astype(F32) + swap(total, "dp", dp, distance).astype(F32)).astype(BF16)
        distance *= 2
    return total


def shard_start(rows, shards):
    return [swap(rows[k], "shard", shards, k) for k in range(1, 4)]


def shard_sum(rows, got, dp):
    return across_planes(sum_of([rows[0]] + got), dp)


def body(dp, shards):
    def on_device(
        tokens, targets, gain_one, bias_one, w_query, w_key, w_value, w_control, w_mix,
        gain_two, bias_two, w_up, bias_up, w_down, bias_down, w_read,
    ):
        count = tokens.shape[0]
        steps = count // CHUNK
        rows = WIDTH // shards
        member = lax.axis_index("dp") % 8
        idx = jnp.stack([member % 2, member // 2, lax.axis_index("shard")]).astype(jnp.int32)
        forward = lambda i: (i, 0)
        back = lambda i: (steps - 1 - i, 0)
        tok = lambda n: ((CHUNK, n), forward)
        parts = (4, 4, PIECE)

        weights = (w_query, w_key, w_value, w_control, w_mix, w_up, w_down, w_read)
        sizes = [(PIECE, COLS_BOTH + 128), (PIECE, COLS_UP), (2, PIECE, COLS_DOWN)]
        vectors = (gain_one, bias_one, gain_two, bias_two, bias_down, bias_up)
        pa, pu, pd = call(
            pack_kernel,
            "pack_weights",
            [(idx, None)] + [(v, None) for v in vectors] + [(w, "hbm") for w in weights],
            [(size, BF16, None) for size in sizes],
            scratch=[pltpu.SemaphoreType.DMA((20,))],
        )
        got_a = near_rows(pa, shards)
        pair_u = near_pair(pu, shards)
        rows_a = jnp.stack([pa[:, :COLS_BOTH]] + [g[:, :COLS_BOTH] for g in got_a])
        vec = jnp.stack([pa[:, COLS_BOTH:]] + [g[:, COLS_BOTH:] for g in got_a])
        rows_a, vec, pair_u, pd, tokens_a = pin(rows_a, vec, pair_u, pd, tokens)
        plane_a = [swap(rows_a, "dp", dp, 2 * k) for k in range(1, 4)]
        got_u = far_pair(pair_u, shards)
        pair_d = near_pair(pd, shards)
        a1, both_t = call(
            first_norm_kernel,
            "first_norm",
            [(idx, None), (vec, None), (tokens_a, None)],
            [
                ((count, WIDTH), BF16, None),
                ((2 * WIDTH + PIECE, count), BF16, None),
            ],
        )
        target = targets.reshape(count, 1)
        plane_a, got_u, pair_d, a1, both_t, target = pin(
            plane_a, got_u, pair_d, a1, both_t, target
        )
        near_a = jnp.stack([rows_a] + plane_a)
        far_a = swap(near_a, "dp", dp, 1)
        got_d = far_pair(pair_d, shards)
        got_u, _ = pin(got_u, near_a)
        rows_u = jnp.concatenate([pair_u, got_u])
        plane_u = plane_start([rows_u] * 4, dp)

        kept = ((2, 2, 128, 256), lambda i: (i, 0, 0, 0))

        def attend(a1, half):
            at = ((4, 4, PIECE, COLS_PROJ), lambda i: (0, 0, 0, half))
            return call(
                attend_kernel,
                "attend",
                [(idx, None), (a1, tok(WIDTH)), (near_a, at), (far_a, at)],
                [
                    ((count, COLS_PROJ), BF16, tok(COLS_PROJ)),
                    ((count, COLS_PROJ), F32, tok(COLS_PROJ)),
                    ((count, 2 * HALF), BF16, tok(2 * HALF)),
                    ((2 * steps, 2, 128, 256), BF16, kept),
                    ((WIDTH, COLS_PROJ), BF16, None),
                ],
                steps,
                [
                    pltpu.VMEM((2, 128, 256), F32),
                    pltpu.VMEM((1, HALF), F32),
                ],
                flops=6e9,
            )

        first = attend(a1, 0)
        first, plane_u, got_d, a1 = pin(first, plane_u, got_d, a1)
        rows_d = jnp.concatenate([pair_d, got_d])
        plane_d = [swap(rows_d[:, 0], "dp", dp, 2 * k) for k in range(1, 3)]
        near_u = jnp.stack([rows_u] + plane_u)
        far_u = swap(near_u, "dp", dp, 1)
        second = attend(a1, 1)
        second, far_u, plane_d = pin(second, far_u, plane_d)
        near_d = jnp.stack([rows_d[:, 0]] + plane_d + [rows_d[:, 1]])
        far_d = swap(near_d, "dp", dp, 1)
        halves = (first, second)
        o0, o1 = first[2], second[2]

        wide = lambda n: ((ROWS, n), forward)
        mixed_at = ((ROWS, HALF), lambda i: (i, 1))
        places = count // ROWS
        out, h, slope, dy, g_bias_down, keep_d, send_d, full_mix, full_up, full_down = call(
            feed_kernel,
            "feed_forward",
            [
                (idx, None), (vec, None), (tokens, wide(WIDTH)), (o0, mixed_at), (o1, mixed_at),
                (target, wide(1)), (near_u, "hbm"), (far_u, "hbm"), (near_d, "hbm"), (far_d, "hbm"),
            ],
            [
                ((count, WIDTH), BF16, "hbm"),
                ((count, WIDTH), F32, "hbm"),
                ((count, FF), BF16, "hbm"),
                ((count, WIDTH), F32, "hbm"),
                ((1, WIDTH), F32, None),
                (parts + (COLS_DOWN,), BF16, None),
                (parts + (COLS_DOWN,), BF16, None),
                ((WIDTH, WIDTH), BF16, "hbm"),
                ((WIDTH, FF), BF16, "hbm"),
                ((FF, WIDTH), BF16, "hbm"),
            ],
            places,
            [
                pltpu.VMEM(parts + (COLS_UP,), BF16),
                pltpu.VMEM(parts + (COLS_UP,), BF16),
                pltpu.VMEM(parts + (COLS_DOWN,), BF16),
                pltpu.VMEM(parts + (COLS_DOWN,), BF16),
                pltpu.VMEM((WIDTH, WIDTH), BF16),
                pltpu.VMEM((WIDTH, FF), BF16),
                pltpu.VMEM((FF, WIDTH), BF16),
                pltpu.VMEM((WIDTH, VOCAB), BF16),
                pltpu.VMEM((count, FF), BF16),
                pltpu.VMEM((count, WIDTH), BF16),
                pltpu.VMEM((count, WIDTH), F32),
                pltpu.VMEM((count, FF), BF16),
                pltpu.VMEM((count, WIDTH), F32),
                pltpu.VMEM((count, VOCAB), BF16),
                pltpu.VMEM((count, WIDTH), BF16),
                pltpu.SemaphoreType.DMA((7,)),
                pltpu.SemaphoreType.DMA((places, 4)),
            ],
            flops=8e9,
        )
        got_d = swap(send_d, "dp", dp, 1)

        dh, d_mixed, g_gain_two, g_bias_two, g_bias_up, keep_u, send_u = call(
            feed_back_kernel,
            "feed_backward",
            [(idx, None), (vec, None)]
            + [(t, "hbm") for t in (h, slope, dy, o0, o1, full_mix, full_up, full_down)],
            [
                ((count, WIDTH), F32, "hbm"),
                ((count, WIDTH), BF16, "hbm"),
                ((1, WIDTH), F32, None),
                ((1, WIDTH), F32, None),
                ((1, FF), F32, None),
                (parts + (COLS_UP,), BF16, None),
                (parts + (COLS_UP,), BF16, None),
            ],
            places,
            [
                pltpu.VMEM((WIDTH, WIDTH), BF16),
                pltpu.VMEM((WIDTH, FF), BF16),
                pltpu.VMEM((FF, WIDTH), BF16),
                pltpu.VMEM((count, WIDTH), F32),
                pltpu.VMEM((count, FF), BF16),
                pltpu.VMEM((count, WIDTH), F32),
                pltpu.VMEM((count, HALF), BF16),
                pltpu.VMEM((count, HALF), BF16),
                pltpu.VMEM((count, FF), BF16),
                pltpu.VMEM((count, WIDTH), BF16),
                pltpu.VMEM((count, WIDTH), BF16),
                pltpu.VMEM((count, WIDTH), F32),
                pltpu.VMEM((count, WIDTH), BF16),
                pltpu.SemaphoreType.DMA((5,)),
                pltpu.SemaphoreType.DMA((places, 3)),
                pltpu.SemaphoreType.DMA((places, 2)),
            ],
            flops=8e9,
        )
        got_d, d_mixed, send_u = pin(got_d, d_mixed, send_u)
        got_u = swap(send_u, "dp", dp, 1)
        sum_d = core_sum(keep_d, got_d)
        sum_d, d_mixed = pin(sum_d, d_mixed)
        got_d = plane_start(sum_d, dp)

        kept_back = ((2, 2, 128, 256), lambda i: (steps - 1 - i, 0, 0, 0))

        def attend_back(half, d_mixed, extra=()):
            proj, floats, mixed, states, w = halves[half]
            wide = ((CHUNK, COLS_PROJ), back)
            column = ((CHUNK, HALF), lambda i: (steps - 1 - i, half))
            last = half == 1
            cols = COLS_LAST if last else COLS_PROJ
            return call(
                attend_back_last_kernel if last else attend_back_kernel,
                "attend_backward",
                [(idx, None), (both_t, "hbm"), (w, "hbm")]
                + [(proj, wide), (floats, wide), (mixed, ((CHUNK, HALF), back))]
                + [(d_mixed, column), (states, kept_back)]
                + [(t, None) for t in extra],
                [
                    ((count, COLS_PROJ), BF16, ((CHUNK, COLS_PROJ), back)),
                    (parts + (cols,), BF16, None),
                    (parts + (cols,), BF16, None),
                ]
                + ([] if last else [((8, WIDTH), F32, None)]),
                steps,
                [
                    pltpu.VMEM((2, 128, 256), F32),
                    pltpu.VMEM((1, HALF), F32),
                    pltpu.VMEM((count, COLS_PROJ), BF16),
                    pltpu.VMEM((2 * WIDTH + PIECE, count), BF16),
                    pltpu.VMEM((WIDTH, COLS_PROJ), BF16),
                    pltpu.SemaphoreType.DMA((2,)),
                ],
                flops=10e9,
            )

        dx0, keep_a, send_a, share = attend_back(0, d_mixed)
        got_d, got_u, send_a, d_mixed = pin(got_d, got_u, send_a, d_mixed)
        got_a = swap(send_a, "dp", dp, 1)
        sum_u = core_sum(keep_u, got_u)
        low_d, high_d = plane_halves(sum_d, got_d)
        sum_u, low_d, high_d, d_mixed = pin(sum_u, low_d, high_d, d_mixed)
        got_u = plane_start(sum_u, dp)
        got_d = half_start(high_d, shards)

        extra = (share, g_gain_two, g_bias_two, g_bias_down, g_bias_up)
        dx1, keep_b, send_b = attend_back(1, d_mixed, extra)
        got_d, got_u, got_a, send_b, dx1 = pin(got_d, got_u, got_a, send_b, dx1)
        got_b = swap(send_b, "dp", dp, 1)
        sum_p = [
            jnp.concatenate(both, axis=-1)
            for both in zip(core_sum(keep_a, got_a), core_sum(keep_b, got_b))
        ]
        sum_p, dx1 = pin(sum_p, dx1)
        got_p = plane_start(sum_p, dp)
        got_u, got_d, _ = pin(got_u, got_d, sum_p)
        low_u, high_u = plane_halves(sum_u, got_u)
        got_u = half_start(high_u, shards)
        pair_d = half_sum(low_d, got_d)
        got_d = last_start(pair_d, shards)
        d_tokens = call(
            inputs_kernel,
            "input_gradient",
            [
                (idx, None), (vec, None), (tokens, tok(WIDTH)), (dh, tok(WIDTH)),
                (dx0, tok(COLS_PROJ)), (dx1, tok(COLS_PROJ)),
                (first[4], None), (second[4], None),
            ],
            [((count, WIDTH), F32, tok(WIDTH))],
            steps,
            flops=3e9,
        )[0]
        got_u, got_d, d_tokens = pin(got_u, got_d, d_tokens)
        pair_u = half_sum(low_u, got_u)
        got_u = last_start(pair_u, shards)
        total_d = last_sum(pair_d, got_d, dp)
        got_p, _, _ = pin(got_p, pair_u, d_tokens)
        rows_p = plane_sum(sum_p, got_p)
        got_p = shard_start(rows_p, shards)
        got_u, _ = pin(got_u, rows_p)
        total_f = jnp.concatenate([last_sum(pair_u, got_u, dp), total_d], axis=-1)
        along_f = swap(total_f, "dp", dp, 4)
        got_p, _ = pin(got_p, total_f)
        total_p = shard_sum(rows_p, got_p, dp)
        plane_p = plane_start([total_p] * 4, dp)
        along_f, _ = pin(along_f, total_p)
        pair_f = jnp.stack([total_f, along_f])
        up_f = swap(pair_f, "dp", dp, 2)
        near_p = jnp.stack([total_p] + plane_p)
        far_p = swap(near_p, "dp", dp, 1)
        g_query, g_key, g_value, g_control, g1, b1, g2, b2, bd, bu = call(
            unpack_proj_kernel,
            "unpack_proj",
            [(idx, None), (near_p, None), (far_p, None)],
            [((rows, WIDTH), F32, None)] * 4 + [((128,), F32, None)] * 5 + [((512,), F32, None)],
        )
        up_f, _ = pin(up_f, g_query)
        near_f = jnp.stack([pair_f, up_f], axis=1).reshape((4,) + total_f.shape)
        far_f = swap(near_f, "dp", dp, 1)
        g_mix, g_up, g_down, g_read = call(
            unpack_feed_kernel,
            "unpack_feed",
            [(idx, None), (near_f, None), (far_f, None)],
            [
                ((rows, WIDTH), F32, None),
                ((rows, FF), F32, None),
                ((4 * rows, WIDTH), F32, None),
                ((rows, VOCAB), F32, None),
            ],
        )
        return (
            out, d_tokens, g1, b1, g_query, g_key, g_value, g_control, g_mix,
            g2, b2, g_up, bu, g_down, bd, g_read,
        )

    return on_device


def solution(mesh):
    dp, shards = mesh.shape["dp"], mesh.shape["shard"]
    vector, matrix = P("shard"), P("shard", None)
    rows = P(("dp", "shard"), None)
    params = (
        vector, vector, matrix, matrix, matrix, matrix, matrix,
        vector, vector, matrix, vector, matrix, vector, matrix,
    )
    return jax.shard_map(
        body(dp, shards),
        mesh=mesh,
        in_specs=(rows, P(("dp", "shard"))) + params,
        out_specs=(rows, rows) + params,
        check_vma=False,
    )
```

```python
import jax
import jax.numpy as jnp
from jax import lax
from jax.experimental import pallas as pl
from jax.experimental.pallas import tpu as pltpu
from jax.sharding import PartitionSpec as P

EPS = 1e-05
WIDTH = 512
HEAD = 64
FF = 2048
VOCAB = 256
SEQ_LEN = 1024
CHUNK = 256
SUB = 128
SUBS = CHUNK // SUB
ROWS = 512
HALF = 256
PIECE = 16
COLS_PROJ = 4 * HALF
COLS_BOTH = 2 * COLS_PROJ
COLS_LAST = COLS_PROJ + 128
COLS_UP = WIDTH + FF
COLS_DOWN = 4 * WIDTH + VOCAB
F32 = jnp.float32
BF16 = jnp.bfloat16
MIB = 1024 * 1024


def nn(a, b):
    return lax.dot_general(a, b, (((1,), (0,)), ((), ())), preferred_element_type=F32)


def nt(a, b):
    return lax.dot_general(a, b, (((1,), (1,)), ((), ())), preferred_element_type=F32)


def tn(a, b):
    return lax.dot_general(a, b, (((0,), (0,)), ((), ())), preferred_element_type=F32)


def norm_parts(values):
    centre = values - jnp.mean(values, axis=-1, keepdims=True)
    inverse = lax.rsqrt(jnp.mean(centre * centre, axis=-1, keepdims=True) + EPS)
    return centre * inverse, inverse


def norm_pull(grad, unit, inverse, gain):
    scaled = grad * gain
    return inverse * (
        scaled
        - jnp.mean(scaled, axis=-1, keepdims=True)
        - unit * jnp.mean(scaled * unit, axis=-1, keepdims=True)
    )


def vector_of(vec_ref, idx, row):
    return jnp.concatenate(
        [vec_ref[s ^ idx[2], row : row + 1, :].astype(F32) for s in range(4)], axis=1
    )


def bias_up_of(vec_ref, idx):
    return jnp.concatenate(
        [
            vec_ref[s ^ idx[2], row : row + 1, :].astype(F32)
            for s in range(4)
            for row in range(5, 9)
        ],
        axis=1,
    )


def each_piece(idx, near, far):
    for c, buf in ((0, near), (1, far)):
        for xy in range(4):
            member = ((xy ^ idx[1]) * 2) + (c ^ idx[0])
            for s in range(4):
                yield s ^ idx[2], member, buf.at[xy, s]


def each_member(idx, near, far):
    for c, buf in ((0, near), (1, far)):
        for xy in range(4):
            yield None, ((xy ^ idx[1]) * 2) + (c ^ idx[0]), buf.at[xy]


def rows_at(start, size):
    return pl.ds(pl.multiple_of(start, PIECE), size)


def put_parts(idx, keep, send, tile, shard, columns):
    for xy in range(4):
        first = tile[32 * xy : 32 * xy + 16]
        second = tile[32 * xy + 16 : 32 * xy + 32]
        own_first = idx[0] == 0
        keep[xy ^ idx[1], shard ^ idx[2], :, columns] = jnp.where(own_first, first, second)
        send[xy ^ idx[1], shard ^ idx[2], :, columns] = jnp.where(own_first, second, first)


def pack_kernel(
    idx, g1, b1, g2, b2, bd, bu, wq, wk, wv, wc, wm, wu, wd, wr, pa, pc, pd, sems
):
    member = idx[1] * 2 + idx[0]
    across = (idx[1] ^ 3) * 2 + idx[0]
    rows = rows_at(member * PIECE, PIECE)
    moves = []
    for j, w in enumerate((wq, wk, wv, wc)):
        for half in range(2):
            start = half * COLS_PROJ + j * HALF
            part = w.at[rows, half * HALF : (half + 1) * HALF]
            moves.append((part, pa.at[:, start : start + HALF]))
    moves.append((wm.at[rows, :], pc.at[:, :WIDTH]))
    moves.append((wu.at[rows, :], pc.at[:, WIDTH:]))
    for place, who in enumerate((member, across)):
        for i in range(4):
            part = wd.at[rows_at(who * 64 + 16 * i, PIECE), :]
            moves.append((part, pd.at[place, :, i * WIDTH : (i + 1) * WIDTH]))
        moves.append((wr.at[rows_at(who * PIECE, PIECE), :], pd.at[place, :, 4 * WIDTH :]))
    copies = [pltpu.make_async_copy(src, dst, sems.at[i]) for i, (src, dst) in enumerate(moves)]
    for copy in copies:
        copy.start()
    lines = [v[...].astype(F32).reshape(1, 128) for v in (g1, b1, g2, b2, bd)]
    lines += [bu[128 * j : 128 * j + 128].astype(F32).reshape(1, 128) for j in range(4)]
    lines.append(jnp.zeros((7, 128), F32))
    pa[:, COLS_BOTH:] = jnp.concatenate(lines, axis=0).astype(BF16)
    for copy in copies:
        copy.wait()


def first_norm_kernel(idx, vec, x, a1, both_t):
    unit, _ = norm_parts(x[...].astype(F32))
    low = (unit * vector_of(vec, idx, 0) + vector_of(vec, idx, 1)).astype(BF16)
    a1[...] = low
    both_t[:WIDTH, :] = low.T
    both_t[WIDTH : 2 * WIDTH, :] = unit.astype(BF16).T
    both_t[2 * WIDTH :, :] = jnp.ones((PIECE, both_t.shape[1]), BF16)


def lanes_low():
    return lax.broadcasted_iota(jnp.int32, (1, 128), 1) < HEAD


def stacked(value):
    low = lanes_low().astype(F32).astype(BF16)
    high = (1.0 - lanes_low().astype(F32)).astype(BF16)
    return jnp.concatenate([value * low, value * high], axis=0)


def head_ones():
    row = (lax.broadcasted_iota(jnp.int32, (256, 128), 0) & 127) < HEAD
    col = lax.broadcasted_iota(jnp.int32, (256, 128), 1) < HEAD
    return (row == col).astype(F32).astype(BF16)


def head_sum(value, ones):
    high = value.astype(BF16)
    rest = (value - high.astype(F32)).astype(BF16)
    return nn(side(high, rest), ones)


def sub_places(subs):
    return [
        (sub, pair, slice(SUB * sub, SUB * sub + SUB), slice(128 * pair, 128 * pair + 128))
        for sub in subs
        for pair in range(2)
    ]


def head_max(value):
    low = lanes_low()
    first = jnp.max(jnp.where(low, value, -jnp.inf), axis=-1, keepdims=True)
    second = jnp.max(jnp.where(low, -jnp.inf, value), axis=-1, keepdims=True)
    return jnp.where(low, first, second)


def same_head():
    row = lax.broadcasted_iota(jnp.int32, (128, 256), 0) < HEAD
    col = (lax.broadcasted_iota(jnp.int32, (128, 256), 1) & 127) < HEAD
    return row == col


def causal_pair(transposed=False):
    row = lax.broadcasted_iota(jnp.int32, (SUB, 2 * SUB), 0)
    col = lax.broadcasted_iota(jnp.int32, (SUB, 2 * SUB), 1) & (SUB - 1)
    return (row <= col) if transposed else (col <= row)


def causal_whole(transposed=False):
    row = lax.broadcasted_iota(jnp.int32, (CHUNK, CHUNK), 0)
    col = lax.broadcasted_iota(jnp.int32, (CHUNK, CHUNK), 1)
    keep = (row <= col) if transposed else (col <= row)
    return keep.astype(F32).astype(BF16)


def side(*values):
    return jnp.concatenate(values, axis=1)


def masked(keep, value):
    return jnp.where(keep, value, 0.0).astype(BF16)


def attend_kernel(idx, a1, near, far, proj_o, float_o, mixed_o, kept, w_o, state, count_z):
    step = pl.program_id(0)

    @pl.when(step == 0)
    def _():
        for shard, member, piece in each_piece(idx, near, far):
            w_o[rows_at(shard * 128 + member * PIECE, PIECE), :] = piece[...]
        state[...] = jnp.zeros_like(state)
        count_z[...] = jnp.zeros_like(count_z)

    a = a1[...]
    q_all = nn(a, w_o[:, :HALF]).astype(BF16)
    k_all = nn(a, w_o[:, HALF : 2 * HALF]).astype(BF16)
    expo = jnp.exp(nn(a, w_o[:, 3 * HALF :]))
    e_all = expo.astype(BF16)
    v_all = nn(a, w_o[:, 2 * HALF : 3 * HALF]).astype(BF16)
    for j, value in enumerate((q_all, k_all, v_all, e_all)):
        proj_o[:, j * HALF : (j + 1) * HALF] = value
    float_o[:, :HALF] = expo
    total = nn(causal_whole(), e_all) + count_z[...]
    count_z[...] = total[CHUNK - 1 :, :]
    inverse = 1.0 / total
    float_o[:, HALF : 2 * HALF] = inverse
    tri, block, ones = causal_pair(), same_head(), head_ones()
    places = sub_places(range(SUBS))
    lows, wide_e, numers, ratios = {}, {}, {}, {}
    for pair in range(2):
        current = state[pair]
        for sub in range(SUBS):
            rows, at = slice(SUB * sub, SUB * sub + SUB), slice(128 * pair, 128 * pair + 128)
            lows[sub, pair] = current.astype(BF16)
            kept[sub, pair] = lows[sub, pair]
            wide_e[sub, pair] = stacked(e_all[rows, at])
            more = tn(e_all[rows, at], side(k_all[rows, at], v_all[rows, at]))
            current = current + jnp.where(block, more, 0.0)
        state[pair] = current
    for sub, pair, rows, at in places:
        scores = masked(tri, nt(q_all[rows, at], stacked(k_all[rows, at])))
        numer = nn(scores, wide_e[sub, pair])
        numers[sub, pair] = numer + nt(q_all[rows, at], lows[sub, pair][:, :128])

    def soften(sub, pair, rows, at):
        inv = inverse[rows, at]
        logits = (HEAD ** -0.5) * numers[sub, pair] * inv
        expd = jnp.exp(logits - head_max(logits))
        probs = expd * (1.0 / head_sum(expd, ones))
        ratios[sub, pair] = (probs * inv).astype(BF16)
        float_o[rows, 2 * HALF + 128 * pair : 2 * HALF + 128 * pair + 128] = logits
        float_o[rows, 3 * HALF + 128 * pair : 3 * HALF + 128 * pair + 128] = probs
        mixed_o[rows, at] = ratios[sub, pair]

    def mix(sub, pair, rows, at):
        mixing = masked(tri, nt(ratios[sub, pair], wide_e[sub, pair]))
        out = nn(mixing, stacked(v_all[rows, at])) + nn(ratios[sub, pair], lows[sub, pair][:, 128:])
        mixed_o[rows, HALF + 128 * pair : HALF + 128 * pair + 128] = out.astype(BF16)

    for i, place in enumerate(places):
        soften(*place)
        if i:
            mix(*places[i - 1])
    mix(*places[-1])


def feed_kernel(
    idx, vec, x, o0, o1, target, up_near_i, up_far_i, down_near_i, down_far_i,
    out_o, h_o, slope_o, dy_o, bias_o, keep, send, mix_o, up_o, down_o,
    up_near, up_far, down_near, down_far,
    w_mix, w_up, w_down, w_read, act_s, out_s, h_s, slope_s, dy_s, dl_s, df_s, sems, row_sems,
):
    step = pl.program_id(0)
    moves = (
        (up_near_i, up_near), (up_far_i, up_far), (down_near_i, down_near), (down_far_i, down_far),
        (w_mix, mix_o), (w_up, up_o), (w_down, down_o),
    )
    copies = [pltpu.make_async_copy(src, dst, sems.at[i]) for i, (src, dst) in enumerate(moves)]

    @pl.when(step == 0)
    def _():
        for copy in copies[:4]:
            copy.start()
        for copy in copies[:2]:
            copy.wait()
        for shard, member, piece in each_piece(idx, up_near, up_far):
            rows = rows_at(shard * 128 + member * PIECE, PIECE)
            w_mix[rows, :] = piece[:, :WIDTH]
            w_up[rows, :] = piece[:, WIDTH:]
        for copy in copies[2:4]:
            copy.wait()
        for shard, member, piece in each_piece(idx, down_near, down_far):
            for i in range(4):
                rows = rows_at(shard * 512 + member * 64 + 16 * i, PIECE)
                w_down[rows, :] = piece[:, i * WIDTH : (i + 1) * WIDTH]
            w_read[rows_at(shard * 128 + member * PIECE, PIECE), :] = piece[:, 4 * WIDTH :]
        for copy in copies[4:]:
            copy.start()
        bias_o[...] = jnp.zeros_like(bias_o)

    def row_copies(place):
        at = pl.ds(pl.multiple_of(place * ROWS, ROWS), ROWS)
        pairs = ((out_s, out_o), (h_s, h_o), (slope_s, slope_o), (dy_s, dy_o))
        return [
            pltpu.make_async_copy(src.at[at], dst.at[at], row_sems.at[place, i])
            for i, (src, dst) in enumerate(pairs)
        ]

    rows = pl.ds(pl.multiple_of(step * ROWS, ROWS), ROWS)
    attn = nn(o0[...], w_mix[:HALF, :]) + nn(o1[...], w_mix[HALF:, :])
    resid = x[...].astype(F32) + attn
    h_s[rows, :] = resid
    unit, _ = norm_parts(resid)
    second = (unit * vector_of(vec, idx, 2) + vector_of(vec, idx, 3)).astype(BF16)
    bias = bias_up_of(vec, idx)
    branch = jnp.zeros((ROWS, WIDTH), F32)
    scale = (2.0 / jnp.pi) ** 0.5
    at = [slice(512 * j, 512 * j + 512) for j in range(4)]
    products = nn(second, w_up[:, at[0]])
    for j in range(4):
        z = products + bias[:, at[j]]
        if j < 3:
            products = nn(second, w_up[:, at[j + 1]])
        zz = z * z
        cdf = 0.5 + 0.5 * jnp.tanh(z * (scale + (scale * 0.044715) * zz))
        active = z * cdf
        slope = cdf + (active - active * cdf) * (2 * scale + (6 * scale * 0.044715) * zz)
        slope_s[rows, at[j]] = slope.astype(BF16)
        act = active.astype(BF16)
        act_s[rows, at[j]] = act
        branch += nn(act, w_down[at[j], :])
    out = (resid + (branch + vector_of(vec, idx, 4))).astype(BF16)
    out_s[rows, :] = out
    logits = nn(out, w_read[...])
    expd = jnp.exp(logits - jnp.max(logits, axis=-1, keepdims=True))
    soft = expd / jnp.sum(expd, axis=-1, keepdims=True)
    classes = lax.broadcasted_iota(jnp.int32, (VOCAB, ROWS), 0)
    hits = jnp.where(classes == target[rows].reshape(1, ROWS), 1.0, 0.0).T
    dl = (soft - hits).astype(BF16)
    dl_s[rows, :] = dl
    dy = nt(dl, w_read[...])
    dy_s[rows, :] = dy
    df = dy.astype(BF16)
    df_s[rows, :] = df
    bias_o[...] += jnp.sum(df.astype(F32), axis=0, keepdims=True)
    for copy in row_copies(step):
        copy.start()

    @pl.when(step == pl.num_programs(0) - 1)
    def _():
        whole = tn(out_s[...], dl_s[...]).astype(BF16)
        for shard in range(4):
            tile = whole[shard * 128 : shard * 128 + 128]
            put_parts(idx, keep, send, tile, shard, slice(4 * WIDTH, None))
            large = tn(act_s[:, shard * 512 : shard * 512 + 512], df_s[...]).astype(BF16)
            for xy in range(4):
                tile = large[xy * 128 : xy * 128 + 128]
                own_first = idx[0] == 0
                for i in range(4):
                    first = tile[16 * i : 16 * i + 16]
                    later = tile[64 + 16 * i : 64 + 16 * i + 16]
                    at = slice(i * WIDTH, (i + 1) * WIDTH)
                    keep[xy ^ idx[1], shard ^ idx[2], :, at] = jnp.where(own_first, first, later)
                    send[xy ^ idx[1], shard ^ idx[2], :, at] = jnp.where(own_first, later, first)
        for copy in copies[4:]:
            copy.wait()
        for place in range(act_s.shape[0] // ROWS):
            for copy in row_copies(place):
                copy.wait()


def feed_back_kernel(
    idx, vec, h_i, slope_i, dy_i, o0_i, o1_i, mix_i, up_i, down_i,
    dh_o, do_o, gain_o, shift_o, bias_o, keep, send,
    w_mix, w_up, w_down, h_s, slope_s, dy_s, o0, o1, dz_s, a2_s, da_s, dh_s, do_s,
    sems, row_sems, out_sems,
):
    step = pl.program_id(0)
    places = dz_s.shape[0] // ROWS
    half = pl.ds(HALF, HALF)
    moves = (
        (down_i, w_down), (up_i, w_up), (mix_i, w_mix), (o0_i.at[:, half], o0), (o1_i.at[:, half], o1)
    )
    copies = [pltpu.make_async_copy(src, dst, sems.at[i]) for i, (src, dst) in enumerate(moves)]

    def row_copies(place):
        at = pl.ds(pl.multiple_of(place * ROWS, ROWS), ROWS)
        pairs = ((dy_i, dy_s), (slope_i, slope_s), (h_i, h_s))
        return [
            pltpu.make_async_copy(src.at[at], dst.at[at], row_sems.at[place, i])
            for i, (src, dst) in enumerate(pairs)
        ]

    def out_copies(place):
        at = pl.ds(pl.multiple_of(place * ROWS, ROWS), ROWS)
        pairs = ((dh_s, dh_o), (do_s, do_o))
        return [
            pltpu.make_async_copy(src.at[at], dst.at[at], out_sems.at[place, i])
            for i, (src, dst) in enumerate(pairs)
        ]

    @pl.when(step == 0)
    def _():
        copies[0].start()
        for copy in row_copies(0):
            copy.start()
        for copy in copies[1:3]:
            copy.start()
        gain_o[...] = jnp.zeros_like(gain_o)
        shift_o[...] = jnp.zeros_like(shift_o)
        bias_o[...] = jnp.zeros_like(bias_o)
        copies[0].wait()

    for copy in row_copies(step)[:2]:
        copy.wait()
    rows = pl.ds(pl.multiple_of(step * ROWS, ROWS), ROWS)
    gain = vector_of(vec, idx, 2)
    d_out = dy_s[rows, :]
    df = d_out.astype(BF16)
    for j in range(4):
        at = slice(512 * j, 512 * j + 512)
        dz = (nt(df, w_down[at, :]) * slope_s[rows, at].astype(F32)).astype(BF16)
        dz_s[rows, at] = dz
        bias_o[:, at] += jnp.sum(dz.astype(F32), axis=0, keepdims=True)

    @pl.when(step == 0)
    def _():
        for place in range(1, places):
            for copy in row_copies(place):
                copy.start()
        for copy in copies[3:]:
            copy.start()
        for copy in copies[1:3]:
            copy.wait()

    row_copies(step)[2].wait()
    d_second = nt(dz_s[rows, :], w_up[...])
    unit, inverse = norm_parts(h_s[rows, :])
    a2_s[rows, :] = (unit * gain + vector_of(vec, idx, 3)).astype(BF16)
    gain_o[...] += jnp.sum(d_second * unit, axis=0, keepdims=True)
    shift_o[...] += jnp.sum(d_second, axis=0, keepdims=True)
    dh = d_out + norm_pull(d_second, unit, inverse, gain)
    dh_s[rows, :] = dh
    da = dh.astype(BF16)
    da_s[rows, :] = da
    do_s[rows, :] = nt(da, w_mix[...]).astype(BF16)
    for copy in out_copies(step):
        copy.start()

    @pl.when(step == pl.num_programs(0) - 1)
    def _():
        for copy in copies[3:]:
            copy.wait()
        for half in range(2):
            large = tn((o0, o1)[half][...], da_s[...]).astype(BF16)
            for i in range(2):
                tile = large[128 * i : 128 * i + 128]
                put_parts(idx, keep, send, tile, 2 * half + i, slice(0, WIDTH))
        for j in range(4):
            large = tn(a2_s[...], dz_s[:, 512 * j : 512 * j + 512]).astype(BF16)
            at = slice(WIDTH + 512 * j, WIDTH + 512 * j + 512)
            for shard in range(4):
                put_parts(idx, keep, send, large[shard * 128 : shard * 128 + 128], shard, at)
        for place in range(places):
            for copy in out_copies(place):
                copy.wait()


def proj_gradient(idx, both_t, w, dx, keep, send):
    on_gain = jnp.zeros((WIDTH, HALF), F32)
    sums = []
    for j in range(4):
        at = slice(j * HALF, (j + 1) * HALF)
        product = nn(both_t[...], dx[:, at])
        low = product[:WIDTH].astype(BF16)
        for shard in range(4):
            put_parts(idx, keep, send, low[shard * 128 : shard * 128 + 128], shard, at)
        on_gain += product[WIDTH : 2 * WIDTH] * w[:, at].astype(F32)
        sums.append(product[2 * WIDTH : 2 * WIDTH + 8])
    sums = side(*sums)
    high = sums.astype(BF16)
    rest = (sums - high.astype(F32)).astype(BF16)
    shift_rows = nt(jnp.concatenate([high, rest], axis=0), w[...])
    gain_column = jnp.sum(on_gain, axis=1, keepdims=True)
    gain_row = side(gain_column, jnp.zeros((WIDTH, 7), F32)).T[:1]
    return jnp.concatenate([gain_row, shift_rows[:1] + shift_rows[8:9], jnp.zeros((6, WIDTH), F32)])


def late_operands(pairs, sems):
    copies = [pltpu.make_async_copy(src, dst, sems.at[i]) for i, (src, dst) in enumerate(pairs)]

    @pl.when(pl.program_id(0) == 0)
    def _():
        for copy in copies:
            copy.start()

    return copies


def attend_back_kernel(
    idx, both_t, w, proj, floats, ratios, do_i, kept,
    dx_o, keep, send, share_o,
    state, count_z, dx_s, both_s, w_s, sems,
):
    copies = late_operands(((both_t, both_s), (w, w_s)), sems)
    attend_back_step(proj, floats, ratios, do_i, kept, dx_o, state, count_z, dx_s)

    @pl.when(pl.program_id(0) == pl.num_programs(0) - 1)
    def _():
        for copy in copies:
            copy.wait()
        share_o[...] = proj_gradient(idx, both_s, w_s, dx_s, keep, send)


def attend_back_last_kernel(
    idx, both_t, w, proj, floats, ratios, do_i, kept,
    share, g_g2, g_b2, g_bd, g_bu,
    dx_o, keep, send,
    state, count_z, dx_s, both_s, w_s, sems,
):
    copies = late_operands(((both_t, both_s), (w, w_s)), sems)
    attend_back_step(proj, floats, ratios, do_i, kept, dx_o, state, count_z, dx_s)

    @pl.when(pl.program_id(0) == pl.num_programs(0) - 1)
    def _():
        for copy in copies:
            copy.wait()
        total = proj_gradient(idx, both_s, w_s, dx_s, keep, send) + share[...]
        for s in range(4):
            at = slice(128 * s, 128 * s + 128)
            lines = [total[:2, at], g_g2[:, at], g_b2[:, at], g_bd[:, at]]
            lines += [g_bu[:, 512 * s + 128 * j : 512 * s + 128 * j + 128] for j in range(4)]
            lines.append(jnp.zeros((7, 128), F32))
            block = jnp.concatenate(lines, axis=0).astype(BF16)
            for xy in range(4):
                keep[xy, s ^ idx[2], :, COLS_PROJ:] = block
                send[xy, s ^ idx[2], :, COLS_PROJ:] = block


def attend_back_step(proj, floats, ratios, do_i, kept, dx_o, state, count_z, dx_s):
    step = pl.program_id(0)
    chunk = pl.num_programs(0) - 1 - step

    @pl.when(step == 0)
    def _():
        state[...] = jnp.zeros_like(state)
        count_z[...] = jnp.zeros_like(count_z)

    def take(ref, j, rows, pair):
        return ref[rows, j * HALF + 128 * pair : j * HALF + 128 * pair + 128]

    tri, trt, block, ones = causal_pair(), causal_pair(True), same_head(), head_ones()
    places = sub_places(reversed(range(SUBS)))
    d_mixes, wide, d_numers, d_totals, others = {}, {}, {}, {}, {}
    for sub, pair, rows, at in places:
        v = take(proj, 2, rows, pair)
        d_mixes[sub, pair] = masked(tri, nt(do_i[rows, at], stacked(v)))
        wide[sub, pair] = stacked(take(proj, 3, rows, pair))
    for sub, pair, rows, at in places:
        do, ratio = do_i[rows, at], ratios[rows, at]
        q, k, v, e = [take(proj, j, rows, pair) for j in range(4)]
        inv, logits, probs = [take(floats, j, rows, pair) for j in (1, 2, 3)]
        d_ratio = nn(d_mixes[sub, pair], wide[sub, pair])
        d_ratio = (d_ratio + nt(do, kept[sub, pair][:, 128:])) * inv
        weighed = d_ratio * probs
        d_logits = weighed - probs * head_sum(weighed, ones)
        d_numers[sub, pair] = ((HEAD ** -0.5) * d_logits * inv).astype(BF16)
        d_totals[sub, pair] = (-(weighed + d_logits * logits) * inv).astype(BF16)
        wide_q, wide_r, wide_do = stacked(q), stacked(ratio), stacked(do)
        scores = masked(trt, nt(k, wide_q))
        mixing = masked(trt, nt(e, wide_r))
        d_mix_t = masked(trt, nt(v, wide_do))
        others[sub, pair] = (scores, d_mix_t, nn(mixing, wide_do), wide_q, wide_r)
    d_total = jnp.concatenate([side(d_totals[sub, 0], d_totals[sub, 1]) for sub in range(SUBS)], axis=0)
    total_z = nn(causal_whole(True), d_total) + count_z[...]
    count_z[...] = total_z[:1, :]
    currents = [state[0], state[1]]
    lows = {}
    for sub, pair, rows, at in places:
        lows[sub, pair] = currents[pair].astype(BF16)
        more = side(
            tn(ratios[rows, at], do_i[rows, at]), tn(d_numers[sub, pair], take(proj, 0, rows, pair))
        )
        currents[pair] = currents[pair] + jnp.where(block, more, 0.0)
    state[0], state[1] = currents
    for sub, pair, rows, at in places:
        k, v, e = [take(proj, j, rows, pair) for j in (1, 2, 3)]
        scores, d_mix_t, dv, wide_q, wide_r = others[sub, pair]
        d_numer, low = d_numers[sub, pair], lows[sub, pair]
        wide_n = stacked(d_numer)
        d_scores = masked(tri, nt(d_numer, wide[sub, pair]))
        d_scores_t = masked(trt, nt(e, wide_n))
        both = nn(e, low)
        de = nn(side(d_mix_t, scores), jnp.concatenate([wide_r, wide_n], axis=0))
        de = de + nt(side(v, k), low) + total_z[rows, at]
        dq = nn(d_scores, stacked(k)) + nn(d_numer, kept[sub, pair][:, :128])
        dk = nn(d_scores_t, wide_q) + both[:, 128:]
        dv = dv + both[:, :128]
        dc = de * take(floats, 0, rows, pair)
        for j, value in enumerate((dq, dk, dv, dc)):
            dx_o[rows, j * HALF + 128 * pair : j * HALF + 128 * pair + 128] = value.astype(BF16)
    dx_s[pl.ds(pl.multiple_of(chunk * CHUNK, CHUNK), CHUNK), :] = dx_o[...]


def inputs_kernel(idx, vec, x, dh, dx0, dx1, w0, w1, dx_o):
    unit, inverse = norm_parts(x[...].astype(F32))
    d_first = nt(dx0[...], w0[...]) + nt(dx1[...], w1[...])
    dx_o[...] = dh[...] + norm_pull(d_first, unit, inverse, vector_of(vec, idx, 0))


def unpack_proj_kernel(idx, near, far, query, key, value, control, g1, b1, g2, b2, bd, bu):
    for shard, member, piece in each_member(idx, near, far):
        rows = rows_at(member * PIECE, PIECE)
        for j, out in enumerate((query, key, value, control)):
            for half in range(2):
                start = half * COLS_PROJ + j * HALF
                out[rows, half * HALF : (half + 1) * HALF] = piece[:, start : start + HALF].astype(F32)

        @pl.when(member == 0)
        def _():
            lines = piece[:, COLS_BOTH:].astype(F32)
            for i, out in enumerate((g1, b1, g2, b2, bd)):
                out[...] = lines[i]
            for i in range(4):
                bu[128 * i : 128 * i + 128] = lines[5 + i]


def unpack_feed_kernel(idx, near, far, mix, up, down, read):
    for shard, member, piece in each_member(idx, near, far):
        rows = rows_at(member * PIECE, PIECE)
        mix[rows, :] = piece[:, :WIDTH].astype(F32)
        up[rows, :] = piece[:, WIDTH:COLS_UP].astype(F32)
        for i in range(4):
            start = COLS_UP + i * WIDTH
            down[rows_at(member * 64 + 16 * i, PIECE), :] = piece[:, start : start + WIDTH].astype(F32)
        read[rows, :] = piece[:, COLS_UP + 4 * WIDTH :].astype(F32)


def shaped(shape, dtype):
    return jax.ShapeDtypeStruct(shape, dtype)


def call(kernel, name, args, outs, steps=None, scratch=(), flops=0, limit=44):
    grid = (steps,) if steps else ()

    def spec(shape, block):
        if block == "hbm":
            return pl.BlockSpec(memory_space=pl.ANY)
        if block is None:
            return pl.BlockSpec(tuple(shape), lambda *_: (0,) * len(shape))
        return pl.BlockSpec(*block)

    in_specs = []
    for array, block in args:
        if array.dtype == jnp.int32 and array.shape == (3,):
            in_specs.append(pl.BlockSpec(memory_space=pltpu.SMEM))
        else:
            in_specs.append(spec(array.shape, block))
    moved = sum(a.size * a.dtype.itemsize for a, _ in args)
    return pl.pallas_call(
        kernel,
        grid=grid,
        in_specs=in_specs,
        out_specs=[spec(shape, block) for shape, _, block in outs],
        out_shape=[shaped(shape, dtype) for shape, dtype, _ in outs],
        scratch_shapes=list(scratch),
        compiler_params=pltpu.CompilerParams(
            vmem_limit_bytes=limit * MIB,
            dimension_semantics=("arbitrary",) * len(grid) if grid else None,
        ),
        cost_estimate=pl.CostEstimate(flops=1000, bytes_accessed=1000, transcendentals=0),
        name=name,
    )(*[array for array, _ in args])


def swap(value, axis, size, distance):
    return lax.ppermute(value, axis, [(i, i ^ distance) for i in range(size)])


def pin(*values):
    return lax.optimization_barrier(values)


def near_rows(piece, shards):
    return [swap(piece, "shard", shards, k) for k in range(1, 4)]


def near_pair(piece, shards):
    return jnp.stack([piece, swap(piece, "shard", shards, 1)])


def far_pair(pair, shards):
    return swap(pair, "shard", shards, 2)


def sum_of(values):
    values = [v.astype(F32) for v in values]
    return ((values[0] + values[1]) + (values[2] + values[3])).astype(BF16)


def core_sum(keep, got):
    return [(keep[k].astype(F32) + got[k].astype(F32)).astype(BF16) for k in range(4)]


def plane_start(parts, dp):
    return [swap(parts[k], "dp", dp, 2 * k) for k in range(1, 4)]


def plane_sum(parts, got):
    return [sum_of([parts[0][k], got[0][k], got[1][k], got[2][k]]) for k in range(4)]


def plane_halves(parts, got):
    total = [p.astype(F32) for p in [parts[0]] + got]
    total = ((total[0] + total[1]) + (total[2] + total[3])).astype(BF16)
    return total[:2], total[2:]


def half_start(high, shards):
    return swap(high, "shard", shards, 2)


def half_sum(low, got):
    return [(low[k].astype(F32) + got[k].astype(F32)).astype(BF16) for k in range(2)]


def last_start(pair, shards):
    return swap(pair[1], "shard", shards, 1)


def last_sum(pair, got, dp):
    return across_planes((pair[0].astype(F32) + got.astype(F32)).astype(BF16), dp)


def across_planes(total, dp):
    distance = 8
    while distance < dp:
        total = (total.astype(F32) + swap(total, "dp", dp, distance).astype(F32)).astype(BF16)
        distance *= 2
    return total


def shard_start(rows, shards):
    return [swap(rows[k], "shard", shards, k) for k in range(1, 4)]


def shard_sum(rows, got, dp):
    return across_planes(sum_of([rows[0]] + got), dp)


def body(dp, shards):
    def on_device(
        tokens, targets, gain_one, bias_one, w_query, w_key, w_value, w_control, w_mix,
        gain_two, bias_two, w_up, bias_up, w_down, bias_down, w_read,
    ):
        count = tokens.shape[0]
        steps = count // CHUNK
        rows = WIDTH // shards
        member = lax.axis_index("dp") % 8
        idx = jnp.stack([member % 2, member // 2, lax.axis_index("shard")]).astype(jnp.int32)
        forward = lambda i: (i, 0)
        back = lambda i: (steps - 1 - i, 0)
        tok = lambda n: ((CHUNK, n), forward)
        parts = (4, 4, PIECE)

        weights = (w_query, w_key, w_value, w_control, w_mix, w_up, w_down, w_read)
        sizes = [(PIECE, COLS_BOTH + 128), (PIECE, COLS_UP), (2, PIECE, COLS_DOWN)]
        vectors = (gain_one, bias_one, gain_two, bias_two, bias_down, bias_up)
        pa, pu, pd = call(
            pack_kernel,
            "pack_weights",
            [(idx, None)] + [(v, None) for v in vectors] + [(w, "hbm") for w in weights],
            [(size, BF16, None) for size in sizes],
            scratch=[pltpu.SemaphoreType.DMA((20,))],
            limit=56,
        )
        got_a = near_rows(pa, shards)
        pair_u = near_pair(pu, shards)
        rows_a = jnp.stack([pa[:, :COLS_BOTH]] + [g[:, :COLS_BOTH] for g in got_a])
        vec = jnp.stack([pa[:, COLS_BOTH:]] + [g[:, COLS_BOTH:] for g in got_a])
        rows_a, vec, pair_u, pd, tokens_a = pin(rows_a, vec, pair_u, pd, tokens)
        plane_a = [swap(rows_a, "dp", dp, 2 * k) for k in range(1, 4)]
        got_u = far_pair(pair_u, shards)
        pair_d = near_pair(pd, shards)
        a1, both_t = call(
            first_norm_kernel,
            "first_norm",
            [(idx, None), (vec, None), (tokens_a, None)],
            [
                ((count, WIDTH), BF16, None),
                ((2 * WIDTH + PIECE, count), BF16, None),
            ],
        )
        plane_a, got_u, pair_d, a1, both_t = pin(plane_a, got_u, pair_d, a1, both_t)
        near_a = jnp.stack([rows_a] + plane_a)
        far_a = swap(near_a, "dp", dp, 1)
        got_d = far_pair(pair_d, shards)
        got_u, _ = pin(got_u, near_a)
        rows_u = jnp.concatenate([pair_u, got_u])
        plane_u = plane_start([rows_u] * 4, dp)

        kept = ((SUBS, 2, 128, 256), lambda i: (i, 0, 0, 0))

        def attend(a1, half):
            at = ((4, 4, PIECE, COLS_PROJ), lambda i: (0, 0, 0, half))
            return call(
                attend_kernel,
                "attend",
                [(idx, None), (a1, tok(WIDTH)), (near_a, at), (far_a, at)],
                [
                    ((count, COLS_PROJ), BF16, tok(COLS_PROJ)),
                    ((count, COLS_PROJ), F32, tok(COLS_PROJ)),
                    ((count, 2 * HALF), BF16, tok(2 * HALF)),
                    ((SUBS * steps, 2, 128, 256), BF16, kept),
                    ((WIDTH, COLS_PROJ), BF16, None),
                ],
                steps,
                [
                    pltpu.VMEM((2, 128, 256), F32),
                    pltpu.VMEM((1, HALF), F32),
                ],
                flops=6e9,
            )

        first = attend(a1, 0)
        first, plane_u, got_d, a1 = pin(first, plane_u, got_d, a1)
        rows_d = jnp.concatenate([pair_d, got_d])
        plane_d = [swap(rows_d[:, 0], "dp", dp, 2 * k) for k in range(1, 3)]
        near_u = jnp.stack([rows_u] + plane_u)
        far_u = swap(near_u, "dp", dp, 1)
        second = attend(a1, 1)
        second, far_u, plane_d = pin(second, far_u, plane_d)
        near_d = jnp.stack([rows_d[:, 0]] + plane_d + [rows_d[:, 1]])
        far_d = swap(near_d, "dp", dp, 1)
        halves = (first, second)
        o0, o1 = first[2], second[2]

        wide = lambda n: ((ROWS, n), forward)
        mixed_at = ((ROWS, HALF), lambda i: (i, 1))
        places = count // ROWS
        out, h, slope, dy, g_bias_down, keep_d, send_d, full_mix, full_up, full_down = call(
            feed_kernel,
            "feed_forward",
            [
                (idx, None), (vec, None), (tokens, wide(WIDTH)), (o0, mixed_at), (o1, mixed_at),
                (targets, None), (near_u, "hbm"), (far_u, "hbm"), (near_d, "hbm"), (far_d, "hbm"),
            ],
            [
                ((count, WIDTH), BF16, "hbm"),
                ((count, WIDTH), F32, "hbm"),
                ((count, FF), BF16, "hbm"),
                ((count, WIDTH), F32, "hbm"),
                ((1, WIDTH), F32, None),
                (parts + (COLS_DOWN,), BF16, None),
                (parts + (COLS_DOWN,), BF16, None),
                ((WIDTH, WIDTH), BF16, "hbm"),
                ((WIDTH, FF), BF16, "hbm"),
                ((FF, WIDTH), BF16, "hbm"),
            ],
            places,
            [
                pltpu.VMEM(parts + (COLS_UP,), BF16),
                pltpu.VMEM(parts + (COLS_UP,), BF16),
                pltpu.VMEM(parts + (COLS_DOWN,), BF16),
                pltpu.VMEM(parts + (COLS_DOWN,), BF16),
                pltpu.VMEM((WIDTH, WIDTH), BF16),
                pltpu.VMEM((WIDTH, FF), BF16),
                pltpu.VMEM((FF, WIDTH), BF16),
                pltpu.VMEM((WIDTH, VOCAB), BF16),
                pltpu.VMEM((count, FF), BF16),
                pltpu.VMEM((count, WIDTH), BF16),
                pltpu.VMEM((count, WIDTH), F32),
                pltpu.VMEM((count, FF), BF16),
                pltpu.VMEM((count, WIDTH), F32),
                pltpu.VMEM((count, VOCAB), BF16),
                pltpu.VMEM((count, WIDTH), BF16),
                pltpu.SemaphoreType.DMA((7,)),
                pltpu.SemaphoreType.DMA((places, 4)),
            ],
            flops=8e9,
            limit=46,
        )
        got_d = swap(send_d, "dp", dp, 1)

        dh, d_mixed, g_gain_two, g_bias_two, g_bias_up, keep_u, send_u = call(
            feed_back_kernel,
            "feed_backward",
            [(idx, None), (vec, None)]
            + [(t, "hbm") for t in (h, slope, dy, o0, o1, full_mix, full_up, full_down)],
            [
                ((count, WIDTH), F32, "hbm"),
                ((count, WIDTH), BF16, "hbm"),
                ((1, WIDTH), F32, None),
                ((1, WIDTH), F32, None),
                ((1, FF), F32, None),
                (parts + (COLS_UP,), BF16, None),
                (parts + (COLS_UP,), BF16, None),
            ],
            places,
            [
                pltpu.VMEM((WIDTH, WIDTH), BF16),
                pltpu.VMEM((WIDTH, FF), BF16),
                pltpu.VMEM((FF, WIDTH), BF16),
                pltpu.VMEM((count, WIDTH), F32),
                pltpu.VMEM((count, FF), BF16),
                pltpu.VMEM((count, WIDTH), F32),
                pltpu.VMEM((count, HALF), BF16),
                pltpu.VMEM((count, HALF), BF16),
                pltpu.VMEM((count, FF), BF16),
                pltpu.VMEM((count, WIDTH), BF16),
                pltpu.VMEM((count, WIDTH), BF16),
                pltpu.VMEM((count, WIDTH), F32),
                pltpu.VMEM((count, WIDTH), BF16),
                pltpu.SemaphoreType.DMA((5,)),
                pltpu.SemaphoreType.DMA((places, 3)),
                pltpu.SemaphoreType.DMA((places, 2)),
            ],
            flops=8e9,
            limit=46,
        )
        got_d, d_mixed, send_u = pin(got_d, d_mixed, send_u)
        got_u = swap(send_u, "dp", dp, 1)
        sum_d = core_sum(keep_d, got_d)
        sum_d, d_mixed = pin(sum_d, d_mixed)
        got_d = plane_start(sum_d, dp)

        kept_back = ((SUBS, 2, 128, 256), lambda i: (steps - 1 - i, 0, 0, 0))

        def attend_back(half, d_mixed, extra=()):
            proj, floats, mixed, states, w = halves[half]
            wide = ((CHUNK, COLS_PROJ), back)
            column = ((CHUNK, HALF), lambda i: (steps - 1 - i, half))
            last = half == 1
            cols = COLS_LAST if last else COLS_PROJ
            return call(
                attend_back_last_kernel if last else attend_back_kernel,
                "attend_backward",
                [(idx, None), (both_t, "hbm"), (w, "hbm")]
                + [(proj, wide), (floats, wide), (mixed, ((CHUNK, HALF), back))]
                + [(d_mixed, column), (states, kept_back)]
                + [(t, None) for t in extra],
                [
                    ((count, COLS_PROJ), BF16, ((CHUNK, COLS_PROJ), back)),
                    (parts + (cols,), BF16, None),
                    (parts + (cols,), BF16, None),
                ]
                + ([] if last else [((8, WIDTH), F32, None)]),
                steps,
                [
                    pltpu.VMEM((2, 128, 256), F32),
                    pltpu.VMEM((1, HALF), F32),
                    pltpu.VMEM((count, COLS_PROJ), BF16),
                    pltpu.VMEM((2 * WIDTH + PIECE, count), BF16),
                    pltpu.VMEM((WIDTH, COLS_PROJ), BF16),
                    pltpu.SemaphoreType.DMA((2,)),
                ],
                flops=10e9,
            )

        dx0, keep_a, send_a, share = attend_back(0, d_mixed)
        got_d, got_u, send_a, d_mixed = pin(got_d, got_u, send_a, d_mixed)
        got_a = swap(send_a, "dp", dp, 1)
        sum_u = core_sum(keep_u, got_u)
        low_d, high_d = plane_halves(sum_d, got_d)
        sum_u, low_d, high_d, d_mixed = pin(sum_u, low_d, high_d, d_mixed)
        got_u = plane_start(sum_u, dp)
        got_d = half_start(high_d, shards)

        extra = (share, g_gain_two, g_bias_two, g_bias_down, g_bias_up)
        dx1, keep_b, send_b = attend_back(1, d_mixed, extra)
        got_d, got_u, got_a, send_b, dx1 = pin(got_d, got_u, got_a, send_b, dx1)
        got_b = swap(send_b, "dp", dp, 1)
        sum_p = [
            jnp.concatenate(both, axis=-1)
            for both in zip(core_sum(keep_a, got_a), core_sum(keep_b, got_b))
        ]
        sum_p, dx1 = pin(sum_p, dx1)
        got_p = plane_start(sum_p, dp)
        got_u, got_d, _ = pin(got_u, got_d, sum_p)
        low_u, high_u = plane_halves(sum_u, got_u)
        got_u = half_start(high_u, shards)
        pair_d = half_sum(low_d, got_d)
        got_d = last_start(pair_d, shards)
        d_tokens = call(
            inputs_kernel,
            "input_gradient",
            [
                (idx, None), (vec, None), (tokens, tok(WIDTH)), (dh, tok(WIDTH)),
                (dx0, tok(COLS_PROJ)), (dx1, tok(COLS_PROJ)),
                (first[4], None), (second[4], None),
            ],
            [((count, WIDTH), F32, tok(WIDTH))],
            steps,
            flops=3e9,
        )[0]
        got_u, got_d, d_tokens = pin(got_u, got_d, d_tokens)
        pair_u = half_sum(low_u, got_u)
        got_u = last_start(pair_u, shards)
        total_d = last_sum(pair_d, got_d, dp)
        got_p, _, _ = pin(got_p, pair_u, d_tokens)
        total_f = jnp.concatenate([last_sum(pair_u, got_u, dp), total_d], axis=-1)
        along_f = swap(total_f, "dp", dp, 4)
        got_p, _ = pin(got_p, total_f)
        rows_p = plane_sum(sum_p, got_p)
        got_p = shard_start(rows_p, shards)
        along_f, _ = pin(along_f, rows_p)
        pair_f = jnp.stack([total_f, along_f])
        up_f = swap(pair_f, "dp", dp, 2)
        got_p, _ = pin(got_p, pair_f)
        total_p = shard_sum(rows_p, got_p, dp)
        plane_p = plane_start([total_p] * 4, dp)
        up_f, _ = pin(up_f, plane_p[0])
        near_f = jnp.stack([pair_f, up_f], axis=1).reshape((4,) + total_f.shape)
        far_f = swap(near_f, "dp", dp, 1)
        g_mix, g_up, g_down, g_read = call(
            unpack_feed_kernel,
            "unpack_feed",
            [(idx, None), (near_f, None), (far_f, None)],
            [
                ((rows, WIDTH), F32, None),
                ((rows, FF), F32, None),
                ((4 * rows, WIDTH), F32, None),
                ((rows, VOCAB), F32, None),
            ],
        )
        near_p = jnp.stack([total_p] + plane_p)
        far_p = swap(near_p, "dp", dp, 1)
        far_p, g_up = pin(far_p, g_up)
        g_query, g_key, g_value, g_control, g1, b1, g2, b2, bd, bu = call(
            unpack_proj_kernel,
            "unpack_proj",
            [(idx, None), (near_p, None), (far_p, None)],
            [((rows, WIDTH), F32, None)] * 4 + [((128,), F32, None)] * 5 + [((512,), F32, None)],
        )
        return (
            out, d_tokens, g1, b1, g_query, g_key, g_value, g_control, g_mix,
            g2, b2, g_up, bu, g_down, bd, g_read,
        )

    return on_device


def solution(mesh):
    dp, shards = mesh.shape["dp"], mesh.shape["shard"]
    vector, matrix = P("shard"), P("shard", None)
    rows = P(("dp", "shard"), None)
    params = (
        vector, vector, matrix, matrix, matrix, matrix, matrix,
        vector, vector, matrix, vector, matrix, vector, matrix,
    )
    return jax.shard_map(
        body(dp, shards),
        mesh=mesh,
        in_specs=(rows, P(("dp", "shard"))) + params,
        out_specs=(rows, rows) + params,
        check_vma=False,
    )
```

```python
import jax
import jax.numpy as jnp
from jax import lax
from jax.experimental import pallas as pl
from jax.experimental.pallas import tpu as pltpu
from jax.sharding import PartitionSpec as P

EPS = 1e-05
WIDTH = 512
HEAD = 64
FF = 2048
VOCAB = 256
SEQ_LEN = 1024
CHUNK = 256
SUB = 128
SUBS = CHUNK // SUB
ROWS = 512
HALF = 256
PIECE = 16
COLS_PROJ = 4 * HALF
COLS_BOTH = 2 * COLS_PROJ
COLS_LAST = COLS_PROJ + 128
COLS_UP = WIDTH + FF
COLS_DOWN = 4 * WIDTH + VOCAB
F32 = jnp.float32
BF16 = jnp.bfloat16
MIB = 1024 * 1024


def nn(a, b):
    return lax.dot_general(a, b, (((1,), (0,)), ((), ())), preferred_element_type=F32)


def nt(a, b):
    return lax.dot_general(a, b, (((1,), (1,)), ((), ())), preferred_element_type=F32)


def tn(a, b):
    return lax.dot_general(a, b, (((0,), (0,)), ((), ())), preferred_element_type=F32)


def norm_parts(values):
    centre = values - jnp.mean(values, axis=-1, keepdims=True)
    inverse = lax.rsqrt(jnp.mean(centre * centre, axis=-1, keepdims=True) + EPS)
    return centre * inverse, inverse


def norm_pull(grad, unit, inverse, gain):
    scaled = grad * gain
    return inverse * (
        scaled
        - jnp.mean(scaled, axis=-1, keepdims=True)
        - unit * jnp.mean(scaled * unit, axis=-1, keepdims=True)
    )


def vector_of(vec_ref, idx, row):
    return jnp.concatenate(
        [vec_ref[s ^ idx[2], row : row + 1, :].astype(F32) for s in range(4)], axis=1
    )


def bias_up_of(vec_ref, idx):
    return jnp.concatenate(
        [
            vec_ref[s ^ idx[2], row : row + 1, :].astype(F32)
            for s in range(4)
            for row in range(5, 9)
        ],
        axis=1,
    )


def each_piece(idx, near, far):
    for c, buf in ((0, near), (1, far)):
        for xy in range(4):
            member = ((xy ^ idx[1]) * 2) + (c ^ idx[0])
            for s in range(4):
                yield s ^ idx[2], member, buf.at[xy, s]


def each_member(idx, near, far):
    for c, buf in ((0, near), (1, far)):
        for xy in range(4):
            yield None, ((xy ^ idx[1]) * 2) + (c ^ idx[0]), buf.at[xy]


def rows_at(start, size):
    return pl.ds(pl.multiple_of(start, PIECE), size)


def put_parts(idx, keep, send, tile, shard, columns):
    for xy in range(4):
        first = tile[32 * xy : 32 * xy + 16]
        second = tile[32 * xy + 16 : 32 * xy + 32]
        own_first = idx[0] == 0
        keep[xy ^ idx[1], shard ^ idx[2], :, columns] = jnp.where(own_first, first, second)
        send[xy ^ idx[1], shard ^ idx[2], :, columns] = jnp.where(own_first, second, first)


def pack_kernel(
    g1, b1, g2, b2, bd, bu, wq, wk, wv, wc, wm, wu, wd, wr, pa, pc, pd, sems
):
    member = lax.axis_index("dp") % 8
    across = member ^ 6
    rows = rows_at(member * PIECE, PIECE)
    moves = []
    for j, w in enumerate((wq, wk, wv, wc)):
        for half in range(2):
            start = half * COLS_PROJ + j * HALF
            part = w.at[rows, half * HALF : (half + 1) * HALF]
            moves.append((part, pa.at[:, start : start + HALF]))
    moves.append((wm.at[rows, :], pc.at[:, :WIDTH]))
    moves.append((wu.at[rows, :], pc.at[:, WIDTH:]))
    for place, who in enumerate((member, across)):
        for i in range(4):
            part = wd.at[rows_at(who * 64 + 16 * i, PIECE), :]
            moves.append((part, pd.at[place, :, i * WIDTH : (i + 1) * WIDTH]))
        moves.append((wr.at[rows_at(who * PIECE, PIECE), :], pd.at[place, :, 4 * WIDTH :]))
    copies = [pltpu.make_async_copy(src, dst, sems.at[i]) for i, (src, dst) in enumerate(moves)]
    for copy in copies:
        copy.start()
    lines = [v[...].astype(F32).reshape(1, 128) for v in (g1, b1, g2, b2, bd)]
    lines += [bu[128 * j : 128 * j + 128].astype(F32).reshape(1, 128) for j in range(4)]
    lines.append(jnp.zeros((7, 128), F32))
    pa[:, COLS_BOTH:] = jnp.concatenate(lines, axis=0).astype(BF16)
    for copy in copies:
        copy.wait()


def first_norm_kernel(idx, vec, x, a1, both_t):
    unit, _ = norm_parts(x[...].astype(F32))
    low = (unit * vector_of(vec, idx, 0) + vector_of(vec, idx, 1)).astype(BF16)
    a1[...] = low
    both_t[:WIDTH, :] = low.T
    both_t[WIDTH : 2 * WIDTH, :] = unit.astype(BF16).T
    both_t[2 * WIDTH :, :] = jnp.ones((PIECE, both_t.shape[1]), BF16)


def lanes_low():
    return lax.broadcasted_iota(jnp.int32, (1, 128), 1) < HEAD


def stacked(value):
    low = lanes_low().astype(F32).astype(BF16)
    high = (1.0 - lanes_low().astype(F32)).astype(BF16)
    return jnp.concatenate([value * low, value * high], axis=0)


def head_ones():
    row = (lax.broadcasted_iota(jnp.int32, (256, 128), 0) & 127) < HEAD
    col = lax.broadcasted_iota(jnp.int32, (256, 128), 1) < HEAD
    return (row == col).astype(F32).astype(BF16)


def head_sum(value, ones):
    high = value.astype(BF16)
    rest = (value - high.astype(F32)).astype(BF16)
    return nn(side(high, rest), ones)


def sub_places(subs):
    return [
        (sub, pair, slice(SUB * sub, SUB * sub + SUB), slice(128 * pair, 128 * pair + 128))
        for sub in subs
        for pair in range(2)
    ]


def head_max(value):
    low = lanes_low()
    first = jnp.max(jnp.where(low, value, -jnp.inf), axis=-1, keepdims=True)
    second = jnp.max(jnp.where(low, -jnp.inf, value), axis=-1, keepdims=True)
    return jnp.where(low, first, second)


def same_head():
    row = lax.broadcasted_iota(jnp.int32, (128, 256), 0) < HEAD
    col = (lax.broadcasted_iota(jnp.int32, (128, 256), 1) & 127) < HEAD
    return row == col


def causal_pair(transposed=False):
    row = lax.broadcasted_iota(jnp.int32, (SUB, 2 * SUB), 0)
    col = lax.broadcasted_iota(jnp.int32, (SUB, 2 * SUB), 1) & (SUB - 1)
    return (row <= col) if transposed else (col <= row)


def causal_whole(transposed=False):
    row = lax.broadcasted_iota(jnp.int32, (CHUNK, CHUNK), 0)
    col = lax.broadcasted_iota(jnp.int32, (CHUNK, CHUNK), 1)
    keep = (row <= col) if transposed else (col <= row)
    return keep.astype(F32).astype(BF16)


def side(*values):
    return jnp.concatenate(values, axis=1)


def masked(keep, value):
    return jnp.where(keep, value, 0.0).astype(BF16)


def attend_kernel(idx, a1, near, far, proj_o, float_o, mixed_o, kept, w_o, state, count_z):
    step = pl.program_id(0)

    @pl.when(step == 0)
    def _():
        for shard, member, piece in each_piece(idx, near, far):
            w_o[rows_at(shard * 128 + member * PIECE, PIECE), :] = piece[...]
        state[...] = jnp.zeros_like(state)
        count_z[...] = jnp.zeros_like(count_z)

    a = a1[...]
    q_all = nn(a, w_o[:, :HALF]).astype(BF16)
    k_all = nn(a, w_o[:, HALF : 2 * HALF]).astype(BF16)
    expo = jnp.exp(nn(a, w_o[:, 3 * HALF :]))
    e_all = expo.astype(BF16)
    v_all = nn(a, w_o[:, 2 * HALF : 3 * HALF]).astype(BF16)
    for j, value in enumerate((q_all, k_all, v_all, e_all)):
        proj_o[:, j * HALF : (j + 1) * HALF] = value
    float_o[:, :HALF] = expo
    total = nn(causal_whole(), e_all) + count_z[...]
    count_z[...] = total[CHUNK - 1 :, :]
    inverse = 1.0 / total
    float_o[:, HALF : 2 * HALF] = inverse
    tri, block, ones = causal_pair(), same_head(), head_ones()
    places = sub_places(range(SUBS))
    lows, wide_e, numers, ratios = {}, {}, {}, {}
    for pair in range(2):
        current = state[pair]
        for sub in range(SUBS):
            rows, at = slice(SUB * sub, SUB * sub + SUB), slice(128 * pair, 128 * pair + 128)
            lows[sub, pair] = current.astype(BF16)
            kept[sub, pair] = lows[sub, pair]
            wide_e[sub, pair] = stacked(e_all[rows, at])
            more = tn(e_all[rows, at], side(k_all[rows, at], v_all[rows, at]))
            current = current + jnp.where(block, more, 0.0)
        state[pair] = current
    for sub, pair, rows, at in places:
        scores = masked(tri, nt(q_all[rows, at], stacked(k_all[rows, at])))
        numer = nn(scores, wide_e[sub, pair])
        numers[sub, pair] = numer + nt(q_all[rows, at], lows[sub, pair][:, :128])

    def soften(sub, pair, rows, at):
        inv = inverse[rows, at]
        logits = (HEAD ** -0.5) * numers[sub, pair] * inv
        expd = jnp.exp(logits - head_max(logits))
        probs = expd * (1.0 / head_sum(expd, ones))
        ratios[sub, pair] = (probs * inv).astype(BF16)
        float_o[rows, 2 * HALF + 128 * pair : 2 * HALF + 128 * pair + 128] = logits
        float_o[rows, 3 * HALF + 128 * pair : 3 * HALF + 128 * pair + 128] = probs
        mixed_o[rows, at] = ratios[sub, pair]

    def mix(sub, pair, rows, at):
        mixing = masked(tri, nt(ratios[sub, pair], wide_e[sub, pair]))
        out = nn(mixing, stacked(v_all[rows, at])) + nn(ratios[sub, pair], lows[sub, pair][:, 128:])
        mixed_o[rows, HALF + 128 * pair : HALF + 128 * pair + 128] = out.astype(BF16)

    for i, place in enumerate(places):
        soften(*place)
        if i:
            mix(*places[i - 1])
    mix(*places[-1])


def feed_kernel(
    idx, vec, x, o0, o1, target, up_near_i, up_far_i, down_near_i, down_far_i,
    out_o, h_o, slope_o, dy_o, bias_o, keep, send, mix_o, up_o, down_o,
    up_near, up_far, down_near, down_far,
    w_mix, w_up, w_down, w_read, act_s, out_s, h_s, slope_s, dy_s, dl_s, df_s, sems, row_sems,
):
    step = pl.program_id(0)
    moves = (
        (up_near_i, up_near), (up_far_i, up_far), (down_near_i, down_near), (down_far_i, down_far),
        (w_mix, mix_o), (w_up, up_o), (w_down, down_o),
    )
    copies = [pltpu.make_async_copy(src, dst, sems.at[i]) for i, (src, dst) in enumerate(moves)]

    @pl.when(step == 0)
    def _():
        for copy in copies[:4]:
            copy.start()
        for copy in copies[:2]:
            copy.wait()
        for shard, member, piece in each_piece(idx, up_near, up_far):
            rows = rows_at(shard * 128 + member * PIECE, PIECE)
            w_mix[rows, :] = piece[:, :WIDTH]
            w_up[rows, :] = piece[:, WIDTH:]
        for copy in copies[2:4]:
            copy.wait()
        for shard, member, piece in each_piece(idx, down_near, down_far):
            for i in range(4):
                rows = rows_at(shard * 512 + member * 64 + 16 * i, PIECE)
                w_down[rows, :] = piece[:, i * WIDTH : (i + 1) * WIDTH]
            w_read[rows_at(shard * 128 + member * PIECE, PIECE), :] = piece[:, 4 * WIDTH :]
        for copy in copies[4:]:
            copy.start()
        bias_o[...] = jnp.zeros_like(bias_o)

    def row_copies(place):
        at = pl.ds(pl.multiple_of(place * ROWS, ROWS), ROWS)
        pairs = ((out_s, out_o), (h_s, h_o), (slope_s, slope_o), (dy_s, dy_o))
        return [
            pltpu.make_async_copy(src.at[at], dst.at[at], row_sems.at[place, i])
            for i, (src, dst) in enumerate(pairs)
        ]

    rows = pl.ds(pl.multiple_of(step * ROWS, ROWS), ROWS)
    attn = nn(o0[...], w_mix[:HALF, :]) + nn(o1[...], w_mix[HALF:, :])
    resid = x[...].astype(F32) + attn
    h_s[rows, :] = resid
    unit, _ = norm_parts(resid)
    second = (unit * vector_of(vec, idx, 2) + vector_of(vec, idx, 3)).astype(BF16)
    bias = bias_up_of(vec, idx)
    branch = jnp.zeros((ROWS, WIDTH), F32)
    scale = (2.0 / jnp.pi) ** 0.5
    at = [slice(512 * j, 512 * j + 512) for j in range(4)]
    products = nn(second, w_up[:, at[0]])
    for j in range(4):
        z = products + bias[:, at[j]]
        if j < 3:
            products = nn(second, w_up[:, at[j + 1]])
        zz = z * z
        cdf = 0.5 + 0.5 * jnp.tanh(z * (scale + (scale * 0.044715) * zz))
        active = z * cdf
        slope = cdf + (active - active * cdf) * (2 * scale + (6 * scale * 0.044715) * zz)
        slope_s[rows, at[j]] = slope.astype(BF16)
        act = active.astype(BF16)
        act_s[rows, at[j]] = act
        branch += nn(act, w_down[at[j], :])
    out = (resid + (branch + vector_of(vec, idx, 4))).astype(BF16)
    out_s[rows, :] = out
    logits = nn(out, w_read[...])
    expd = jnp.exp(logits - jnp.max(logits, axis=-1, keepdims=True))
    soft = expd / jnp.sum(expd, axis=-1, keepdims=True)
    classes = lax.broadcasted_iota(jnp.int32, (VOCAB, ROWS), 0)
    hits = jnp.where(classes == target[rows].reshape(1, ROWS), 1.0, 0.0).T
    dl = (soft - hits).astype(BF16)
    dl_s[rows, :] = dl
    dy = nt(dl, w_read[...])
    dy_s[rows, :] = dy
    df = dy.astype(BF16)
    df_s[rows, :] = df
    bias_o[...] += jnp.sum(df.astype(F32), axis=0, keepdims=True)
    for copy in row_copies(step):
        copy.start()

    @pl.when(step == pl.num_programs(0) - 1)
    def _():
        whole = tn(out_s[...], dl_s[...]).astype(BF16)
        for shard in range(4):
            tile = whole[shard * 128 : shard * 128 + 128]
            put_parts(idx, keep, send, tile, shard, slice(4 * WIDTH, None))
            large = tn(act_s[:, shard * 512 : shard * 512 + 512], df_s[...]).astype(BF16)
            for xy in range(4):
                tile = large[xy * 128 : xy * 128 + 128]
                own_first = idx[0] == 0
                for i in range(4):
                    first = tile[16 * i : 16 * i + 16]
                    later = tile[64 + 16 * i : 64 + 16 * i + 16]
                    at = slice(i * WIDTH, (i + 1) * WIDTH)
                    keep[xy ^ idx[1], shard ^ idx[2], :, at] = jnp.where(own_first, first, later)
                    send[xy ^ idx[1], shard ^ idx[2], :, at] = jnp.where(own_first, later, first)
        for copy in copies[4:]:
            copy.wait()
        for place in range(act_s.shape[0] // ROWS):
            for copy in row_copies(place):
                copy.wait()


def feed_back_kernel(
    idx, vec, h_i, slope_i, dy_i, o0_i, o1_i, mix_i, up_i, down_i,
    dh_o, do_o, gain_o, shift_o, bias_o, keep, send,
    w_mix, w_up, w_down, h_s, slope_s, dy_s, o0, o1, dz_s, a2_s, da_s, dh_s, do_s,
    sems, row_sems, out_sems,
):
    step = pl.program_id(0)
    places = dz_s.shape[0] // ROWS
    half = pl.ds(HALF, HALF)
    moves = (
        (down_i, w_down), (up_i, w_up), (mix_i, w_mix), (o0_i.at[:, half], o0), (o1_i.at[:, half], o1)
    )
    copies = [pltpu.make_async_copy(src, dst, sems.at[i]) for i, (src, dst) in enumerate(moves)]

    def row_copies(place):
        at = pl.ds(pl.multiple_of(place * ROWS, ROWS), ROWS)
        pairs = ((dy_i, dy_s), (slope_i, slope_s), (h_i, h_s))
        return [
            pltpu.make_async_copy(src.at[at], dst.at[at], row_sems.at[place, i])
            for i, (src, dst) in enumerate(pairs)
        ]

    def out_copies(place):
        at = pl.ds(pl.multiple_of(place * ROWS, ROWS), ROWS)
        pairs = ((dh_s, dh_o), (do_s, do_o))
        return [
            pltpu.make_async_copy(src.at[at], dst.at[at], out_sems.at[place, i])
            for i, (src, dst) in enumerate(pairs)
        ]

    @pl.when(step == 0)
    def _():
        copies[0].start()
        for copy in row_copies(0):
            copy.start()
        for copy in copies[1:3]:
            copy.start()
        gain_o[...] = jnp.zeros_like(gain_o)
        shift_o[...] = jnp.zeros_like(shift_o)
        bias_o[...] = jnp.zeros_like(bias_o)
        copies[0].wait()

    for copy in row_copies(step)[:2]:
        copy.wait()
    rows = pl.ds(pl.multiple_of(step * ROWS, ROWS), ROWS)
    gain = vector_of(vec, idx, 2)
    d_out = dy_s[rows, :]
    df = d_out.astype(BF16)
    for j in range(4):
        at = slice(512 * j, 512 * j + 512)
        dz = (nt(df, w_down[at, :]) * slope_s[rows, at].astype(F32)).astype(BF16)
        dz_s[rows, at] = dz
        bias_o[:, at] += jnp.sum(dz.astype(F32), axis=0, keepdims=True)

    @pl.when(step == 0)
    def _():
        for place in range(1, places):
            for copy in row_copies(place):
                copy.start()
        for copy in copies[3:]:
            copy.start()
        for copy in copies[1:3]:
            copy.wait()

    row_copies(step)[2].wait()
    d_second = nt(dz_s[rows, :], w_up[...])
    unit, inverse = norm_parts(h_s[rows, :])
    a2_s[rows, :] = (unit * gain + vector_of(vec, idx, 3)).astype(BF16)
    gain_o[...] += jnp.sum(d_second * unit, axis=0, keepdims=True)
    shift_o[...] += jnp.sum(d_second, axis=0, keepdims=True)
    dh = d_out + norm_pull(d_second, unit, inverse, gain)
    dh_s[rows, :] = dh
    da = dh.astype(BF16)
    da_s[rows, :] = da
    do_s[rows, :] = nt(da, w_mix[...]).astype(BF16)
    for copy in out_copies(step):
        copy.start()

    @pl.when(step == pl.num_programs(0) - 1)
    def _():
        for copy in copies[3:]:
            copy.wait()
        for half in range(2):
            large = tn((o0, o1)[half][...], da_s[...]).astype(BF16)
            for i in range(2):
                tile = large[128 * i : 128 * i + 128]
                put_parts(idx, keep, send, tile, 2 * half + i, slice(0, WIDTH))
        for j in range(4):
            large = tn(a2_s[...], dz_s[:, 512 * j : 512 * j + 512]).astype(BF16)
            at = slice(WIDTH + 512 * j, WIDTH + 512 * j + 512)
            for shard in range(4):
                put_parts(idx, keep, send, large[shard * 128 : shard * 128 + 128], shard, at)
        for place in range(places):
            for copy in out_copies(place):
                copy.wait()


def proj_gradient(idx, both_t, w, dx, keep, send):
    on_gain = jnp.zeros((WIDTH, HALF), F32)
    sums = []
    for j in range(4):
        at = slice(j * HALF, (j + 1) * HALF)
        product = nn(both_t[...], dx[:, at])
        low = product[:WIDTH].astype(BF16)
        for shard in range(4):
            put_parts(idx, keep, send, low[shard * 128 : shard * 128 + 128], shard, at)
        on_gain += product[WIDTH : 2 * WIDTH] * w[:, at].astype(F32)
        sums.append(product[2 * WIDTH : 2 * WIDTH + 8])
    sums = side(*sums)
    high = sums.astype(BF16)
    rest = (sums - high.astype(F32)).astype(BF16)
    shift_rows = nt(jnp.concatenate([high, rest], axis=0), w[...])
    gain_column = jnp.sum(on_gain, axis=1, keepdims=True)
    gain_row = side(gain_column, jnp.zeros((WIDTH, 7), F32)).T[:1]
    return jnp.concatenate([gain_row, shift_rows[:1] + shift_rows[8:9], jnp.zeros((6, WIDTH), F32)])


def late_operands(pairs, sems):
    copies = [pltpu.make_async_copy(src, dst, sems.at[i]) for i, (src, dst) in enumerate(pairs)]

    @pl.when(pl.program_id(0) == 0)
    def _():
        for copy in copies:
            copy.start()

    return copies


def attend_back_kernel(
    idx, both_t, w, proj, floats, ratios, do_i, kept,
    dx_o, keep, send, share_o,
    state, count_z, dx_s, both_s, w_s, sems,
):
    copies = late_operands(((both_t, both_s), (w, w_s)), sems)
    attend_back_step(proj, floats, ratios, do_i, kept, dx_o, state, count_z, dx_s)

    @pl.when(pl.program_id(0) == pl.num_programs(0) - 1)
    def _():
        for copy in copies:
            copy.wait()
        share_o[...] = proj_gradient(idx, both_s, w_s, dx_s, keep, send)


def attend_back_last_kernel(
    idx, both_t, w, proj, floats, ratios, do_i, kept,
    share, g_g2, g_b2, g_bd, g_bu,
    dx_o, keep, send,
    state, count_z, dx_s, both_s, w_s, sems,
):
    copies = late_operands(((both_t, both_s), (w, w_s)), sems)
    attend_back_step(proj, floats, ratios, do_i, kept, dx_o, state, count_z, dx_s)

    @pl.when(pl.program_id(0) == pl.num_programs(0) - 1)
    def _():
        for copy in copies:
            copy.wait()
        total = proj_gradient(idx, both_s, w_s, dx_s, keep, send) + share[...]
        for s in range(4):
            at = slice(128 * s, 128 * s + 128)
            lines = [total[:2, at], g_g2[:, at], g_b2[:, at], g_bd[:, at]]
            lines += [g_bu[:, 512 * s + 128 * j : 512 * s + 128 * j + 128] for j in range(4)]
            lines.append(jnp.zeros((7, 128), F32))
            block = jnp.concatenate(lines, axis=0).astype(BF16)
            for xy in range(4):
                keep[xy, s ^ idx[2], :, COLS_PROJ:] = block
                send[xy, s ^ idx[2], :, COLS_PROJ:] = block


def attend_back_step(proj, floats, ratios, do_i, kept, dx_o, state, count_z, dx_s):
    step = pl.program_id(0)
    chunk = pl.num_programs(0) - 1 - step

    @pl.when(step == 0)
    def _():
        state[...] = jnp.zeros_like(state)
        count_z[...] = jnp.zeros_like(count_z)

    def take(ref, j, rows, pair):
        return ref[rows, j * HALF + 128 * pair : j * HALF + 128 * pair + 128]

    tri, trt, block, ones = causal_pair(), causal_pair(True), same_head(), head_ones()
    places = sub_places(reversed(range(SUBS)))
    d_mixes, wide, d_numers, d_totals, others = {}, {}, {}, {}, {}
    for sub, pair, rows, at in places:
        v = take(proj, 2, rows, pair)
        d_mixes[sub, pair] = masked(tri, nt(do_i[rows, at], stacked(v)))
        wide[sub, pair] = stacked(take(proj, 3, rows, pair))
    for sub, pair, rows, at in places:
        do, ratio = do_i[rows, at], ratios[rows, at]
        q, k, v, e = [take(proj, j, rows, pair) for j in range(4)]
        inv, logits, probs = [take(floats, j, rows, pair) for j in (1, 2, 3)]
        d_ratio = nn(d_mixes[sub, pair], wide[sub, pair])
        d_ratio = (d_ratio + nt(do, kept[sub, pair][:, 128:])) * inv
        weighed = d_ratio * probs
        d_logits = weighed - probs * head_sum(weighed, ones)
        d_numers[sub, pair] = ((HEAD ** -0.5) * d_logits * inv).astype(BF16)
        d_totals[sub, pair] = (-(weighed + d_logits * logits) * inv).astype(BF16)
        wide_q, wide_r, wide_do = stacked(q), stacked(ratio), stacked(do)
        scores = masked(trt, nt(k, wide_q))
        mixing = masked(trt, nt(e, wide_r))
        d_mix_t = masked(trt, nt(v, wide_do))
        others[sub, pair] = (scores, d_mix_t, nn(mixing, wide_do), wide_q, wide_r)
    d_total = jnp.concatenate([side(d_totals[sub, 0], d_totals[sub, 1]) for sub in range(SUBS)], axis=0)
    total_z = nn(causal_whole(True), d_total) + count_z[...]
    count_z[...] = total_z[:1, :]
    currents = [state[0], state[1]]
    lows = {}
    for sub, pair, rows, at in places:
        lows[sub, pair] = currents[pair].astype(BF16)
        more = side(
            tn(ratios[rows, at], do_i[rows, at]), tn(d_numers[sub, pair], take(proj, 0, rows, pair))
        )
        currents[pair] = currents[pair] + jnp.where(block, more, 0.0)
    state[0], state[1] = currents
    for sub, pair, rows, at in places:
        k, v, e = [take(proj, j, rows, pair) for j in (1, 2, 3)]
        scores, d_mix_t, dv, wide_q, wide_r = others[sub, pair]
        d_numer, low = d_numers[sub, pair], lows[sub, pair]
        wide_n = stacked(d_numer)
        d_scores = masked(tri, nt(d_numer, wide[sub, pair]))
        d_scores_t = masked(trt, nt(e, wide_n))
        both = nn(e, low)
        de = nn(side(d_mix_t, scores), jnp.concatenate([wide_r, wide_n], axis=0))
        de = de + nt(side(v, k), low) + total_z[rows, at]
        dq = nn(d_scores, stacked(k)) + nn(d_numer, kept[sub, pair][:, :128])
        dk = nn(d_scores_t, wide_q) + both[:, 128:]
        dv = dv + both[:, :128]
        dc = de * take(floats, 0, rows, pair)
        for j, value in enumerate((dq, dk, dv, dc)):
            dx_o[rows, j * HALF + 128 * pair : j * HALF + 128 * pair + 128] = value.astype(BF16)
    dx_s[pl.ds(pl.multiple_of(chunk * CHUNK, CHUNK), CHUNK), :] = dx_o[...]


def inputs_kernel(idx, vec, x, dh, dx0, dx1, w0, w1, dx_o):
    unit, inverse = norm_parts(x[...].astype(F32))
    d_first = nt(dx0[...], w0[...]) + nt(dx1[...], w1[...])
    dx_o[...] = dh[...] + norm_pull(d_first, unit, inverse, vector_of(vec, idx, 0))


def unpack_proj_kernel(idx, near, far, query, key, value, control, g1, b1, g2, b2, bd, bu):
    for shard, member, piece in each_member(idx, near, far):
        rows = rows_at(member * PIECE, PIECE)
        for j, out in enumerate((query, key, value, control)):
            for half in range(2):
                start = half * COLS_PROJ + j * HALF
                out[rows, half * HALF : (half + 1) * HALF] = piece[:, start : start + HALF].astype(F32)

        @pl.when(member == 0)
        def _():
            lines = piece[:, COLS_BOTH:].astype(F32)
            for i, out in enumerate((g1, b1, g2, b2, bd)):
                out[...] = lines[i]
            for i in range(4):
                bu[128 * i : 128 * i + 128] = lines[5 + i]


def unpack_feed_kernel(idx, near, far, mix, up, down, read):
    for shard, member, piece in each_member(idx, near, far):
        rows = rows_at(member * PIECE, PIECE)
        mix[rows, :] = piece[:, :WIDTH].astype(F32)
        up[rows, :] = piece[:, WIDTH:COLS_UP].astype(F32)
        for i in range(4):
            start = COLS_UP + i * WIDTH
            down[rows_at(member * 64 + 16 * i, PIECE), :] = piece[:, start : start + WIDTH].astype(F32)
        read[rows, :] = piece[:, COLS_UP + 4 * WIDTH :].astype(F32)


def shaped(shape, dtype):
    return jax.ShapeDtypeStruct(shape, dtype)


def call(kernel, name, args, outs, steps=None, scratch=(), flops=0, limit=44):
    grid = (steps,) if steps else ()

    def spec(shape, block):
        if block == "hbm":
            return pl.BlockSpec(memory_space=pl.ANY)
        if block is None:
            return pl.BlockSpec(tuple(shape), lambda *_: (0,) * len(shape))
        return pl.BlockSpec(*block)

    in_specs = []
    for array, block in args:
        if array.dtype == jnp.int32 and array.shape == (3,):
            in_specs.append(pl.BlockSpec(memory_space=pltpu.SMEM))
        else:
            in_specs.append(spec(array.shape, block))
    moved = sum(a.size * a.dtype.itemsize for a, _ in args)
    return pl.pallas_call(
        kernel,
        grid=grid,
        in_specs=in_specs,
        out_specs=[spec(shape, block) for shape, _, block in outs],
        out_shape=[shaped(shape, dtype) for shape, dtype, _ in outs],
        scratch_shapes=list(scratch),
        compiler_params=pltpu.CompilerParams(
            vmem_limit_bytes=limit * MIB,
            dimension_semantics=("arbitrary",) * len(grid) if grid else None,
        ),
        cost_estimate=pl.CostEstimate(flops=1000, bytes_accessed=1000, transcendentals=0),
        name=name,
    )(*[array for array, _ in args])


def swap(value, axis, size, distance):
    return lax.ppermute(value, axis, [(i, i ^ distance) for i in range(size)])


def pin(*values):
    return lax.optimization_barrier(values)


def near_rows(piece, shards):
    return [swap(piece, "shard", shards, k) for k in range(1, 4)]


def near_pair(piece, shards):
    return jnp.stack([piece, swap(piece, "shard", shards, 1)])


def far_pair(pair, shards):
    return swap(pair, "shard", shards, 2)


def sum_of(values):
    values = [v.astype(F32) for v in values]
    return ((values[0] + values[1]) + (values[2] + values[3])).astype(BF16)


def core_sum(keep, got):
    return [(keep[k].astype(F32) + got[k].astype(F32)).astype(BF16) for k in range(4)]


def plane_start(parts, dp):
    return [swap(parts[k], "dp", dp, 2 * k) for k in range(1, 4)]


def plane_sum(parts, got):
    return [sum_of([parts[0][k], got[0][k], got[1][k], got[2][k]]) for k in range(4)]


def plane_halves(parts, got):
    total = [p.astype(F32) for p in [parts[0]] + got]
    total = ((total[0] + total[1]) + (total[2] + total[3])).astype(BF16)
    return total[:2], total[2:]


def half_start(high, shards):
    return swap(high, "shard", shards, 2)


def half_sum(low, got):
    return [(low[k].astype(F32) + got[k].astype(F32)).astype(BF16) for k in range(2)]


def last_start(pair, shards):
    return swap(pair[1], "shard", shards, 1)


def last_sum(pair, got, dp):
    return across_planes((pair[0].astype(F32) + got.astype(F32)).astype(BF16), dp)


def across_planes(total, dp):
    distance = 8
    while distance < dp:
        total = (total.astype(F32) + swap(total, "dp", dp, distance).astype(F32)).astype(BF16)
        distance *= 2
    return total


def shard_start(rows, shards):
    return [swap(rows[k], "shard", shards, k) for k in range(1, 4)]


def shard_sum(rows, got, dp):
    return across_planes(sum_of([rows[0]] + got), dp)


def body(dp, shards):
    def on_device(
        tokens, targets, gain_one, bias_one, w_query, w_key, w_value, w_control, w_mix,
        gain_two, bias_two, w_up, bias_up, w_down, bias_down, w_read,
    ):
        count = tokens.shape[0]
        steps = count // CHUNK
        rows = WIDTH // shards
        member = lax.axis_index("dp") % 8
        idx = jnp.stack([member % 2, member // 2, lax.axis_index("shard")]).astype(jnp.int32)
        forward = lambda i: (i, 0)
        back = lambda i: (steps - 1 - i, 0)
        tok = lambda n: ((CHUNK, n), forward)
        parts = (4, 4, PIECE)

        weights = (w_query, w_key, w_value, w_control, w_mix, w_up, w_down, w_read)
        sizes = [(PIECE, COLS_BOTH + 128), (PIECE, COLS_UP), (2, PIECE, COLS_DOWN)]
        vectors = (gain_one, bias_one, gain_two, bias_two, bias_down, bias_up)
        pa, pu, pd = call(
            pack_kernel,
            "pack_weights",
            [(v, None) for v in vectors] + [(w, "hbm") for w in weights],
            [(size, BF16, None) for size in sizes],
            scratch=[pltpu.SemaphoreType.DMA((20,))],
            limit=56,
        )
        got_a = near_rows(pa, shards)
        pair_u = near_pair(pu, shards)
        rows_a = jnp.stack([pa[:, :COLS_BOTH]] + [g[:, :COLS_BOTH] for g in got_a])
        vec = jnp.stack([pa[:, COLS_BOTH:]] + [g[:, COLS_BOTH:] for g in got_a])
        rows_a, vec, pd, tokens_a = pin(rows_a, vec, pd, tokens)
        plane_a = [swap(rows_a, "dp", dp, 2 * k) for k in range(1, 4)]
        got_u = far_pair(pair_u, shards)
        pair_d = near_pair(pd, shards)
        a1, both_t = call(
            first_norm_kernel,
            "first_norm",
            [(idx, None), (vec, None), (tokens_a, None)],
            [
                ((count, WIDTH), BF16, None),
                ((2 * WIDTH + PIECE, count), BF16, None),
            ],
        )
        plane_a, got_u, a1, both_t = pin(plane_a, got_u, a1, both_t)
        near_a = jnp.stack([rows_a] + plane_a)
        far_a = swap(near_a, "dp", dp, 1)
        pair_d, _ = pin(pair_d, near_a)
        got_d = far_pair(pair_d, shards)
        got_u, _ = pin(got_u, near_a)
        rows_u = jnp.concatenate([pair_u, got_u])
        plane_u = plane_start([rows_u] * 4, dp)

        kept = ((SUBS, 2, 128, 256), lambda i: (i, 0, 0, 0))

        def attend(a1, half):
            at = ((4, 4, PIECE, COLS_PROJ), lambda i: (0, 0, 0, half))
            return call(
                attend_kernel,
                "attend",
                [(idx, None), (a1, tok(WIDTH)), (near_a, at), (far_a, at)],
                [
                    ((count, COLS_PROJ), BF16, tok(COLS_PROJ)),
                    ((count, COLS_PROJ), F32, tok(COLS_PROJ)),
                    ((count, 2 * HALF), BF16, tok(2 * HALF)),
                    ((SUBS * steps, 2, 128, 256), BF16, kept),
                    ((WIDTH, COLS_PROJ), BF16, None),
                ],
                steps,
                [
                    pltpu.VMEM((2, 128, 256), F32),
                    pltpu.VMEM((1, HALF), F32),
                ],
                flops=6e9,
            )

        first = attend(a1, 0)
        first, plane_u, got_d, a1 = pin(first, plane_u, got_d, a1)
        rows_d = jnp.concatenate([pair_d, got_d])
        plane_d = [swap(rows_d[:, 0], "dp", dp, 2 * k) for k in range(1, 3)]
        near_u = jnp.stack([rows_u] + plane_u)
        far_u = swap(near_u, "dp", dp, 1)
        second = attend(a1, 1)
        second, far_u, plane_d = pin(second, far_u, plane_d)
        near_d = jnp.stack([rows_d[:, 0]] + plane_d + [rows_d[:, 1]])
        far_d = swap(near_d, "dp", dp, 1)
        halves = (first, second)
        o0, o1 = first[2], second[2]

        wide = lambda n: ((ROWS, n), forward)
        mixed_at = ((ROWS, HALF), lambda i: (i, 1))
        places = count // ROWS
        out, h, slope, dy, g_bias_down, keep_d, send_d, full_mix, full_up, full_down = call(
            feed_kernel,
            "feed_forward",
            [
                (idx, None), (vec, None), (tokens, wide(WIDTH)), (o0, mixed_at), (o1, mixed_at),
                (targets, None), (near_u, "hbm"), (far_u, "hbm"), (near_d, "hbm"), (far_d, "hbm"),
            ],
            [
                ((count, WIDTH), BF16, "hbm"),
                ((count, WIDTH), F32, "hbm"),
                ((count, FF), BF16, "hbm"),
                ((count, WIDTH), F32, "hbm"),
                ((1, WIDTH), F32, None),
                (parts + (COLS_DOWN,), BF16, None),
                (parts + (COLS_DOWN,), BF16, None),
                ((WIDTH, WIDTH), BF16, "hbm"),
                ((WIDTH, FF), BF16, "hbm"),
                ((FF, WIDTH), BF16, "hbm"),
            ],
            places,
            [
                pltpu.VMEM(parts + (COLS_UP,), BF16),
                pltpu.VMEM(parts + (COLS_UP,), BF16),
                pltpu.VMEM(parts + (COLS_DOWN,), BF16),
                pltpu.VMEM(parts + (COLS_DOWN,), BF16),
                pltpu.VMEM((WIDTH, WIDTH), BF16),
                pltpu.VMEM((WIDTH, FF), BF16),
                pltpu.VMEM((FF, WIDTH), BF16),
                pltpu.VMEM((WIDTH, VOCAB), BF16),
                pltpu.VMEM((count, FF), BF16),
                pltpu.VMEM((count, WIDTH), BF16),
                pltpu.VMEM((count, WIDTH), F32),
                pltpu.VMEM((count, FF), BF16),
                pltpu.VMEM((count, WIDTH), F32),
                pltpu.VMEM((count, VOCAB), BF16),
                pltpu.VMEM((count, WIDTH), BF16),
                pltpu.SemaphoreType.DMA((7,)),
                pltpu.SemaphoreType.DMA((places, 4)),
            ],
            flops=8e9,
            limit=46,
        )
        got_d = swap(send_d, "dp", dp, 1)

        dh, d_mixed, g_gain_two, g_bias_two, g_bias_up, keep_u, send_u = call(
            feed_back_kernel,
            "feed_backward",
            [(idx, None), (vec, None)]
            + [(t, "hbm") for t in (h, slope, dy, o0, o1, full_mix, full_up, full_down)],
            [
                ((count, WIDTH), F32, "hbm"),
                ((count, WIDTH), BF16, "hbm"),
                ((1, WIDTH), F32, None),
                ((1, WIDTH), F32, None),
                ((1, FF), F32, None),
                (parts + (COLS_UP,), BF16, None),
                (parts + (COLS_UP,), BF16, None),
            ],
            places,
            [
                pltpu.VMEM((WIDTH, WIDTH), BF16),
                pltpu.VMEM((WIDTH, FF), BF16),
                pltpu.VMEM((FF, WIDTH), BF16),
                pltpu.VMEM((count, WIDTH), F32),
                pltpu.VMEM((count, FF), BF16),
                pltpu.VMEM((count, WIDTH), F32),
                pltpu.VMEM((count, HALF), BF16),
                pltpu.VMEM((count, HALF), BF16),
                pltpu.VMEM((count, FF), BF16),
                pltpu.VMEM((count, WIDTH), BF16),
                pltpu.VMEM((count, WIDTH), BF16),
                pltpu.VMEM((count, WIDTH), F32),
                pltpu.VMEM((count, WIDTH), BF16),
                pltpu.SemaphoreType.DMA((5,)),
                pltpu.SemaphoreType.DMA((places, 3)),
                pltpu.SemaphoreType.DMA((places, 2)),
            ],
            flops=8e9,
            limit=46,
        )
        got_d, d_mixed, send_u = pin(got_d, d_mixed, send_u)
        got_u = swap(send_u, "dp", dp, 1)
        sum_d = core_sum(keep_d, got_d)
        sum_d, d_mixed = pin(sum_d, d_mixed)
        got_d = plane_start(sum_d, dp)

        kept_back = ((SUBS, 2, 128, 256), lambda i: (steps - 1 - i, 0, 0, 0))

        def attend_back(half, d_mixed, extra=()):
            proj, floats, mixed, states, w = halves[half]
            wide = ((CHUNK, COLS_PROJ), back)
            column = ((CHUNK, HALF), lambda i: (steps - 1 - i, half))
            last = half == 1
            cols = COLS_LAST if last else COLS_PROJ
            return call(
                attend_back_last_kernel if last else attend_back_kernel,
                "attend_backward",
                [(idx, None), (both_t, "hbm"), (w, "hbm")]
                + [(proj, wide), (floats, wide), (mixed, ((CHUNK, HALF), back))]
                + [(d_mixed, column), (states, kept_back)]
                + [(t, None) for t in extra],
                [
                    ((count, COLS_PROJ), BF16, ((CHUNK, COLS_PROJ), back)),
                    (parts + (cols,), BF16, None),
                    (parts + (cols,), BF16, None),
                ]
                + ([] if last else [((8, WIDTH), F32, None)]),
                steps,
                [
                    pltpu.VMEM((2, 128, 256), F32),
                    pltpu.VMEM((1, HALF), F32),
                    pltpu.VMEM((count, COLS_PROJ), BF16),
                    pltpu.VMEM((2 * WIDTH + PIECE, count), BF16),
                    pltpu.VMEM((WIDTH, COLS_PROJ), BF16),
                    pltpu.SemaphoreType.DMA((2,)),
                ],
                flops=10e9,
            )

        dx0, keep_a, send_a, share = attend_back(0, d_mixed)
        got_d, got_u, send_a, d_mixed = pin(got_d, got_u, send_a, d_mixed)
        got_a = swap(send_a, "dp", dp, 1)
        sum_u = core_sum(keep_u, got_u)
        low_d, high_d = plane_halves(sum_d, got_d)
        sum_u, low_d, high_d, d_mixed = pin(sum_u, low_d, high_d, d_mixed)
        got_u = plane_start(sum_u, dp)
        got_d = half_start(high_d, shards)

        extra = (share, g_gain_two, g_bias_two, g_bias_down, g_bias_up)
        dx1, keep_b, send_b = attend_back(1, d_mixed, extra)
        got_d, got_u, got_a, send_b, dx1 = pin(got_d, got_u, got_a, send_b, dx1)
        got_b = swap(send_b, "dp", dp, 1)
        sum_p = [
            jnp.concatenate(both, axis=-1)
            for both in zip(core_sum(keep_a, got_a), core_sum(keep_b, got_b))
        ]
        sum_p, dx1 = pin(sum_p, dx1)
        got_p = plane_start(sum_p, dp)
        got_u, got_d, _ = pin(got_u, got_d, sum_p)
        low_u, high_u = plane_halves(sum_u, got_u)
        got_u = half_start(high_u, shards)
        pair_d = half_sum(low_d, got_d)
        got_d = last_start(pair_d, shards)
        d_tokens = call(
            inputs_kernel,
            "input_gradient",
            [
                (idx, None), (vec, None), (tokens, tok(WIDTH)), (dh, tok(WIDTH)),
                (dx0, tok(COLS_PROJ)), (dx1, tok(COLS_PROJ)),
                (first[4], None), (second[4], None),
            ],
            [((count, WIDTH), F32, tok(WIDTH))],
            steps,
            flops=3e9,
        )[0]
        got_u, got_d, d_tokens = pin(got_u, got_d, d_tokens)
        pair_u = half_sum(low_u, got_u)
        got_u = last_start(pair_u, shards)
        total_d = last_sum(pair_d, got_d, dp)
        got_p, _, _ = pin(got_p, pair_u, d_tokens)
        total_f = jnp.concatenate([last_sum(pair_u, got_u, dp), total_d], axis=-1)
        along_f = swap(total_f, "dp", dp, 4)
        got_p, _ = pin(got_p, total_f)
        rows_p = plane_sum(sum_p, got_p)
        got_p = shard_start(rows_p, shards)
        along_f, _ = pin(along_f, rows_p)
        pair_f = jnp.stack([total_f, along_f])
        up_f = swap(pair_f, "dp", dp, 2)
        got_p, _ = pin(got_p, pair_f)
        total_p = shard_sum(rows_p, got_p, dp)
        plane_p = plane_start([total_p] * 4, dp)
        up_f, _ = pin(up_f, plane_p[0])
        near_f = jnp.stack([pair_f, up_f], axis=1).reshape((4,) + total_f.shape)
        far_f = swap(near_f, "dp", dp, 1)
        g_mix, g_up, g_down, g_read = call(
            unpack_feed_kernel,
            "unpack_feed",
            [(idx, None), (near_f, None), (far_f, None)],
            [
                ((rows, WIDTH), F32, None),
                ((rows, FF), F32, None),
                ((4 * rows, WIDTH), F32, None),
                ((rows, VOCAB), F32, None),
            ],
        )
        near_p = jnp.stack([total_p] + plane_p)
        far_p = swap(near_p, "dp", dp, 1)
        far_p, g_up = pin(far_p, g_up)
        g_query, g_key, g_value, g_control, g1, b1, g2, b2, bd, bu = call(
            unpack_proj_kernel,
            "unpack_proj",
            [(idx, None), (near_p, None), (far_p, None)],
            [((rows, WIDTH), F32, None)] * 4 + [((128,), F32, None)] * 5 + [((512,), F32, None)],
        )
        return (
            out, d_tokens, g1, b1, g_query, g_key, g_value, g_control, g_mix,
            g2, b2, g_up, bu, g_down, bd, g_read,
        )

    return on_device


def solution(mesh):
    dp, shards = mesh.shape["dp"], mesh.shape["shard"]
    vector, matrix = P("shard"), P("shard", None)
    rows = P(("dp", "shard"), None)
    params = (
        vector, vector, matrix, matrix, matrix, matrix, matrix,
        vector, vector, matrix, vector, matrix, vector, matrix,
    )
    return jax.shard_map(
        body(dp, shards),
        mesh=mesh,
        in_specs=(rows, P(("dp", "shard"))) + params,
        out_specs=(rows, rows) + params,
        check_vma=False,
    )
```

```python
import jax
import jax.numpy as jnp
from jax import lax
from jax.experimental import pallas as pl
from jax.experimental.pallas import tpu as pltpu
from jax.sharding import PartitionSpec as P

EPS = 1e-05
WIDTH = 512
HEAD = 64
FF = 2048
VOCAB = 256
SEQ_LEN = 1024
CHUNK = 256
SUB = 128
SUBS = CHUNK // SUB
ROWS = 512
HALF = 256
PIECE = 16
COLS_PROJ = 4 * HALF
COLS_BOTH = 2 * COLS_PROJ
COLS_LAST = COLS_PROJ + 128
COLS_UP = WIDTH + FF
COLS_DOWN = 4 * WIDTH + VOCAB
F32 = jnp.float32
BF16 = jnp.bfloat16
MIB = 1024 * 1024


def nn(a, b):
    return lax.dot_general(a, b, (((1,), (0,)), ((), ())), preferred_element_type=F32)


def nt(a, b):
    return lax.dot_general(a, b, (((1,), (1,)), ((), ())), preferred_element_type=F32)


def tn(a, b):
    return lax.dot_general(a, b, (((0,), (0,)), ((), ())), preferred_element_type=F32)


def norm_parts(values):
    centre = values - jnp.mean(values, axis=-1, keepdims=True)
    inverse = lax.rsqrt(jnp.mean(centre * centre, axis=-1, keepdims=True) + EPS)
    return centre * inverse, inverse


def norm_pull(grad, unit, inverse, gain):
    scaled = grad * gain
    return inverse * (
        scaled
        - jnp.mean(scaled, axis=-1, keepdims=True)
        - unit * jnp.mean(scaled * unit, axis=-1, keepdims=True)
    )


def vector_of(vec_ref, idx, row):
    return jnp.concatenate(
        [vec_ref[s ^ idx[2], row : row + 1, :].astype(F32) for s in range(4)], axis=1
    )


def bias_up_of(vec_ref, idx):
    return jnp.concatenate(
        [
            vec_ref[s ^ idx[2], row : row + 1, :].astype(F32)
            for s in range(4)
            for row in range(5, 9)
        ],
        axis=1,
    )


def each_piece(idx, near, far):
    for c, buf in ((0, near), (1, far)):
        for xy in range(4):
            member = ((xy ^ idx[1]) * 2) + (c ^ idx[0])
            for s in range(4):
                yield s ^ idx[2], member, buf.at[xy, s]


def each_member(idx, near, far):
    for c, buf in ((0, near), (1, far)):
        for xy in range(4):
            yield None, ((xy ^ idx[1]) * 2) + (c ^ idx[0]), buf.at[xy]


def rows_at(start, size):
    return pl.ds(pl.multiple_of(start, PIECE), size)


def put_parts(idx, keep, send, tile, shard, columns):
    for xy in range(4):
        first = tile[32 * xy : 32 * xy + 16]
        second = tile[32 * xy + 16 : 32 * xy + 32]
        own_first = idx[0] == 0
        keep[xy ^ idx[1], shard ^ idx[2], :, columns] = jnp.where(own_first, first, second)
        send[xy ^ idx[1], shard ^ idx[2], :, columns] = jnp.where(own_first, second, first)


def pack_kernel(
    g1, b1, g2, b2, bd, bu, wq, wk, wv, wc, wm, wu, wd, wr, pa, pc, pd, sems
):
    member = lax.axis_index("dp") % 8
    across = member ^ 6
    rows = rows_at(member * PIECE, PIECE)
    moves = []
    for j, w in enumerate((wq, wk, wv, wc)):
        for half in range(2):
            start = half * COLS_PROJ + j * HALF
            part = w.at[rows, half * HALF : (half + 1) * HALF]
            moves.append((part, pa.at[:, start : start + HALF]))
    moves.append((wm.at[rows, :], pc.at[:, :WIDTH]))
    moves.append((wu.at[rows, :], pc.at[:, WIDTH:]))
    for place, who in enumerate((member, across)):
        for i in range(4):
            part = wd.at[rows_at(who * 64 + 16 * i, PIECE), :]
            moves.append((part, pd.at[place, :, i * WIDTH : (i + 1) * WIDTH]))
        moves.append((wr.at[rows_at(who * PIECE, PIECE), :], pd.at[place, :, 4 * WIDTH :]))
    copies = [pltpu.make_async_copy(src, dst, sems.at[i]) for i, (src, dst) in enumerate(moves)]
    for copy in copies:
        copy.start()
    lines = [v[...].astype(F32).reshape(1, 128) for v in (g1, b1, g2, b2, bd)]
    lines += [bu[128 * j : 128 * j + 128].astype(F32).reshape(1, 128) for j in range(4)]
    lines.append(jnp.zeros((7, 128), F32))
    pa[:, COLS_BOTH:] = jnp.concatenate(lines, axis=0).astype(BF16)
    for copy in copies:
        copy.wait()


def first_norm_kernel(idx, vec, x, a1, both_t):
    unit, _ = norm_parts(x[...].astype(F32))
    low = (unit * vector_of(vec, idx, 0) + vector_of(vec, idx, 1)).astype(BF16)
    a1[...] = low
    both_t[:WIDTH, :] = low.T
    both_t[WIDTH : 2 * WIDTH, :] = unit.astype(BF16).T
    both_t[2 * WIDTH :, :] = jnp.ones((PIECE, both_t.shape[1]), BF16)


def lanes_low():
    return lax.broadcasted_iota(jnp.int32, (1, 128), 1) < HEAD


def stacked(value):
    low = lanes_low().astype(F32).astype(BF16)
    high = (1.0 - lanes_low().astype(F32)).astype(BF16)
    return jnp.concatenate([value * low, value * high], axis=0)


def head_ones():
    row = (lax.broadcasted_iota(jnp.int32, (256, 128), 0) & 127) < HEAD
    col = lax.broadcasted_iota(jnp.int32, (256, 128), 1) < HEAD
    return (row == col).astype(F32).astype(BF16)


def head_sum(value, ones):
    high = value.astype(BF16)
    rest = (value - high.astype(F32)).astype(BF16)
    return nn(side(high, rest), ones)


def sub_places(subs):
    return [
        (sub, pair, slice(SUB * sub, SUB * sub + SUB), slice(128 * pair, 128 * pair + 128))
        for sub in subs
        for pair in range(2)
    ]


def head_max(value):
    low = lanes_low()
    first = jnp.max(jnp.where(low, value, -jnp.inf), axis=-1, keepdims=True)
    second = jnp.max(jnp.where(low, -jnp.inf, value), axis=-1, keepdims=True)
    return jnp.where(low, first, second)


def same_head():
    row = lax.broadcasted_iota(jnp.int32, (128, 256), 0) < HEAD
    col = (lax.broadcasted_iota(jnp.int32, (128, 256), 1) & 127) < HEAD
    return row == col


def causal_pair(transposed=False):
    row = lax.broadcasted_iota(jnp.int32, (SUB, 2 * SUB), 0)
    col = lax.broadcasted_iota(jnp.int32, (SUB, 2 * SUB), 1) & (SUB - 1)
    return (row <= col) if transposed else (col <= row)


def causal_whole(transposed=False):
    row = lax.broadcasted_iota(jnp.int32, (CHUNK, CHUNK), 0)
    col = lax.broadcasted_iota(jnp.int32, (CHUNK, CHUNK), 1)
    keep = (row <= col) if transposed else (col <= row)
    return keep.astype(F32).astype(BF16)


def side(*values):
    return jnp.concatenate(values, axis=1)


def masked(keep, value):
    return jnp.where(keep, value, 0.0).astype(BF16)


def attend_kernel(idx, a1, near, far, proj_o, float_o, mixed_o, kept, w_o, state, count_z):
    step = pl.program_id(0)

    @pl.when(step == 0)
    def _():
        for shard, member, piece in each_piece(idx, near, far):
            w_o[rows_at(shard * 128 + member * PIECE, PIECE), :] = piece[...]
        state[...] = jnp.zeros_like(state)
        count_z[...] = jnp.zeros_like(count_z)

    a = a1[...]
    q_all = nn(a, w_o[:, :HALF]).astype(BF16)
    k_all = nn(a, w_o[:, HALF : 2 * HALF]).astype(BF16)
    expo = jnp.exp(nn(a, w_o[:, 3 * HALF :]))
    e_all = expo.astype(BF16)
    v_all = nn(a, w_o[:, 2 * HALF : 3 * HALF]).astype(BF16)
    for j, value in enumerate((q_all, k_all, v_all, e_all)):
        proj_o[:, j * HALF : (j + 1) * HALF] = value
    float_o[:, :HALF] = expo
    total = nn(causal_whole(), e_all) + count_z[...]
    count_z[...] = total[CHUNK - 1 :, :]
    inverse = 1.0 / total
    float_o[:, HALF : 2 * HALF] = inverse
    tri, block, ones = causal_pair(), same_head(), head_ones()
    places = sub_places(range(SUBS))
    lows, wide_e, numers, ratios = {}, {}, {}, {}
    for pair in range(2):
        current = state[pair]
        for sub in range(SUBS):
            rows, at = slice(SUB * sub, SUB * sub + SUB), slice(128 * pair, 128 * pair + 128)
            lows[sub, pair] = current.astype(BF16)
            kept[sub, pair] = lows[sub, pair]
            wide_e[sub, pair] = stacked(e_all[rows, at])
            more = tn(e_all[rows, at], side(k_all[rows, at], v_all[rows, at]))
            current = current + jnp.where(block, more, 0.0)
        state[pair] = current
    for sub, pair, rows, at in places:
        scores = masked(tri, nt(q_all[rows, at], stacked(k_all[rows, at])))
        numer = nn(scores, wide_e[sub, pair])
        numers[sub, pair] = numer + nt(q_all[rows, at], lows[sub, pair][:, :128])

    def soften(sub, pair, rows, at):
        inv = inverse[rows, at]
        logits = (HEAD ** -0.5) * numers[sub, pair] * inv
        expd = jnp.exp(logits - head_max(logits))
        probs = expd * (1.0 / head_sum(expd, ones))
        ratios[sub, pair] = (probs * inv).astype(BF16)
        float_o[rows, 2 * HALF + 128 * pair : 2 * HALF + 128 * pair + 128] = logits
        float_o[rows, 3 * HALF + 128 * pair : 3 * HALF + 128 * pair + 128] = probs
        mixed_o[rows, at] = ratios[sub, pair]

    def mix(sub, pair, rows, at):
        mixing = masked(tri, nt(ratios[sub, pair], wide_e[sub, pair]))
        out = nn(mixing, stacked(v_all[rows, at])) + nn(ratios[sub, pair], lows[sub, pair][:, 128:])
        mixed_o[rows, HALF + 128 * pair : HALF + 128 * pair + 128] = out.astype(BF16)

    for i, place in enumerate(places):
        soften(*place)
        if i:
            mix(*places[i - 1])
    mix(*places[-1])


def feed_kernel(
    idx, vec, x, o0, o1, target, up_near_i, up_far_i, down_near_i, ends_i, sides_i,
    out_o, h_o, slope_o, dy_o, bias_o, keep, send, mix_o, up_o, down_o,
    up_near, up_far, down_near, down_far,
    w_mix, w_up, w_down, w_read, act_s, out_s, h_s, slope_s, dy_s, dl_s, df_s, sems, row_sems,
):
    step = pl.program_id(0)
    moves = (
        (up_near_i, up_near), (up_far_i, up_far), (down_near_i, down_near),
        (ends_i.at[0], down_far.at[0]), (ends_i.at[1], down_far.at[3]), (sides_i, down_far.at[1:3]),
        (w_mix, mix_o), (w_up, up_o), (w_down, down_o),
    )
    copies = [pltpu.make_async_copy(src, dst, sems.at[i]) for i, (src, dst) in enumerate(moves)]

    @pl.when(step == 0)
    def _():
        for copy in copies[:6]:
            copy.start()
        for copy in copies[:2]:
            copy.wait()
        for shard, member, piece in each_piece(idx, up_near, up_far):
            rows = rows_at(shard * 128 + member * PIECE, PIECE)
            w_mix[rows, :] = piece[:, :WIDTH]
            w_up[rows, :] = piece[:, WIDTH:]
        for copy in copies[2:6]:
            copy.wait()
        for shard, member, piece in each_piece(idx, down_near, down_far):
            for i in range(4):
                rows = rows_at(shard * 512 + member * 64 + 16 * i, PIECE)
                w_down[rows, :] = piece[:, i * WIDTH : (i + 1) * WIDTH]
            w_read[rows_at(shard * 128 + member * PIECE, PIECE), :] = piece[:, 4 * WIDTH :]
        for copy in copies[6:]:
            copy.start()
        bias_o[...] = jnp.zeros_like(bias_o)

    def row_copies(place):
        at = pl.ds(pl.multiple_of(place * ROWS, ROWS), ROWS)
        pairs = ((out_s, out_o), (h_s, h_o), (slope_s, slope_o), (dy_s, dy_o))
        return [
            pltpu.make_async_copy(src.at[at], dst.at[at], row_sems.at[place, i])
            for i, (src, dst) in enumerate(pairs)
        ]

    rows = pl.ds(pl.multiple_of(step * ROWS, ROWS), ROWS)
    attn = nn(o0[...], w_mix[:HALF, :]) + nn(o1[...], w_mix[HALF:, :])
    resid = x[...].astype(F32) + attn
    h_s[rows, :] = resid
    unit, _ = norm_parts(resid)
    second = (unit * vector_of(vec, idx, 2) + vector_of(vec, idx, 3)).astype(BF16)
    bias = bias_up_of(vec, idx)
    branch = jnp.zeros((ROWS, WIDTH), F32)
    scale = (2.0 / jnp.pi) ** 0.5
    at = [slice(512 * j, 512 * j + 512) for j in range(4)]
    products = nn(second, w_up[:, at[0]])
    for j in range(4):
        z = products + bias[:, at[j]]
        if j < 3:
            products = nn(second, w_up[:, at[j + 1]])
        zz = z * z
        cdf = 0.5 + 0.5 * jnp.tanh(z * (scale + (scale * 0.044715) * zz))
        active = z * cdf
        slope = cdf + (active - active * cdf) * (2 * scale + (6 * scale * 0.044715) * zz)
        slope_s[rows, at[j]] = slope.astype(BF16)
        act = active.astype(BF16)
        act_s[rows, at[j]] = act
        branch += nn(act, w_down[at[j], :])
    out = (resid + (branch + vector_of(vec, idx, 4))).astype(BF16)
    out_s[rows, :] = out
    logits = nn(out, w_read[...])
    expd = jnp.exp(logits - jnp.max(logits, axis=-1, keepdims=True))
    soft = expd / jnp.sum(expd, axis=-1, keepdims=True)
    classes = lax.broadcasted_iota(jnp.int32, (VOCAB, ROWS), 0)
    hits = jnp.where(classes == target[rows].reshape(1, ROWS), 1.0, 0.0).T
    dl = (soft - hits).astype(BF16)
    dl_s[rows, :] = dl
    dy = nt(dl, w_read[...])
    dy_s[rows, :] = dy
    df = dy.astype(BF16)
    df_s[rows, :] = df
    bias_o[...] += jnp.sum(df.astype(F32), axis=0, keepdims=True)
    for copy in row_copies(step):
        copy.start()

    @pl.when(step == pl.num_programs(0) - 1)
    def _():
        whole = tn(out_s[...], dl_s[...]).astype(BF16)
        for shard in range(4):
            tile = whole[shard * 128 : shard * 128 + 128]
            put_parts(idx, keep, send, tile, shard, slice(4 * WIDTH, None))
            large = tn(act_s[:, shard * 512 : shard * 512 + 512], df_s[...]).astype(BF16)
            for xy in range(4):
                tile = large[xy * 128 : xy * 128 + 128]
                own_first = idx[0] == 0
                for i in range(4):
                    first = tile[16 * i : 16 * i + 16]
                    later = tile[64 + 16 * i : 64 + 16 * i + 16]
                    at = slice(i * WIDTH, (i + 1) * WIDTH)
                    keep[xy ^ idx[1], shard ^ idx[2], :, at] = jnp.where(own_first, first, later)
                    send[xy ^ idx[1], shard ^ idx[2], :, at] = jnp.where(own_first, later, first)
        for copy in copies[6:]:
            copy.wait()
        for place in range(act_s.shape[0] // ROWS):
            for copy in row_copies(place):
                copy.wait()


def feed_back_kernel(
    idx, vec, h_i, slope_i, dy_i, o0_i, o1_i, mix_i, up_i, down_i,
    dh_o, do_o, gain_o, shift_o, bias_o, keep, send,
    w_mix, w_up, w_down, h_s, slope_s, dy_s, o0, o1, dz_s, a2_s, da_s, dh_s, do_s,
    sems, row_sems, out_sems,
):
    step = pl.program_id(0)
    places = dz_s.shape[0] // ROWS
    half = pl.ds(HALF, HALF)
    moves = (
        (down_i, w_down), (up_i, w_up), (mix_i, w_mix), (o0_i.at[:, half], o0), (o1_i.at[:, half], o1)
    )
    copies = [pltpu.make_async_copy(src, dst, sems.at[i]) for i, (src, dst) in enumerate(moves)]

    def row_copies(place):
        at = pl.ds(pl.multiple_of(place * ROWS, ROWS), ROWS)
        pairs = ((dy_i, dy_s), (slope_i, slope_s), (h_i, h_s))
        return [
            pltpu.make_async_copy(src.at[at], dst.at[at], row_sems.at[place, i])
            for i, (src, dst) in enumerate(pairs)
        ]

    def out_copies(place):
        at = pl.ds(pl.multiple_of(place * ROWS, ROWS), ROWS)
        pairs = ((dh_s, dh_o), (do_s, do_o))
        return [
            pltpu.make_async_copy(src.at[at], dst.at[at], out_sems.at[place, i])
            for i, (src, dst) in enumerate(pairs)
        ]

    @pl.when(step == 0)
    def _():
        copies[0].start()
        for copy in row_copies(0):
            copy.start()
        for copy in copies[1:3]:
            copy.start()
        gain_o[...] = jnp.zeros_like(gain_o)
        shift_o[...] = jnp.zeros_like(shift_o)
        bias_o[...] = jnp.zeros_like(bias_o)
        copies[0].wait()

    for copy in row_copies(step)[:2]:
        copy.wait()
    rows = pl.ds(pl.multiple_of(step * ROWS, ROWS), ROWS)
    gain = vector_of(vec, idx, 2)
    d_out = dy_s[rows, :]
    df = d_out.astype(BF16)
    for j in range(4):
        at = slice(512 * j, 512 * j + 512)
        dz = (nt(df, w_down[at, :]) * slope_s[rows, at].astype(F32)).astype(BF16)
        dz_s[rows, at] = dz
        bias_o[:, at] += jnp.sum(dz.astype(F32), axis=0, keepdims=True)

    @pl.when(step == 0)
    def _():
        for place in range(1, places):
            for copy in row_copies(place):
                copy.start()
        for copy in copies[3:]:
            copy.start()
        for copy in copies[1:3]:
            copy.wait()

    row_copies(step)[2].wait()
    d_second = nt(dz_s[rows, :], w_up[...])
    unit, inverse = norm_parts(h_s[rows, :])
    a2_s[rows, :] = (unit * gain + vector_of(vec, idx, 3)).astype(BF16)
    gain_o[...] += jnp.sum(d_second * unit, axis=0, keepdims=True)
    shift_o[...] += jnp.sum(d_second, axis=0, keepdims=True)
    dh = d_out + norm_pull(d_second, unit, inverse, gain)
    dh_s[rows, :] = dh
    da = dh.astype(BF16)
    da_s[rows, :] = da
    do_s[rows, :] = nt(da, w_mix[...]).astype(BF16)
    for copy in out_copies(step):
        copy.start()

    @pl.when(step == pl.num_programs(0) - 1)
    def _():
        for copy in copies[3:]:
            copy.wait()
        for half in range(2):
            large = tn((o0, o1)[half][...], da_s[...]).astype(BF16)
            for i in range(2):
                tile = large[128 * i : 128 * i + 128]
                put_parts(idx, keep, send, tile, 2 * half + i, slice(0, WIDTH))
        for j in range(4):
            large = tn(a2_s[...], dz_s[:, 512 * j : 512 * j + 512]).astype(BF16)
            at = slice(WIDTH + 512 * j, WIDTH + 512 * j + 512)
            for shard in range(4):
                put_parts(idx, keep, send, large[shard * 128 : shard * 128 + 128], shard, at)
        for place in range(places):
            for copy in out_copies(place):
                copy.wait()


def proj_gradient(idx, both_t, w, dx, keep, send):
    on_gain = jnp.zeros((WIDTH, HALF), F32)
    sums = []
    for j in range(4):
        at = slice(j * HALF, (j + 1) * HALF)
        product = nn(both_t[...], dx[:, at])
        low = product[:WIDTH].astype(BF16)
        for shard in range(4):
            put_parts(idx, keep, send, low[shard * 128 : shard * 128 + 128], shard, at)
        on_gain += product[WIDTH : 2 * WIDTH] * w[:, at].astype(F32)
        sums.append(product[2 * WIDTH : 2 * WIDTH + 8])
    sums = side(*sums)
    high = sums.astype(BF16)
    rest = (sums - high.astype(F32)).astype(BF16)
    shift_rows = nt(jnp.concatenate([high, rest], axis=0), w[...])
    gain_column = jnp.sum(on_gain, axis=1, keepdims=True)
    gain_row = side(gain_column, jnp.zeros((WIDTH, 7), F32)).T[:1]
    return jnp.concatenate([gain_row, shift_rows[:1] + shift_rows[8:9], jnp.zeros((6, WIDTH), F32)])


def late_operands(pairs, sems):
    copies = [pltpu.make_async_copy(src, dst, sems.at[i]) for i, (src, dst) in enumerate(pairs)]

    @pl.when(pl.program_id(0) == 0)
    def _():
        for copy in copies:
            copy.start()

    return copies


def attend_back_kernel(
    idx, both_t, w, proj, floats, ratios, do_i, kept,
    dx_o, keep, send, share_o,
    state, count_z, dx_s, both_s, w_s, sems,
):
    copies = late_operands(((both_t, both_s), (w, w_s)), sems)
    attend_back_step(proj, floats, ratios, do_i, kept, dx_o, state, count_z, dx_s)

    @pl.when(pl.program_id(0) == pl.num_programs(0) - 1)
    def _():
        for copy in copies:
            copy.wait()
        share_o[...] = proj_gradient(idx, both_s, w_s, dx_s, keep, send)


def attend_back_last_kernel(
    idx, both_t, w, proj, floats, ratios, do_i, kept,
    share, g_g2, g_b2, g_bd, g_bu,
    dx_o, keep, send,
    state, count_z, dx_s, both_s, w_s, sems,
):
    copies = late_operands(((both_t, both_s), (w, w_s)), sems)
    attend_back_step(proj, floats, ratios, do_i, kept, dx_o, state, count_z, dx_s)

    @pl.when(pl.program_id(0) == pl.num_programs(0) - 1)
    def _():
        for copy in copies:
            copy.wait()
        total = proj_gradient(idx, both_s, w_s, dx_s, keep, send) + share[...]
        for s in range(4):
            at = slice(128 * s, 128 * s + 128)
            lines = [total[:2, at], g_g2[:, at], g_b2[:, at], g_bd[:, at]]
            lines += [g_bu[:, 512 * s + 128 * j : 512 * s + 128 * j + 128] for j in range(4)]
            lines.append(jnp.zeros((7, 128), F32))
            block = jnp.concatenate(lines, axis=0).astype(BF16)
            for xy in range(4):
                keep[xy, s ^ idx[2], :, COLS_PROJ:] = block
                send[xy, s ^ idx[2], :, COLS_PROJ:] = block


def attend_back_step(proj, floats, ratios, do_i, kept, dx_o, state, count_z, dx_s):
    step = pl.program_id(0)
    chunk = pl.num_programs(0) - 1 - step

    @pl.when(step == 0)
    def _():
        state[...] = jnp.zeros_like(state)
        count_z[...] = jnp.zeros_like(count_z)

    def take(ref, j, rows, pair):
        return ref[rows, j * HALF + 128 * pair : j * HALF + 128 * pair + 128]

    tri, trt, block, ones = causal_pair(), causal_pair(True), same_head(), head_ones()
    places = sub_places(reversed(range(SUBS)))
    d_mixes, wide, d_numers, d_totals, others = {}, {}, {}, {}, {}
    for sub, pair, rows, at in places:
        v = take(proj, 2, rows, pair)
        d_mixes[sub, pair] = masked(tri, nt(do_i[rows, at], stacked(v)))
        wide[sub, pair] = stacked(take(proj, 3, rows, pair))
    for sub, pair, rows, at in places:
        do, ratio = do_i[rows, at], ratios[rows, at]
        q, k, v, e = [take(proj, j, rows, pair) for j in range(4)]
        inv, logits, probs = [take(floats, j, rows, pair) for j in (1, 2, 3)]
        d_ratio = nn(d_mixes[sub, pair], wide[sub, pair])
        d_ratio = (d_ratio + nt(do, kept[sub, pair][:, 128:])) * inv
        weighed = d_ratio * probs
        d_logits = weighed - probs * head_sum(weighed, ones)
        d_numers[sub, pair] = ((HEAD ** -0.5) * d_logits * inv).astype(BF16)
        d_totals[sub, pair] = (-(weighed + d_logits * logits) * inv).astype(BF16)
        wide_q, wide_r, wide_do = stacked(q), stacked(ratio), stacked(do)
        scores = masked(trt, nt(k, wide_q))
        mixing = masked(trt, nt(e, wide_r))
        d_mix_t = masked(trt, nt(v, wide_do))
        others[sub, pair] = (scores, d_mix_t, nn(mixing, wide_do), wide_q, wide_r)
    d_total = jnp.concatenate([side(d_totals[sub, 0], d_totals[sub, 1]) for sub in range(SUBS)], axis=0)
    total_z = nn(causal_whole(True), d_total) + count_z[...]
    count_z[...] = total_z[:1, :]
    currents = [state[0], state[1]]
    lows = {}
    for sub, pair, rows, at in places:
        lows[sub, pair] = currents[pair].astype(BF16)
        more = side(
            tn(ratios[rows, at], do_i[rows, at]), tn(d_numers[sub, pair], take(proj, 0, rows, pair))
        )
        currents[pair] = currents[pair] + jnp.where(block, more, 0.0)
    state[0], state[1] = currents
    for sub, pair, rows, at in places:
        k, v, e = [take(proj, j, rows, pair) for j in (1, 2, 3)]
        scores, d_mix_t, dv, wide_q, wide_r = others[sub, pair]
        d_numer, low = d_numers[sub, pair], lows[sub, pair]
        wide_n = stacked(d_numer)
        d_scores = masked(tri, nt(d_numer, wide[sub, pair]))
        d_scores_t = masked(trt, nt(e, wide_n))
        both = nn(e, low)
        de = nn(side(d_mix_t, scores), jnp.concatenate([wide_r, wide_n], axis=0))
        de = de + nt(side(v, k), low) + total_z[rows, at]
        dq = nn(d_scores, stacked(k)) + nn(d_numer, kept[sub, pair][:, :128])
        dk = nn(d_scores_t, wide_q) + both[:, 128:]
        dv = dv + both[:, :128]
        dc = de * take(floats, 0, rows, pair)
        for j, value in enumerate((dq, dk, dv, dc)):
            dx_o[rows, j * HALF + 128 * pair : j * HALF + 128 * pair + 128] = value.astype(BF16)
    dx_s[pl.ds(pl.multiple_of(chunk * CHUNK, CHUNK), CHUNK), :] = dx_o[...]


def inputs_kernel(idx, vec, x, dh, dx0, dx1, w0, w1, dx_o):
    unit, inverse = norm_parts(x[...].astype(F32))
    d_first = nt(dx0[...], w0[...]) + nt(dx1[...], w1[...])
    dx_o[...] = dh[...] + norm_pull(d_first, unit, inverse, vector_of(vec, idx, 0))


def unpack_proj_kernel(idx, near, far, query, key, value, control, g1, b1, g2, b2, bd, bu):
    for shard, member, piece in each_member(idx, near, far):
        rows = rows_at(member * PIECE, PIECE)
        for j, out in enumerate((query, key, value, control)):
            for half in range(2):
                start = half * COLS_PROJ + j * HALF
                out[rows, half * HALF : (half + 1) * HALF] = piece[:, start : start + HALF].astype(F32)

        @pl.when(member == 0)
        def _():
            lines = piece[:, COLS_BOTH:].astype(F32)
            for i, out in enumerate((g1, b1, g2, b2, bd)):
                out[...] = lines[i]
            for i in range(4):
                bu[128 * i : 128 * i + 128] = lines[5 + i]


def unpack_feed_kernel(idx, near, far, mix, up, down, read):
    for shard, member, piece in each_member(idx, near, far):
        rows = rows_at(member * PIECE, PIECE)
        mix[rows, :] = piece[:, :WIDTH].astype(F32)
        up[rows, :] = piece[:, WIDTH:COLS_UP].astype(F32)
        for i in range(4):
            start = COLS_UP + i * WIDTH
            down[rows_at(member * 64 + 16 * i, PIECE), :] = piece[:, start : start + WIDTH].astype(F32)
        read[rows, :] = piece[:, COLS_UP + 4 * WIDTH :].astype(F32)


def shaped(shape, dtype):
    return jax.ShapeDtypeStruct(shape, dtype)


def call(kernel, name, args, outs, steps=None, scratch=(), flops=0, limit=44):
    grid = (steps,) if steps else ()

    def spec(shape, block):
        if block == "hbm":
            return pl.BlockSpec(memory_space=pl.ANY)
        if block is None:
            return pl.BlockSpec(tuple(shape), lambda *_: (0,) * len(shape))
        return pl.BlockSpec(*block)

    in_specs = []
    for array, block in args:
        if array.dtype == jnp.int32 and array.shape == (3,):
            in_specs.append(pl.BlockSpec(memory_space=pltpu.SMEM))
        else:
            in_specs.append(spec(array.shape, block))
    moved = sum(a.size * a.dtype.itemsize for a, _ in args)
    return pl.pallas_call(
        kernel,
        grid=grid,
        in_specs=in_specs,
        out_specs=[spec(shape, block) for shape, _, block in outs],
        out_shape=[shaped(shape, dtype) for shape, dtype, _ in outs],
        scratch_shapes=list(scratch),
        compiler_params=pltpu.CompilerParams(
            vmem_limit_bytes=limit * MIB,
            dimension_semantics=("arbitrary",) * len(grid) if grid else None,
        ),
        cost_estimate=pl.CostEstimate(flops=1000, bytes_accessed=1000, transcendentals=0),
        name=name,
    )(*[array for array, _ in args])


def swap(value, axis, size, distance):
    return lax.ppermute(value, axis, [(i, i ^ distance) for i in range(size)])


def pin(*values):
    return lax.optimization_barrier(values)


def near_rows(piece, shards):
    return [swap(piece, "shard", shards, k) for k in range(1, 4)]


def near_pair(piece, shards):
    return jnp.stack([piece, swap(piece, "shard", shards, 1)])


def far_pair(pair, shards):
    return swap(pair, "shard", shards, 2)


def sum_of(values):
    values = [v.astype(F32) for v in values]
    return ((values[0] + values[1]) + (values[2] + values[3])).astype(BF16)


def core_sum(keep, got):
    return [(keep[k].astype(F32) + got[k].astype(F32)).astype(BF16) for k in range(4)]


def plane_start(parts, dp):
    return [swap(parts[k], "dp", dp, 2 * k) for k in range(1, 4)]


def plane_sum(parts, got):
    return [sum_of([parts[0][k], got[0][k], got[1][k], got[2][k]]) for k in range(4)]


def plane_halves(parts, got):
    total = [p.astype(F32) for p in [parts[0]] + got]
    total = ((total[0] + total[1]) + (total[2] + total[3])).astype(BF16)
    return total[:2], total[2:]


def half_start(high, shards):
    return swap(high, "shard", shards, 2)


def half_sum(low, got):
    return [(low[k].astype(F32) + got[k].astype(F32)).astype(BF16) for k in range(2)]


def last_start(pair, shards):
    return swap(pair[1], "shard", shards, 1)


def last_sum(pair, got, dp):
    return across_planes((pair[0].astype(F32) + got.astype(F32)).astype(BF16), dp)


def across_planes(total, dp):
    distance = 8
    while distance < dp:
        total = (total.astype(F32) + swap(total, "dp", dp, distance).astype(F32)).astype(BF16)
        distance *= 2
    return total


def shard_start(rows, shards):
    return [swap(rows[k], "shard", shards, k) for k in range(1, 4)]


def shard_sum(rows, got, dp):
    return across_planes(sum_of([rows[0]] + got), dp)


def body(dp, shards):
    def on_device(
        tokens, targets, gain_one, bias_one, w_query, w_key, w_value, w_control, w_mix,
        gain_two, bias_two, w_up, bias_up, w_down, bias_down, w_read,
    ):
        count = tokens.shape[0]
        steps = count // CHUNK
        rows = WIDTH // shards
        member = lax.axis_index("dp") % 8
        idx = jnp.stack([member % 2, member // 2, lax.axis_index("shard")]).astype(jnp.int32)
        forward = lambda i: (i, 0)
        back = lambda i: (steps - 1 - i, 0)
        tok = lambda n: ((CHUNK, n), forward)
        parts = (4, 4, PIECE)

        weights = (w_query, w_key, w_value, w_control, w_mix, w_up, w_down, w_read)
        sizes = [(PIECE, COLS_BOTH + 128), (PIECE, COLS_UP), (2, PIECE, COLS_DOWN)]
        vectors = (gain_one, bias_one, gain_two, bias_two, bias_down, bias_up)
        pa, pu, pd = call(
            pack_kernel,
            "pack_weights",
            [(v, None) for v in vectors] + [(w, "hbm") for w in weights],
            [(size, BF16, None) for size in sizes],
            scratch=[pltpu.SemaphoreType.DMA((20,))],
            limit=56,
        )
        got_a = near_rows(pa, shards)
        pair_u = near_pair(pu, shards)
        rows_a = jnp.stack([pa[:, :COLS_BOTH]] + [g[:, :COLS_BOTH] for g in got_a])
        vec = jnp.stack([pa[:, COLS_BOTH:]] + [g[:, COLS_BOTH:] for g in got_a])
        rows_a, vec, pd, tokens_a = pin(rows_a, vec, pd, tokens)
        plane_a = [swap(rows_a, "dp", dp, 2 * k) for k in range(1, 4)]
        got_u = far_pair(pair_u, shards)
        pair_d = near_pair(pd, shards)
        a1, both_t = call(
            first_norm_kernel,
            "first_norm",
            [(idx, None), (vec, None), (tokens_a, None)],
            [
                ((count, WIDTH), BF16, None),
                ((2 * WIDTH + PIECE, count), BF16, None),
            ],
        )
        plane_a, got_u, a1, both_t = pin(plane_a, got_u, a1, both_t)
        near_a = jnp.stack([rows_a] + plane_a)
        far_a = swap(near_a, "dp", dp, 1)
        pair_d, _ = pin(pair_d, near_a)
        got_d = far_pair(pair_d, shards)
        got_u, _ = pin(got_u, near_a)
        rows_u = jnp.concatenate([pair_u, got_u])
        plane_u = plane_start([rows_u] * 4, dp)

        kept = ((SUBS, 2, 128, 256), lambda i: (i, 0, 0, 0))

        def attend(a1, half):
            at = ((4, 4, PIECE, COLS_PROJ), lambda i: (0, 0, 0, half))
            return call(
                attend_kernel,
                "attend",
                [(idx, None), (a1, tok(WIDTH)), (near_a, at), (far_a, at)],
                [
                    ((count, COLS_PROJ), BF16, tok(COLS_PROJ)),
                    ((count, COLS_PROJ), F32, tok(COLS_PROJ)),
                    ((count, 2 * HALF), BF16, tok(2 * HALF)),
                    ((SUBS * steps, 2, 128, 256), BF16, kept),
                    ((WIDTH, COLS_PROJ), BF16, None),
                ],
                steps,
                [
                    pltpu.VMEM((2, 128, 256), F32),
                    pltpu.VMEM((1, HALF), F32),
                ],
                flops=6e9,
            )

        first = attend(a1, 0)
        first, plane_u, got_d, a1 = pin(first, plane_u, got_d, a1)
        rows_d = jnp.concatenate([pair_d, got_d])
        plane_d = [swap(rows_d[:, 0], "dp", dp, 2 * k) for k in range(1, 3)]
        near_u = jnp.stack([rows_u] + plane_u)
        far_u = swap(near_u, "dp", dp, 1)
        ends_d = swap(jnp.stack([rows_d[:, 0], rows_d[:, 1]]), "dp", dp, 1)
        second = attend(a1, 1)
        second, far_u, ends_d, plane_d = pin(second, far_u, ends_d, plane_d)
        near_d = jnp.stack([rows_d[:, 0]] + plane_d + [rows_d[:, 1]])
        sides_d = swap(jnp.stack(plane_d), "dp", dp, 1)
        halves = (first, second)
        o0, o1 = first[2], second[2]

        wide = lambda n: ((ROWS, n), forward)
        mixed_at = ((ROWS, HALF), lambda i: (i, 1))
        places = count // ROWS
        out, h, slope, dy, g_bias_down, keep_d, send_d, full_mix, full_up, full_down = call(
            feed_kernel,
            "feed_forward",
            [
                (idx, None), (vec, None), (tokens, wide(WIDTH)), (o0, mixed_at), (o1, mixed_at),
                (targets, None), (near_u, "hbm"), (far_u, "hbm"), (near_d, "hbm"),
                (ends_d, "hbm"), (sides_d, "hbm"),
            ],
            [
                ((count, WIDTH), BF16, "hbm"),
                ((count, WIDTH), F32, "hbm"),
                ((count, FF), BF16, "hbm"),
                ((count, WIDTH), F32, "hbm"),
                ((1, WIDTH), F32, None),
                (parts + (COLS_DOWN,), BF16, None),
                (parts + (COLS_DOWN,), BF16, None),
                ((WIDTH, WIDTH), BF16, "hbm"),
                ((WIDTH, FF), BF16, "hbm"),
                ((FF, WIDTH), BF16, "hbm"),
            ],
            places,
            [
                pltpu.VMEM(parts + (COLS_UP,), BF16),
                pltpu.VMEM(parts + (COLS_UP,), BF16),
                pltpu.VMEM(parts + (COLS_DOWN,), BF16),
                pltpu.VMEM(parts + (COLS_DOWN,), BF16),
                pltpu.VMEM((WIDTH, WIDTH), BF16),
                pltpu.VMEM((WIDTH, FF), BF16),
                pltpu.VMEM((FF, WIDTH), BF16),
                pltpu.VMEM((WIDTH, VOCAB), BF16),
                pltpu.VMEM((count, FF), BF16),
                pltpu.VMEM((count, WIDTH), BF16),
                pltpu.VMEM((count, WIDTH), F32),
                pltpu.VMEM((count, FF), BF16),
                pltpu.VMEM((count, WIDTH), F32),
                pltpu.VMEM((count, VOCAB), BF16),
                pltpu.VMEM((count, WIDTH), BF16),
                pltpu.SemaphoreType.DMA((9,)),
                pltpu.SemaphoreType.DMA((places, 4)),
            ],
            flops=8e9,
            limit=46,
        )
        got_d = swap(send_d, "dp", dp, 1)

        dh, d_mixed, g_gain_two, g_bias_two, g_bias_up, keep_u, send_u = call(
            feed_back_kernel,
            "feed_backward",
            [(idx, None), (vec, None)]
            + [(t, "hbm") for t in (h, slope, dy, o0, o1, full_mix, full_up, full_down)],
            [
                ((count, WIDTH), F32, "hbm"),
                ((count, WIDTH), BF16, "hbm"),
                ((1, WIDTH), F32, None),
                ((1, WIDTH), F32, None),
                ((1, FF), F32, None),
                (parts + (COLS_UP,), BF16, None),
                (parts + (COLS_UP,), BF16, None),
            ],
            places,
            [
                pltpu.VMEM((WIDTH, WIDTH), BF16),
                pltpu.VMEM((WIDTH, FF), BF16),
                pltpu.VMEM((FF, WIDTH), BF16),
                pltpu.VMEM((count, WIDTH), F32),
                pltpu.VMEM((count, FF), BF16),
                pltpu.VMEM((count, WIDTH), F32),
                pltpu.VMEM((count, HALF), BF16),
                pltpu.VMEM((count, HALF), BF16),
                pltpu.VMEM((count, FF), BF16),
                pltpu.VMEM((count, WIDTH), BF16),
                pltpu.VMEM((count, WIDTH), BF16),
                pltpu.VMEM((count, WIDTH), F32),
                pltpu.VMEM((count, WIDTH), BF16),
                pltpu.SemaphoreType.DMA((5,)),
                pltpu.SemaphoreType.DMA((places, 3)),
                pltpu.SemaphoreType.DMA((places, 2)),
            ],
            flops=8e9,
            limit=46,
        )
        got_d, d_mixed, send_u = pin(got_d, d_mixed, send_u)
        got_u = swap(send_u, "dp", dp, 1)
        sum_d = core_sum(keep_d, got_d)
        sum_d, d_mixed = pin(sum_d, d_mixed)
        got_d = plane_start(sum_d, dp)

        kept_back = ((SUBS, 2, 128, 256), lambda i: (steps - 1 - i, 0, 0, 0))

        def attend_back(half, d_mixed, extra=()):
            proj, floats, mixed, states, w = halves[half]
            wide = ((CHUNK, COLS_PROJ), back)
            column = ((CHUNK, HALF), lambda i: (steps - 1 - i, half))
            last = half == 1
            cols = COLS_LAST if last else COLS_PROJ
            return call(
                attend_back_last_kernel if last else attend_back_kernel,
                "attend_backward",
                [(idx, None), (both_t, "hbm"), (w, "hbm")]
                + [(proj, wide), (floats, wide), (mixed, ((CHUNK, HALF), back))]
                + [(d_mixed, column), (states, kept_back)]
                + [(t, None) for t in extra],
                [
                    ((count, COLS_PROJ), BF16, ((CHUNK, COLS_PROJ), back)),
                    (parts + (cols,), BF16, None),
                    (parts + (cols,), BF16, None),
                ]
                + ([] if last else [((8, WIDTH), F32, None)]),
                steps,
                [
                    pltpu.VMEM((2, 128, 256), F32),
                    pltpu.VMEM((1, HALF), F32),
                    pltpu.VMEM((count, COLS_PROJ), BF16),
                    pltpu.VMEM((2 * WIDTH + PIECE, count), BF16),
                    pltpu.VMEM((WIDTH, COLS_PROJ), BF16),
                    pltpu.SemaphoreType.DMA((2,)),
                ],
                flops=10e9,
            )

        dx0, keep_a, send_a, share = attend_back(0, d_mixed)
        got_d, got_u, send_a, d_mixed = pin(got_d, got_u, send_a, d_mixed)
        got_a = swap(send_a, "dp", dp, 1)
        sum_u = core_sum(keep_u, got_u)
        low_d, high_d = plane_halves(sum_d, got_d)
        sum_u, low_d, high_d, d_mixed = pin(sum_u, low_d, high_d, d_mixed)
        got_u = plane_start(sum_u, dp)
        got_d = half_start(high_d, shards)

        extra = (share, g_gain_two, g_bias_two, g_bias_down, g_bias_up)
        dx1, keep_b, send_b = attend_back(1, d_mixed, extra)
        got_d, got_u, got_a, send_b, dx1 = pin(got_d, got_u, got_a, send_b, dx1)
        got_b = swap(send_b, "dp", dp, 1)
        sum_p = [
            jnp.concatenate(both, axis=-1)
            for both in zip(core_sum(keep_a, got_a), core_sum(keep_b, got_b))
        ]
        sum_p, dx1 = pin(sum_p, dx1)
        got_p = plane_start(sum_p, dp)
        got_u, got_d, _ = pin(got_u, got_d, sum_p)
        low_u, high_u = plane_halves(sum_u, got_u)
        got_u = half_start(high_u, shards)
        pair_d = half_sum(low_d, got_d)
        got_d = last_start(pair_d, shards)
        d_tokens = call(
            inputs_kernel,
            "input_gradient",
            [
                (idx, None), (vec, None), (tokens, tok(WIDTH)), (dh, tok(WIDTH)),
                (dx0, tok(COLS_PROJ)), (dx1, tok(COLS_PROJ)),
                (first[4], None), (second[4], None),
            ],
            [((count, WIDTH), F32, tok(WIDTH))],
            steps,
            flops=3e9,
        )[0]
        got_u, got_d, d_tokens = pin(got_u, got_d, d_tokens)
        pair_u = half_sum(low_u, got_u)
        got_u = last_start(pair_u, shards)
        total_d = last_sum(pair_d, got_d, dp)
        got_p, _, _ = pin(got_p, pair_u, d_tokens)
        total_f = jnp.concatenate([last_sum(pair_u, got_u, dp), total_d], axis=-1)
        along_f = swap(total_f, "dp", dp, 4)
        got_p, _ = pin(got_p, total_f)
        rows_p = plane_sum(sum_p, got_p)
        got_p = shard_start(rows_p, shards)
        along_f, _ = pin(along_f, rows_p)
        pair_f = jnp.stack([total_f, along_f])
        up_f = swap(pair_f, "dp", dp, 2)
        got_p, _ = pin(got_p, pair_f)
        total_p = shard_sum(rows_p, got_p, dp)
        plane_p = plane_start([total_p] * 4, dp)
        up_f, _ = pin(up_f, plane_p[0])
        near_f = jnp.stack([pair_f, up_f], axis=1).reshape((4,) + total_f.shape)
        far_f = swap(near_f, "dp", dp, 1)
        g_mix, g_up, g_down, g_read = call(
            unpack_feed_kernel,
            "unpack_feed",
            [(idx, None), (near_f, None), (far_f, None)],
            [
                ((rows, WIDTH), F32, None),
                ((rows, FF), F32, None),
                ((4 * rows, WIDTH), F32, None),
                ((rows, VOCAB), F32, None),
            ],
        )
        near_p = jnp.stack([total_p] + plane_p)
        far_p = swap(near_p, "dp", dp, 1)
        far_p, g_up = pin(far_p, g_up)
        g_query, g_key, g_value, g_control, g1, b1, g2, b2, bd, bu = call(
            unpack_proj_kernel,
            "unpack_proj",
            [(idx, None), (near_p, None), (far_p, None)],
            [((rows, WIDTH), F32, None)] * 4 + [((128,), F32, None)] * 5 + [((512,), F32, None)],
        )
        return (
            out, d_tokens, g1, b1, g_query, g_key, g_value, g_control, g_mix,
            g2, b2, g_up, bu, g_down, bd, g_read,
        )

    return on_device


def solution(mesh):
    dp, shards = mesh.shape["dp"], mesh.shape["shard"]
    vector, matrix = P("shard"), P("shard", None)
    rows = P(("dp", "shard"), None)
    params = (
        vector, vector, matrix, matrix, matrix, matrix, matrix,
        vector, vector, matrix, vector, matrix, vector, matrix,
    )
    return jax.shard_map(
        body(dp, shards),
        mesh=mesh,
        in_specs=(rows, P(("dp", "shard"))) + params,
        out_specs=(rows, rows) + params,
        check_vma=False,
    )
```

```python
import jax
import jax.numpy as jnp
from jax import lax
from jax.experimental import pallas as pl
from jax.experimental.pallas import tpu as pltpu
from jax.sharding import PartitionSpec as P

EPS = 1e-05
WIDTH = 512
HEAD = 64
FF = 2048
VOCAB = 256
SEQ_LEN = 1024
CHUNK = 256
SUB = 128
SUBS = CHUNK // SUB
ROWS = 512
HALF = 256
PIECE = 16
COLS_PROJ = 4 * HALF
COLS_BOTH = 2 * COLS_PROJ
COLS_LAST = COLS_PROJ + 128
COLS_UP = WIDTH + FF
COLS_DOWN = 4 * WIDTH + VOCAB
F32 = jnp.float32
BF16 = jnp.bfloat16
MIB = 1024 * 1024


def nn(a, b):
    return lax.dot_general(a, b, (((1,), (0,)), ((), ())), preferred_element_type=F32)


def nt(a, b):
    return lax.dot_general(a, b, (((1,), (1,)), ((), ())), preferred_element_type=F32)


def tn(a, b):
    return lax.dot_general(a, b, (((0,), (0,)), ((), ())), preferred_element_type=F32)


def norm_parts(values):
    centre = values - jnp.mean(values, axis=-1, keepdims=True)
    inverse = lax.rsqrt(jnp.mean(centre * centre, axis=-1, keepdims=True) + EPS)
    return centre * inverse, inverse


def norm_pull(grad, unit, inverse, gain):
    scaled = grad * gain
    return inverse * (
        scaled
        - jnp.mean(scaled, axis=-1, keepdims=True)
        - unit * jnp.mean(scaled * unit, axis=-1, keepdims=True)
    )


def vector_of(vec_ref, idx, row):
    return jnp.concatenate(
        [vec_ref[s ^ idx[2], row : row + 1, :].astype(F32) for s in range(4)], axis=1
    )


def bias_up_of(vec_ref, idx):
    return jnp.concatenate(
        [
            vec_ref[s ^ idx[2], row : row + 1, :].astype(F32)
            for s in range(4)
            for row in range(5, 9)
        ],
        axis=1,
    )


def each_piece(idx, near, far):
    for c, buf in ((0, near), (1, far)):
        for xy in range(4):
            member = ((xy ^ idx[1]) * 2) + (c ^ idx[0])
            for s in range(4):
                yield s ^ idx[2], member, buf.at[xy, s]


def each_member(idx, near, far):
    for c, buf in ((0, near), (1, far)):
        for xy in range(4):
            yield None, ((xy ^ idx[1]) * 2) + (c ^ idx[0]), buf.at[xy]


def rows_at(start, size):
    return pl.ds(pl.multiple_of(start, PIECE), size)


def put_parts(idx, keep, send, tile, shard, columns):
    for xy in range(4):
        first = tile[32 * xy : 32 * xy + 16]
        second = tile[32 * xy + 16 : 32 * xy + 32]
        own_first = idx[0] == 0
        keep[xy ^ idx[1], shard ^ idx[2], :, columns] = jnp.where(own_first, first, second)
        send[xy ^ idx[1], shard ^ idx[2], :, columns] = jnp.where(own_first, second, first)


def run_moves(moves, sems, between=lambda: None):
    copies = [pltpu.make_async_copy(src, dst, sems.at[i]) for i, (src, dst) in enumerate(moves)]
    for copy in copies:
        copy.start()
    between()
    for copy in copies:
        copy.wait()


def pack_kernel(g1, b1, g2, b2, bd, bu, wq, wk, wv, wc, pa, sems):
    rows = rows_at(lax.axis_index("dp") % 8 * PIECE, PIECE)
    moves = []
    for j, w in enumerate((wq, wk, wv, wc)):
        for half in range(2):
            start = half * COLS_PROJ + j * HALF
            part = w.at[rows, half * HALF : (half + 1) * HALF]
            moves.append((part, pa.at[:, start : start + HALF]))

    def vectors():
        lines = [v[...].astype(F32).reshape(1, 128) for v in (g1, b1, g2, b2, bd)]
        lines += [bu[128 * j : 128 * j + 128].astype(F32).reshape(1, 128) for j in range(4)]
        lines.append(jnp.zeros((7, 128), F32))
        pa[:, COLS_BOTH:] = jnp.concatenate(lines, axis=0).astype(BF16)

    run_moves(moves, sems, vectors)


def pack_feed_kernel(wm, wu, wd, wr, pa, pc, pd, sems):
    member = lax.axis_index("dp") % 8
    rows = rows_at(member * PIECE, PIECE)
    moves = [(wm.at[rows, :], pc.at[:, :WIDTH]), (wu.at[rows, :], pc.at[:, WIDTH:])]
    for place, who in enumerate((member, member ^ 6)):
        for i in range(4):
            part = wd.at[rows_at(who * 64 + 16 * i, PIECE), :]
            moves.append((part, pd.at[place, :, i * WIDTH : (i + 1) * WIDTH]))
        moves.append((wr.at[rows_at(who * PIECE, PIECE), :], pd.at[place, :, 4 * WIDTH :]))
    run_moves(moves, sems)


def first_norm_kernel(idx, vec, x, a1, both_t):
    unit, _ = norm_parts(x[...].astype(F32))
    low = (unit * vector_of(vec, idx, 0) + vector_of(vec, idx, 1)).astype(BF16)
    a1[...] = low
    both_t[:WIDTH, :] = low.T
    both_t[WIDTH : 2 * WIDTH, :] = unit.astype(BF16).T
    both_t[2 * WIDTH :, :] = jnp.ones((PIECE, both_t.shape[1]), BF16)


def lanes_low():
    return lax.broadcasted_iota(jnp.int32, (1, 128), 1) < HEAD


def stacked(value):
    low = lanes_low().astype(F32).astype(BF16)
    high = (1.0 - lanes_low().astype(F32)).astype(BF16)
    return jnp.concatenate([value * low, value * high], axis=0)


def head_ones():
    row = (lax.broadcasted_iota(jnp.int32, (256, 128), 0) & 127) < HEAD
    col = lax.broadcasted_iota(jnp.int32, (256, 128), 1) < HEAD
    return (row == col).astype(F32).astype(BF16)


def head_sum(value, ones):
    high = value.astype(BF16)
    rest = (value - high.astype(F32)).astype(BF16)
    return nn(side(high, rest), ones)


def sub_places(subs):
    return [
        (sub, pair, slice(SUB * sub, SUB * sub + SUB), slice(128 * pair, 128 * pair + 128))
        for sub in subs
        for pair in range(2)
    ]


def head_max(value):
    low = lanes_low()
    first = jnp.max(jnp.where(low, value, -jnp.inf), axis=-1, keepdims=True)
    second = jnp.max(jnp.where(low, -jnp.inf, value), axis=-1, keepdims=True)
    return jnp.where(low, first, second)


def same_head():
    row = lax.broadcasted_iota(jnp.int32, (128, 256), 0) < HEAD
    col = (lax.broadcasted_iota(jnp.int32, (128, 256), 1) & 127) < HEAD
    return row == col


def causal_pair(transposed=False):
    row = lax.broadcasted_iota(jnp.int32, (SUB, 2 * SUB), 0)
    col = lax.broadcasted_iota(jnp.int32, (SUB, 2 * SUB), 1) & (SUB - 1)
    return (row <= col) if transposed else (col <= row)


def causal_whole(transposed=False):
    row = lax.broadcasted_iota(jnp.int32, (CHUNK, CHUNK), 0)
    col = lax.broadcasted_iota(jnp.int32, (CHUNK, CHUNK), 1)
    keep = (row <= col) if transposed else (col <= row)
    return keep.astype(F32).astype(BF16)


def side(*values):
    return jnp.concatenate(values, axis=1)


def masked(keep, value):
    return jnp.where(keep, value, 0.0).astype(BF16)


def attend_kernel(idx, a1, near, far, proj_o, float_o, mixed_o, kept, w_o, state, count_z):
    step = pl.program_id(0)

    @pl.when(step == 0)
    def _():
        for shard, member, piece in each_piece(idx, near, far):
            w_o[rows_at(shard * 128 + member * PIECE, PIECE), :] = piece[...]
        state[...] = jnp.zeros_like(state)
        count_z[...] = jnp.zeros_like(count_z)

    a = a1[...]
    q_all = nn(a, w_o[:, :HALF]).astype(BF16)
    k_all = nn(a, w_o[:, HALF : 2 * HALF]).astype(BF16)
    expo = jnp.exp(nn(a, w_o[:, 3 * HALF :]))
    e_all = expo.astype(BF16)
    v_all = nn(a, w_o[:, 2 * HALF : 3 * HALF]).astype(BF16)
    for j, value in enumerate((q_all, k_all, v_all, e_all)):
        proj_o[:, j * HALF : (j + 1) * HALF] = value
    float_o[:, :HALF] = expo
    total = nn(causal_whole(), e_all) + count_z[...]
    count_z[...] = total[CHUNK - 1 :, :]
    inverse = 1.0 / total
    float_o[:, HALF : 2 * HALF] = inverse
    tri, block, ones = causal_pair(), same_head(), head_ones()
    places = sub_places(range(SUBS))
    lows, wide_e, numers, ratios = {}, {}, {}, {}
    for pair in range(2):
        current = state[pair]
        for sub in range(SUBS):
            rows, at = slice(SUB * sub, SUB * sub + SUB), slice(128 * pair, 128 * pair + 128)
            lows[sub, pair] = current.astype(BF16)
            kept[sub, pair] = lows[sub, pair]
            wide_e[sub, pair] = stacked(e_all[rows, at])
            more = tn(e_all[rows, at], side(k_all[rows, at], v_all[rows, at]))
            current = current + jnp.where(block, more, 0.0)
        state[pair] = current
    for sub, pair, rows, at in places:
        scores = masked(tri, nt(q_all[rows, at], stacked(k_all[rows, at])))
        numer = nn(scores, wide_e[sub, pair])
        numers[sub, pair] = numer + nt(q_all[rows, at], lows[sub, pair][:, :128])

    def soften(sub, pair, rows, at):
        inv = inverse[rows, at]
        logits = (HEAD ** -0.5) * numers[sub, pair] * inv
        expd = jnp.exp(logits - head_max(logits))
        probs = expd * (1.0 / head_sum(expd, ones))
        ratios[sub, pair] = (probs * inv).astype(BF16)
        float_o[rows, 2 * HALF + 128 * pair : 2 * HALF + 128 * pair + 128] = logits
        float_o[rows, 3 * HALF + 128 * pair : 3 * HALF + 128 * pair + 128] = probs
        mixed_o[rows, at] = ratios[sub, pair]

    def mix(sub, pair, rows, at):
        mixing = masked(tri, nt(ratios[sub, pair], wide_e[sub, pair]))
        out = nn(mixing, stacked(v_all[rows, at])) + nn(ratios[sub, pair], lows[sub, pair][:, 128:])
        mixed_o[rows, HALF + 128 * pair : HALF + 128 * pair + 128] = out.astype(BF16)

    for i, place in enumerate(places):
        soften(*place)
        if i:
            mix(*places[i - 1])
    mix(*places[-1])


def feed_kernel(
    idx, vec, x, o0, o1, target, up_near_i, up_far_i, down_near_i, ends_i, sides_i,
    out_o, h_o, slope_o, dy_o, bias_o, keep, send, mix_o, up_o, down_o,
    up_near, up_far, down_near, down_far,
    w_mix, w_up, w_down, w_read, act_s, out_s, h_s, slope_s, dy_s, dl_s, df_s, sems, row_sems,
):
    step = pl.program_id(0)
    moves = (
        (up_near_i, up_near), (up_far_i, up_far), (down_near_i, down_near),
        (ends_i.at[0], down_far.at[0]), (ends_i.at[1], down_far.at[3]), (sides_i, down_far.at[1:3]),
        (w_mix, mix_o), (w_up, up_o), (w_down, down_o),
    )
    copies = [pltpu.make_async_copy(src, dst, sems.at[i]) for i, (src, dst) in enumerate(moves)]

    @pl.when(step == 0)
    def _():
        for copy in copies[:6]:
            copy.start()
        for copy in copies[:2]:
            copy.wait()
        for shard, member, piece in each_piece(idx, up_near, up_far):
            rows = rows_at(shard * 128 + member * PIECE, PIECE)
            w_mix[rows, :] = piece[:, :WIDTH]
            w_up[rows, :] = piece[:, WIDTH:]
        for copy in copies[2:6]:
            copy.wait()
        for shard, member, piece in each_piece(idx, down_near, down_far):
            for i in range(4):
                rows = rows_at(shard * 512 + member * 64 + 16 * i, PIECE)
                w_down[rows, :] = piece[:, i * WIDTH : (i + 1) * WIDTH]
            w_read[rows_at(shard * 128 + member * PIECE, PIECE), :] = piece[:, 4 * WIDTH :]
        for copy in copies[6:]:
            copy.start()
        bias_o[...] = jnp.zeros_like(bias_o)

    def row_copies(place):
        at = pl.ds(pl.multiple_of(place * ROWS, ROWS), ROWS)
        pairs = ((out_s, out_o), (h_s, h_o), (slope_s, slope_o), (dy_s, dy_o))
        return [
            pltpu.make_async_copy(src.at[at], dst.at[at], row_sems.at[place, i])
            for i, (src, dst) in enumerate(pairs)
        ]

    rows = pl.ds(pl.multiple_of(step * ROWS, ROWS), ROWS)
    attn = nn(o0[...], w_mix[:HALF, :]) + nn(o1[...], w_mix[HALF:, :])
    resid = x[...].astype(F32) + attn
    h_s[rows, :] = resid
    unit, _ = norm_parts(resid)
    second = (unit * vector_of(vec, idx, 2) + vector_of(vec, idx, 3)).astype(BF16)
    bias = bias_up_of(vec, idx)
    branch = jnp.zeros((ROWS, WIDTH), F32)
    scale = (2.0 / jnp.pi) ** 0.5
    at = [slice(512 * j, 512 * j + 512) for j in range(4)]
    products = nn(second, w_up[:, at[0]])
    for j in range(4):
        z = products + bias[:, at[j]]
        if j < 3:
            products = nn(second, w_up[:, at[j + 1]])
        zz = z * z
        cdf = 0.5 + 0.5 * jnp.tanh(z * (scale + (scale * 0.044715) * zz))
        active = z * cdf
        slope = cdf + (active - active * cdf) * (2 * scale + (6 * scale * 0.044715) * zz)
        slope_s[rows, at[j]] = slope.astype(BF16)
        act = active.astype(BF16)
        act_s[rows, at[j]] = act
        branch += nn(act, w_down[at[j], :])
    out = (resid + (branch + vector_of(vec, idx, 4))).astype(BF16)
    out_s[rows, :] = out
    logits = nn(out, w_read[...])
    expd = jnp.exp(logits - jnp.max(logits, axis=-1, keepdims=True))
    soft = expd / jnp.sum(expd, axis=-1, keepdims=True)
    classes = lax.broadcasted_iota(jnp.int32, (VOCAB, ROWS), 0)
    hits = jnp.where(classes == target[rows].reshape(1, ROWS), 1.0, 0.0).T
    dl = (soft - hits).astype(BF16)
    dl_s[rows, :] = dl
    dy = nt(dl, w_read[...])
    dy_s[rows, :] = dy
    df = dy.astype(BF16)
    df_s[rows, :] = df
    bias_o[...] += jnp.sum(df.astype(F32), axis=0, keepdims=True)
    for copy in row_copies(step):
        copy.start()

    @pl.when(step == pl.num_programs(0) - 1)
    def _():
        whole = tn(out_s[...], dl_s[...]).astype(BF16)
        for shard in range(4):
            tile = whole[shard * 128 : shard * 128 + 128]
            put_parts(idx, keep, send, tile, shard, slice(4 * WIDTH, None))
            large = tn(act_s[:, shard * 512 : shard * 512 + 512], df_s[...]).astype(BF16)
            for xy in range(4):
                tile = large[xy * 128 : xy * 128 + 128]
                own_first = idx[0] == 0
                for i in range(4):
                    first = tile[16 * i : 16 * i + 16]
                    later = tile[64 + 16 * i : 64 + 16 * i + 16]
                    at = slice(i * WIDTH, (i + 1) * WIDTH)
                    keep[xy ^ idx[1], shard ^ idx[2], :, at] = jnp.where(own_first, first, later)
                    send[xy ^ idx[1], shard ^ idx[2], :, at] = jnp.where(own_first, later, first)
        for copy in copies[6:]:
            copy.wait()
        for place in range(act_s.shape[0] // ROWS):
            for copy in row_copies(place):
                copy.wait()


def feed_back_kernel(
    idx, vec, h_i, slope_i, dy_i, o0_i, o1_i, mix_i, up_i, down_i,
    dh_o, do_o, gain_o, shift_o, bias_o, keep, send,
    w_mix, w_up, w_down, h_s, slope_s, dy_s, o0, o1, dz_s, a2_s, da_s, dh_s, do_s,
    sems, row_sems, out_sems,
):
    step = pl.program_id(0)
    places = dz_s.shape[0] // ROWS
    half = pl.ds(HALF, HALF)
    moves = (
        (down_i, w_down), (up_i, w_up), (mix_i, w_mix), (o0_i.at[:, half], o0), (o1_i.at[:, half], o1)
    )
    copies = [pltpu.make_async_copy(src, dst, sems.at[i]) for i, (src, dst) in enumerate(moves)]

    def row_copies(place):
        at = pl.ds(pl.multiple_of(place * ROWS, ROWS), ROWS)
        pairs = ((dy_i, dy_s), (slope_i, slope_s), (h_i, h_s))
        return [
            pltpu.make_async_copy(src.at[at], dst.at[at], row_sems.at[place, i])
            for i, (src, dst) in enumerate(pairs)
        ]

    def out_copies(place):
        at = pl.ds(pl.multiple_of(place * ROWS, ROWS), ROWS)
        pairs = ((dh_s, dh_o), (do_s, do_o))
        return [
            pltpu.make_async_copy(src.at[at], dst.at[at], out_sems.at[place, i])
            for i, (src, dst) in enumerate(pairs)
        ]

    @pl.when(step == 0)
    def _():
        copies[0].start()
        for copy in row_copies(0):
            copy.start()
        for copy in copies[1:3]:
            copy.start()
        gain_o[...] = jnp.zeros_like(gain_o)
        shift_o[...] = jnp.zeros_like(shift_o)
        bias_o[...] = jnp.zeros_like(bias_o)
        copies[0].wait()

    for copy in row_copies(step)[:2]:
        copy.wait()
    rows = pl.ds(pl.multiple_of(step * ROWS, ROWS), ROWS)
    gain = vector_of(vec, idx, 2)
    d_out = dy_s[rows, :]
    df = d_out.astype(BF16)
    for j in range(4):
        at = slice(512 * j, 512 * j + 512)
        dz = (nt(df, w_down[at, :]) * slope_s[rows, at].astype(F32)).astype(BF16)
        dz_s[rows, at] = dz
        bias_o[:, at] += jnp.sum(dz.astype(F32), axis=0, keepdims=True)

    @pl.when(step == 0)
    def _():
        for place in range(1, places):
            for copy in row_copies(place):
                copy.start()
        for copy in copies[3:]:
            copy.start()
        for copy in copies[1:3]:
            copy.wait()

    row_copies(step)[2].wait()
    d_second = nt(dz_s[rows, :], w_up[...])
    unit, inverse = norm_parts(h_s[rows, :])
    a2_s[rows, :] = (unit * gain + vector_of(vec, idx, 3)).astype(BF16)
    gain_o[...] += jnp.sum(d_second * unit, axis=0, keepdims=True)
    shift_o[...] += jnp.sum(d_second, axis=0, keepdims=True)
    dh = d_out + norm_pull(d_second, unit, inverse, gain)
    dh_s[rows, :] = dh
    da = dh.astype(BF16)
    da_s[rows, :] = da
    do_s[rows, :] = nt(da, w_mix[...]).astype(BF16)
    for copy in out_copies(step):
        copy.start()

    @pl.when(step == pl.num_programs(0) - 1)
    def _():
        for copy in copies[3:]:
            copy.wait()
        for half in range(2):
            large = tn((o0, o1)[half][...], da_s[...]).astype(BF16)
            for i in range(2):
                tile = large[128 * i : 128 * i + 128]
                put_parts(idx, keep, send, tile, 2 * half + i, slice(0, WIDTH))
        for j in range(4):
            large = tn(a2_s[...], dz_s[:, 512 * j : 512 * j + 512]).astype(BF16)
            at = slice(WIDTH + 512 * j, WIDTH + 512 * j + 512)
            for shard in range(4):
                put_parts(idx, keep, send, large[shard * 128 : shard * 128 + 128], shard, at)
        for place in range(places):
            for copy in out_copies(place):
                copy.wait()


def proj_gradient(idx, both_t, w, dx, keep, send):
    on_gain = jnp.zeros((WIDTH, HALF), F32)
    sums = []
    for j in range(4):
        at = slice(j * HALF, (j + 1) * HALF)
        product = nn(both_t[...], dx[:, at])
        low = product[:WIDTH].astype(BF16)
        for shard in range(4):
            put_parts(idx, keep, send, low[shard * 128 : shard * 128 + 128], shard, at)
        on_gain += product[WIDTH : 2 * WIDTH] * w[:, at].astype(F32)
        sums.append(product[2 * WIDTH : 2 * WIDTH + 8])
    sums = side(*sums)
    high = sums.astype(BF16)
    rest = (sums - high.astype(F32)).astype(BF16)
    shift_rows = nt(jnp.concatenate([high, rest], axis=0), w[...])
    gain_column = jnp.sum(on_gain, axis=1, keepdims=True)
    gain_row = side(gain_column, jnp.zeros((WIDTH, 7), F32)).T[:1]
    return jnp.concatenate([gain_row, shift_rows[:1] + shift_rows[8:9], jnp.zeros((6, WIDTH), F32)])


def late_operands(pairs, sems):
    copies = [pltpu.make_async_copy(src, dst, sems.at[i]) for i, (src, dst) in enumerate(pairs)]

    @pl.when(pl.program_id(0) == 0)
    def _():
        for copy in copies:
            copy.start()

    return copies


def attend_back_kernel(
    idx, both_t, w, proj, floats, ratios, do_i, kept,
    dx_o, keep, send, share_o,
    state, count_z, dx_s, both_s, w_s, sems,
):
    copies = late_operands(((both_t, both_s), (w, w_s)), sems)
    attend_back_step(proj, floats, ratios, do_i, kept, dx_o, state, count_z, dx_s)

    @pl.when(pl.program_id(0) == pl.num_programs(0) - 1)
    def _():
        for copy in copies:
            copy.wait()
        share_o[...] = proj_gradient(idx, both_s, w_s, dx_s, keep, send)


def attend_back_last_kernel(
    idx, both_t, w, proj, floats, ratios, do_i, kept,
    share, g_g2, g_b2, g_bd, g_bu,
    dx_o, keep, send,
    state, count_z, dx_s, both_s, w_s, sems,
):
    copies = late_operands(((both_t, both_s), (w, w_s)), sems)
    attend_back_step(proj, floats, ratios, do_i, kept, dx_o, state, count_z, dx_s)

    @pl.when(pl.program_id(0) == pl.num_programs(0) - 1)
    def _():
        for copy in copies:
            copy.wait()
        total = proj_gradient(idx, both_s, w_s, dx_s, keep, send) + share[...]
        for s in range(4):
            at = slice(128 * s, 128 * s + 128)
            lines = [total[:2, at], g_g2[:, at], g_b2[:, at], g_bd[:, at]]
            lines += [g_bu[:, 512 * s + 128 * j : 512 * s + 128 * j + 128] for j in range(4)]
            lines.append(jnp.zeros((7, 128), F32))
            block = jnp.concatenate(lines, axis=0).astype(BF16)
            for xy in range(4):
                keep[xy, s ^ idx[2], :, COLS_PROJ:] = block
                send[xy, s ^ idx[2], :, COLS_PROJ:] = block


def attend_back_step(proj, floats, ratios, do_i, kept, dx_o, state, count_z, dx_s):
    step = pl.program_id(0)
    chunk = pl.num_programs(0) - 1 - step

    @pl.when(step == 0)
    def _():
        state[...] = jnp.zeros_like(state)
        count_z[...] = jnp.zeros_like(count_z)

    def take(ref, j, rows, pair):
        return ref[rows, j * HALF + 128 * pair : j * HALF + 128 * pair + 128]

    tri, trt, block, ones = causal_pair(), causal_pair(True), same_head(), head_ones()
    places = sub_places(reversed(range(SUBS)))
    d_mixes, wide, d_numers, d_totals, others = {}, {}, {}, {}, {}
    for sub, pair, rows, at in places:
        v = take(proj, 2, rows, pair)
        d_mixes[sub, pair] = masked(tri, nt(do_i[rows, at], stacked(v)))
        wide[sub, pair] = stacked(take(proj, 3, rows, pair))
    for sub, pair, rows, at in places:
        do, ratio = do_i[rows, at], ratios[rows, at]
        q, k, v, e = [take(proj, j, rows, pair) for j in range(4)]
        inv, logits, probs = [take(floats, j, rows, pair) for j in (1, 2, 3)]
        d_ratio = nn(d_mixes[sub, pair], wide[sub, pair])
        d_ratio = (d_ratio + nt(do, kept[sub, pair][:, 128:])) * inv
        weighed = d_ratio * probs
        d_logits = weighed - probs * head_sum(weighed, ones)
        d_numers[sub, pair] = ((HEAD ** -0.5) * d_logits * inv).astype(BF16)
        d_totals[sub, pair] = (-(weighed + d_logits * logits) * inv).astype(BF16)
        wide_q, wide_r, wide_do = stacked(q), stacked(ratio), stacked(do)
        scores = masked(trt, nt(k, wide_q))
        mixing = masked(trt, nt(e, wide_r))
        d_mix_t = masked(trt, nt(v, wide_do))
        others[sub, pair] = (scores, d_mix_t, nn(mixing, wide_do), wide_q, wide_r)
    d_total = jnp.concatenate([side(d_totals[sub, 0], d_totals[sub, 1]) for sub in range(SUBS)], axis=0)
    total_z = nn(causal_whole(True), d_total) + count_z[...]
    count_z[...] = total_z[:1, :]
    currents = [state[0], state[1]]
    lows = {}
    for sub, pair, rows, at in places:
        lows[sub, pair] = currents[pair].astype(BF16)
        more = side(
            tn(ratios[rows, at], do_i[rows, at]), tn(d_numers[sub, pair], take(proj, 0, rows, pair))
        )
        currents[pair] = currents[pair] + jnp.where(block, more, 0.0)
    state[0], state[1] = currents
    for sub, pair, rows, at in places:
        k, v, e = [take(proj, j, rows, pair) for j in (1, 2, 3)]
        scores, d_mix_t, dv, wide_q, wide_r = others[sub, pair]
        d_numer, low = d_numers[sub, pair], lows[sub, pair]
        wide_n = stacked(d_numer)
        d_scores = masked(tri, nt(d_numer, wide[sub, pair]))
        d_scores_t = masked(trt, nt(e, wide_n))
        both = nn(e, low)
        de = nn(side(d_mix_t, scores), jnp.concatenate([wide_r, wide_n], axis=0))
        de = de + nt(side(v, k), low) + total_z[rows, at]
        dq = nn(d_scores, stacked(k)) + nn(d_numer, kept[sub, pair][:, :128])
        dk = nn(d_scores_t, wide_q) + both[:, 128:]
        dv = dv + both[:, :128]
        dc = de * take(floats, 0, rows, pair)
        for j, value in enumerate((dq, dk, dv, dc)):
            dx_o[rows, j * HALF + 128 * pair : j * HALF + 128 * pair + 128] = value.astype(BF16)
    dx_s[pl.ds(pl.multiple_of(chunk * CHUNK, CHUNK), CHUNK), :] = dx_o[...]


def inputs_kernel(idx, vec, x, dh, dx0, dx1, w0, w1, dx_o):
    unit, inverse = norm_parts(x[...].astype(F32))
    d_first = nt(dx0[...], w0[...]) + nt(dx1[...], w1[...])
    dx_o[...] = dh[...] + norm_pull(d_first, unit, inverse, vector_of(vec, idx, 0))


def unpack_proj_kernel(idx, near, far, query, key, value, control, g1, b1, g2, b2, bd, bu):
    for shard, member, piece in each_member(idx, near, far):
        rows = rows_at(member * PIECE, PIECE)
        for j, out in enumerate((query, key, value, control)):
            for half in range(2):
                start = half * COLS_PROJ + j * HALF
                out[rows, half * HALF : (half + 1) * HALF] = piece[:, start : start + HALF].astype(F32)

        @pl.when(member == 0)
        def _():
            lines = piece[:, COLS_BOTH:].astype(F32)
            for i, out in enumerate((g1, b1, g2, b2, bd)):
                out[...] = lines[i]
            for i in range(4):
                bu[128 * i : 128 * i + 128] = lines[5 + i]


def unpack_feed_kernel(idx, near, far, mix, up, down, read):
    for shard, member, piece in each_member(idx, near, far):
        rows = rows_at(member * PIECE, PIECE)
        mix[rows, :] = piece[:, :WIDTH].astype(F32)
        up[rows, :] = piece[:, WIDTH:COLS_UP].astype(F32)
        for i in range(4):
            start = COLS_UP + i * WIDTH
            down[rows_at(member * 64 + 16 * i, PIECE), :] = piece[:, start : start + WIDTH].astype(F32)
        read[rows, :] = piece[:, COLS_UP + 4 * WIDTH :].astype(F32)


def shaped(shape, dtype):
    return jax.ShapeDtypeStruct(shape, dtype)


def call(kernel, name, args, outs, steps=None, scratch=(), flops=0, limit=44):
    grid = (steps,) if steps else ()

    def spec(shape, block):
        if block == "hbm":
            return pl.BlockSpec(memory_space=pl.ANY)
        if block is None:
            return pl.BlockSpec(tuple(shape), lambda *_: (0,) * len(shape))
        return pl.BlockSpec(*block)

    in_specs = []
    for array, block in args:
        if array.dtype == jnp.int32 and array.shape == (3,):
            in_specs.append(pl.BlockSpec(memory_space=pltpu.SMEM))
        else:
            in_specs.append(spec(array.shape, block))
    moved = sum(a.size * a.dtype.itemsize for a, _ in args)
    return pl.pallas_call(
        kernel,
        grid=grid,
        in_specs=in_specs,
        out_specs=[spec(shape, block) for shape, _, block in outs],
        out_shape=[shaped(shape, dtype) for shape, dtype, _ in outs],
        scratch_shapes=list(scratch),
        compiler_params=pltpu.CompilerParams(
            vmem_limit_bytes=limit * MIB,
            dimension_semantics=("arbitrary",) * len(grid) if grid else None,
        ),
        cost_estimate=pl.CostEstimate(flops=1000, bytes_accessed=1000, transcendentals=0),
        name=name,
    )(*[array for array, _ in args])


def swap(value, axis, size, distance):
    return lax.ppermute(value, axis, [(i, i ^ distance) for i in range(size)])


def pin(*values):
    return lax.optimization_barrier(values)


def near_rows(piece, shards):
    return [swap(piece, "shard", shards, k) for k in range(1, 4)]


def near_pair(piece, shards):
    return jnp.stack([piece, swap(piece, "shard", shards, 1)])


def far_pair(pair, shards):
    return swap(pair, "shard", shards, 2)


def sum_of(values):
    values = [v.astype(F32) for v in values]
    return ((values[0] + values[1]) + (values[2] + values[3])).astype(BF16)


def core_sum(keep, got):
    return [(keep[k].astype(F32) + got[k].astype(F32)).astype(BF16) for k in range(4)]


def plane_start(parts, dp):
    return [swap(parts[k], "dp", dp, 2 * k) for k in range(1, 4)]


def plane_sum(parts, got):
    return [sum_of([parts[0][k], got[0][k], got[1][k], got[2][k]]) for k in range(4)]


def plane_halves(parts, got):
    total = [p.astype(F32) for p in [parts[0]] + got]
    total = ((total[0] + total[1]) + (total[2] + total[3])).astype(BF16)
    return total[:2], total[2:]


def half_start(high, shards):
    return swap(high, "shard", shards, 2)


def half_sum(low, got):
    return [(low[k].astype(F32) + got[k].astype(F32)).astype(BF16) for k in range(2)]


def last_start(pair, shards):
    return swap(pair[1], "shard", shards, 1)


def last_sum(pair, got, dp):
    return across_planes((pair[0].astype(F32) + got.astype(F32)).astype(BF16), dp)


def across_planes(total, dp):
    distance = 8
    while distance < dp:
        total = (total.astype(F32) + swap(total, "dp", dp, distance).astype(F32)).astype(BF16)
        distance *= 2
    return total


def shard_start(rows, shards):
    return [swap(rows[k], "shard", shards, k) for k in range(1, 4)]


def shard_sum(rows, got, dp):
    return across_planes(sum_of([rows[0]] + got), dp)


def body(dp, shards):
    def on_device(
        tokens, targets, gain_one, bias_one, w_query, w_key, w_value, w_control, w_mix,
        gain_two, bias_two, w_up, bias_up, w_down, bias_down, w_read,
    ):
        count = tokens.shape[0]
        steps = count // CHUNK
        rows = WIDTH // shards
        member = lax.axis_index("dp") % 8
        idx = jnp.stack([member % 2, member // 2, lax.axis_index("shard")]).astype(jnp.int32)
        forward = lambda i: (i, 0)
        back = lambda i: (steps - 1 - i, 0)
        tok = lambda n: ((CHUNK, n), forward)
        parts = (4, 4, PIECE)

        vectors = (gain_one, bias_one, gain_two, bias_two, bias_down, bias_up)
        pa = call(
            pack_kernel,
            "pack_projections",
            [(v, None) for v in vectors]
            + [(w, "hbm") for w in (w_query, w_key, w_value, w_control)],
            [((PIECE, COLS_BOTH + 128), BF16, None)],
            scratch=[pltpu.SemaphoreType.DMA((8,))],
            limit=56,
        )[0]
        got_a = near_rows(pa, shards)
        pu, pd = call(
            pack_feed_kernel,
            "pack_feed",
            [(w, "hbm") for w in (w_mix, w_up, w_down, w_read)] + [(pa, "hbm")],
            [((PIECE, COLS_UP), BF16, None), ((2, PIECE, COLS_DOWN), BF16, None)],
            scratch=[pltpu.SemaphoreType.DMA((12,))],
            limit=56,
        )
        pair_u = near_pair(pu, shards)
        rows_a = jnp.stack([pa[:, :COLS_BOTH]] + [g[:, :COLS_BOTH] for g in got_a])
        vec = jnp.stack([pa[:, COLS_BOTH:]] + [g[:, COLS_BOTH:] for g in got_a])
        rows_a, vec, pd, tokens_a = pin(rows_a, vec, pd, tokens)
        plane_a = [swap(rows_a, "dp", dp, 2 * k) for k in range(1, 4)]
        got_u = far_pair(pair_u, shards)
        pair_d = near_pair(pd, shards)
        a1, both_t = call(
            first_norm_kernel,
            "first_norm",
            [(idx, None), (vec, None), (tokens_a, None)],
            [
                ((count, WIDTH), BF16, None),
                ((2 * WIDTH + PIECE, count), BF16, None),
            ],
        )
        plane_a, got_u, a1, both_t = pin(plane_a, got_u, a1, both_t)
        near_a = jnp.stack([rows_a] + plane_a)
        far_a = swap(near_a, "dp", dp, 1)
        pair_d, _ = pin(pair_d, near_a)
        got_d = far_pair(pair_d, shards)
        got_u, _ = pin(got_u, near_a)
        rows_u = jnp.concatenate([pair_u, got_u])
        plane_u = plane_start([rows_u] * 4, dp)

        kept = ((SUBS, 2, 128, 256), lambda i: (i, 0, 0, 0))

        def attend(a1, half):
            at = ((4, 4, PIECE, COLS_PROJ), lambda i: (0, 0, 0, half))
            return call(
                attend_kernel,
                "attend",
                [(idx, None), (a1, tok(WIDTH)), (near_a, at), (far_a, at)],
                [
                    ((count, COLS_PROJ), BF16, tok(COLS_PROJ)),
                    ((count, COLS_PROJ), F32, tok(COLS_PROJ)),
                    ((count, 2 * HALF), BF16, tok(2 * HALF)),
                    ((SUBS * steps, 2, 128, 256), BF16, kept),
                    ((WIDTH, COLS_PROJ), BF16, None),
                ],
                steps,
                [
                    pltpu.VMEM((2, 128, 256), F32),
                    pltpu.VMEM((1, HALF), F32),
                ],
                flops=6e9,
            )

        first = attend(a1, 0)
        first, plane_u, got_d, a1 = pin(first, plane_u, got_d, a1)
        rows_d = jnp.concatenate([pair_d, got_d])
        plane_d = [swap(rows_d[:, 0], "dp", dp, 2 * k) for k in range(1, 3)]
        near_u = jnp.stack([rows_u] + plane_u)
        far_u = swap(near_u, "dp", dp, 1)
        ends_d = swap(jnp.stack([rows_d[:, 0], rows_d[:, 1]]), "dp", dp, 1)
        second = attend(a1, 1)
        second, far_u, ends_d, plane_d = pin(second, far_u, ends_d, plane_d)
        near_d = jnp.stack([rows_d[:, 0]] + plane_d + [rows_d[:, 1]])
        sides_d = swap(jnp.stack(plane_d), "dp", dp, 1)
        halves = (first, second)
        o0, o1 = first[2], second[2]

        wide = lambda n: ((ROWS, n), forward)
        mixed_at = ((ROWS, HALF), lambda i: (i, 1))
        places = count // ROWS
        out, h, slope, dy, g_bias_down, keep_d, send_d, full_mix, full_up, full_down = call(
            feed_kernel,
            "feed_forward",
            [
                (idx, None), (vec, None), (tokens, wide(WIDTH)), (o0, mixed_at), (o1, mixed_at),
                (targets, None), (near_u, "hbm"), (far_u, "hbm"), (near_d, "hbm"),
                (ends_d, "hbm"), (sides_d, "hbm"),
            ],
            [
                ((count, WIDTH), BF16, "hbm"),
                ((count, WIDTH), F32, "hbm"),
                ((count, FF), BF16, "hbm"),
                ((count, WIDTH), F32, "hbm"),
                ((1, WIDTH), F32, None),
                (parts + (COLS_DOWN,), BF16, None),
                (parts + (COLS_DOWN,), BF16, None),
                ((WIDTH, WIDTH), BF16, "hbm"),
                ((WIDTH, FF), BF16, "hbm"),
                ((FF, WIDTH), BF16, "hbm"),
            ],
            places,
            [
                pltpu.VMEM(parts + (COLS_UP,), BF16),
                pltpu.VMEM(parts + (COLS_UP,), BF16),
                pltpu.VMEM(parts + (COLS_DOWN,), BF16),
                pltpu.VMEM(parts + (COLS_DOWN,), BF16),
                pltpu.VMEM((WIDTH, WIDTH), BF16),
                pltpu.VMEM((WIDTH, FF), BF16),
                pltpu.VMEM((FF, WIDTH), BF16),
                pltpu.VMEM((WIDTH, VOCAB), BF16),
                pltpu.VMEM((count, FF), BF16),
                pltpu.VMEM((count, WIDTH), BF16),
                pltpu.VMEM((count, WIDTH), F32),
                pltpu.VMEM((count, FF), BF16),
                pltpu.VMEM((count, WIDTH), F32),
                pltpu.VMEM((count, VOCAB), BF16),
                pltpu.VMEM((count, WIDTH), BF16),
                pltpu.SemaphoreType.DMA((9,)),
                pltpu.SemaphoreType.DMA((places, 4)),
            ],
            flops=8e9,
            limit=46,
        )
        got_d = swap(send_d, "dp", dp, 1)

        dh, d_mixed, g_gain_two, g_bias_two, g_bias_up, keep_u, send_u = call(
            feed_back_kernel,
            "feed_backward",
            [(idx, None), (vec, None)]
            + [(t, "hbm") for t in (h, slope, dy, o0, o1, full_mix, full_up, full_down)],
            [
                ((count, WIDTH), F32, "hbm"),
                ((count, WIDTH), BF16, "hbm"),
                ((1, WIDTH), F32, None),
                ((1, WIDTH), F32, None),
                ((1, FF), F32, None),
                (parts + (COLS_UP,), BF16, None),
                (parts + (COLS_UP,), BF16, None),
            ],
            places,
            [
                pltpu.VMEM((WIDTH, WIDTH), BF16),
                pltpu.VMEM((WIDTH, FF), BF16),
                pltpu.VMEM((FF, WIDTH), BF16),
                pltpu.VMEM((count, WIDTH), F32),
                pltpu.VMEM((count, FF), BF16),
                pltpu.VMEM((count, WIDTH), F32),
                pltpu.VMEM((count, HALF), BF16),
                pltpu.VMEM((count, HALF), BF16),
                pltpu.VMEM((count, FF), BF16),
                pltpu.VMEM((count, WIDTH), BF16),
                pltpu.VMEM((count, WIDTH), BF16),
                pltpu.VMEM((count, WIDTH), F32),
                pltpu.VMEM((count, WIDTH), BF16),
                pltpu.SemaphoreType.DMA((5,)),
                pltpu.SemaphoreType.DMA((places, 3)),
                pltpu.SemaphoreType.DMA((places, 2)),
            ],
            flops=8e9,
            limit=46,
        )
        got_d, d_mixed, send_u = pin(got_d, d_mixed, send_u)
        got_u = swap(send_u, "dp", dp, 1)
        sum_d = core_sum(keep_d, got_d)
        sum_d, d_mixed = pin(sum_d, d_mixed)
        got_d = plane_start(sum_d, dp)

        kept_back = ((SUBS, 2, 128, 256), lambda i: (steps - 1 - i, 0, 0, 0))

        def attend_back(half, d_mixed, extra=()):
            proj, floats, mixed, states, w = halves[half]
            wide = ((CHUNK, COLS_PROJ), back)
            column = ((CHUNK, HALF), lambda i: (steps - 1 - i, half))
            last = half == 1
            cols = COLS_LAST if last else COLS_PROJ
            return call(
                attend_back_last_kernel if last else attend_back_kernel,
                "attend_backward",
                [(idx, None), (both_t, "hbm"), (w, "hbm")]
                + [(proj, wide), (floats, wide), (mixed, ((CHUNK, HALF), back))]
                + [(d_mixed, column), (states, kept_back)]
                + [(t, None) for t in extra],
                [
                    ((count, COLS_PROJ), BF16, ((CHUNK, COLS_PROJ), back)),
                    (parts + (cols,), BF16, None),
                    (parts + (cols,), BF16, None),
                ]
                + ([] if last else [((8, WIDTH), F32, None)]),
                steps,
                [
                    pltpu.VMEM((2, 128, 256), F32),
                    pltpu.VMEM((1, HALF), F32),
                    pltpu.VMEM((count, COLS_PROJ), BF16),
                    pltpu.VMEM((2 * WIDTH + PIECE, count), BF16),
                    pltpu.VMEM((WIDTH, COLS_PROJ), BF16),
                    pltpu.SemaphoreType.DMA((2,)),
                ],
                flops=10e9,
            )

        dx0, keep_a, send_a, share = attend_back(0, d_mixed)
        got_d, got_u, send_a, d_mixed = pin(got_d, got_u, send_a, d_mixed)
        got_a = swap(send_a, "dp", dp, 1)
        sum_u = core_sum(keep_u, got_u)
        low_d, high_d = plane_halves(sum_d, got_d)
        sum_u, low_d, high_d, d_mixed = pin(sum_u, low_d, high_d, d_mixed)
        got_u = plane_start(sum_u, dp)
        got_d = half_start(high_d, shards)

        extra = (share, g_gain_two, g_bias_two, g_bias_down, g_bias_up)
        dx1, keep_b, send_b = attend_back(1, d_mixed, extra)
        got_d, got_u, got_a, send_b, dx1 = pin(got_d, got_u, got_a, send_b, dx1)
        got_b = swap(send_b, "dp", dp, 1)
        sum_p = [
            jnp.concatenate(both, axis=-1)
            for both in zip(core_sum(keep_a, got_a), core_sum(keep_b, got_b))
        ]
        sum_p, dx1 = pin(sum_p, dx1)
        got_p = plane_start(sum_p, dp)
        got_u, got_d, _ = pin(got_u, got_d, sum_p)
        low_u, high_u = plane_halves(sum_u, got_u)
        got_u = half_start(high_u, shards)
        pair_d = half_sum(low_d, got_d)
        got_d = last_start(pair_d, shards)
        d_tokens = call(
            inputs_kernel,
            "input_gradient",
            [
                (idx, None), (vec, None), (tokens, tok(WIDTH)), (dh, tok(WIDTH)),
                (dx0, tok(COLS_PROJ)), (dx1, tok(COLS_PROJ)),
                (first[4], None), (second[4], None),
            ],
            [((count, WIDTH), F32, tok(WIDTH))],
            steps,
            flops=3e9,
        )[0]
        got_u, got_d, d_tokens = pin(got_u, got_d, d_tokens)
        pair_u = half_sum(low_u, got_u)
        got_u = last_start(pair_u, shards)
        total_d = last_sum(pair_d, got_d, dp)
        got_p, _, _ = pin(got_p, pair_u, d_tokens)
        total_f = jnp.concatenate([last_sum(pair_u, got_u, dp), total_d], axis=-1)
        along_f = swap(total_f, "dp", dp, 4)
        got_p, _ = pin(got_p, total_f)
        rows_p = plane_sum(sum_p, got_p)
        got_p = shard_start(rows_p, shards)
        along_f, _ = pin(along_f, rows_p)
        pair_f = jnp.stack([total_f, along_f])
        up_f = swap(pair_f, "dp", dp, 2)
        got_p, _ = pin(got_p, pair_f)
        total_p = shard_sum(rows_p, got_p, dp)
        plane_p = plane_start([total_p] * 4, dp)
        up_f, _ = pin(up_f, plane_p[0])
        near_f = jnp.stack([pair_f, up_f], axis=1).reshape((4,) + total_f.shape)
        far_f = swap(near_f, "dp", dp, 1)
        g_mix, g_up, g_down, g_read = call(
            unpack_feed_kernel,
            "unpack_feed",
            [(idx, None), (near_f, None), (far_f, None)],
            [
                ((rows, WIDTH), F32, None),
                ((rows, FF), F32, None),
                ((4 * rows, WIDTH), F32, None),
                ((rows, VOCAB), F32, None),
            ],
        )
        near_p = jnp.stack([total_p] + plane_p)
        far_p = swap(near_p, "dp", dp, 1)
        far_p, g_up = pin(far_p, g_up)
        g_query, g_key, g_value, g_control, g1, b1, g2, b2, bd, bu = call(
            unpack_proj_kernel,
            "unpack_proj",
            [(idx, None), (near_p, None), (far_p, None)],
            [((rows, WIDTH), F32, None)] * 4 + [((128,), F32, None)] * 5 + [((512,), F32, None)],
        )
        return (
            out, d_tokens, g1, b1, g_query, g_key, g_value, g_control, g_mix,
            g2, b2, g_up, bu, g_down, bd, g_read,
        )

    return on_device


def solution(mesh):
    dp, shards = mesh.shape["dp"], mesh.shape["shard"]
    vector, matrix = P("shard"), P("shard", None)
    rows = P(("dp", "shard"), None)
    params = (
        vector, vector, matrix, matrix, matrix, matrix, matrix,
        vector, vector, matrix, vector, matrix, vector, matrix,
    )
    return jax.shard_map(
        body(dp, shards),
        mesh=mesh,
        in_specs=(rows, P(("dp", "shard"))) + params,
        out_specs=(rows, rows) + params,
        check_vma=False,
    )
```
